32 devices in a mesh: tm: 8 (over z, x), slots: 4 (over y, core).
Axes of the slice: x: 2, y: 2, z: 4, core: 2. Of those that a mesh axis runs over, the one named last changes fastest.
Arguments:
- features: bfloat16 [32, 1536, 512], P('slots', 'tm'), may hold values from -6 to 6
- lengths: int32 [32], P('slots'), may hold values from 50 to 1536, as said below
- cotangent: bfloat16 [32, 1536, 512], P('slots', 'tm'), may hold values from -6 to 6
- front_gain: bfloat16 [512], P('slots'), may hold values from 0.5 to 1.5
- front_in: bfloat16 [512, 2048], P('slots'), may hold values from -0.25 to 0.25
- front_out: bfloat16 [2048, 512], P('slots'), may hold values from -0.25 to 0.25
- mixer_gain: bfloat16 [512], P('slots'), may hold values from 0.5 to 1.5
- query_weight: bfloat16 [512, 512], P('slots'), may hold values from -0.25 to 0.25
- key_weight: bfloat16 [512, 512], P('slots'), may hold values from -0.25 to 0.25
- value_weight: bfloat16 [512, 512], P('slots'), may hold values from -0.25 to 0.25
- output_weight: bfloat16 [512, 512], P('slots'), may hold values from -1 to 1
- conv_gain: bfloat16 [512], P('slots'), may hold values from 0.5 to 1.5
- expand_weight: bfloat16 [512, 1024], P('slots'), may hold values from -0.25 to 0.25
- depth_weight: bfloat16 [512, 31], P('slots'), may hold values from -1 to 1
- batch_gain: bfloat16 [512], P('slots'), may hold values from 0.5 to 1.5
- batch_bias: bfloat16 [512], P('slots'), may hold values from -3 to 3
- project_weight: bfloat16 [512, 512], P('slots'), may hold values from -0.25 to 0.25
- back_gain: bfloat16 [512], P('slots'), may hold values from 0.5 to 1.5
- back_in: bfloat16 [512, 2048], P('slots'), may hold values from -0.25 to 0.25
- back_out: bfloat16 [2048, 512], P('slots'), may hold values from -0.25 to 0.25
- final_gain: bfloat16 [512], P('slots'), may hold values from 0.5 to 1.5
Outputs:
- output: bfloat16 [32, 1536, 512], P('slots', 'tm')
- grad_features: bfloat16 [32, 1536, 512], P('slots', 'tm')
- grad_front_gain: float32 [512], P('slots')
- grad_front_in: float32 [512, 2048], P('slots')
- grad_front_out: float32 [2048, 512], P('slots')
- grad_mixer_gain: float32 [512], P('slots')
- grad_query_weight: float32 [512, 512], P('slots')
- grad_key_weight: float32 [512, 512], P('slots')
- grad_value_weight: float32 [512, 512], P('slots')
- grad_output_weight: float32 [512, 512], P('slots')
- grad_conv_gain: float32 [512], P('slots')
- grad_expand_weight: float32 [512, 1024], P('slots')
- grad_depth_weight: float32 [512, 31], P('slots')
- grad_batch_gain: float32 [512], P('slots')
- grad_batch_bias: float32 [512], P('slots')
- grad_project_weight: float32 [512, 512], P('slots')
- grad_back_gain: float32 [512], P('slots')
- grad_back_in: float32 [512, 2048], P('slots')
- grad_back_out: float32 [2048, 512], P('slots')
- grad_final_gain: float32 [512], P('slots')
The draws below stay inside these ranges and needn't reach their ends.
Inputs may be any that keep to these rules, and one draw needn't show every extreme that they name: `lengths`: in each aligned block of 8 slots (the slots of one index of slots) one length or more equals 1536.
All inputs are finite; a program needn't handle non-finite values.
Results may differ from the reference program's by a relative error of at most 0.022.
Values may be sent and summed in bfloat16 or wider, within the bound.
A program may use at most 320 MiB of HBM per device.

```python
import math
import jax
import jax.numpy as jnp
from jax import lax

D = 512
FF = 2048
HEADS = 8
HEAD_DIM = 64
KERNEL = 31
HALF = 15
LEN = 1536
MIN_LEN = 50
UTT_DEV = 8
UTTERANCES = 32


def draw_lengths(key, part):
    key = jax.random.fold_in(key, 11)
    key_first, key_second, key_pick = jax.random.split(key, 3)
    first_draw = jax.random.randint(key_first, (UTTERANCES,), 0, 1024)
    second_draw = jax.random.randint(key_second, (UTTERANCES,), 0, 1024)
    span_frames = LEN - MIN_LEN
    ragged = MIN_LEN + span_frames * first_draw // 1024 * second_draw // 1024
    picked = jax.random.randint(key_pick, (UTTERANCES // UTT_DEV,), 0, UTT_DEV)
    slot_place = jnp.arange(UTTERANCES, dtype=jnp.int32)
    longest = slot_place % UTT_DEV == jnp.repeat(picked, UTT_DEV)
    return jnp.where(longest, LEN, ragged).astype(jnp.int32)


def block_scale(own_key, extent, cuts, smallest, high):
    def one(position, parts):
        draws = jax.random.uniform(jax.random.fold_in(jax.random.fold_in(own_key, 6), position), (parts,), jnp.float32, smallest / len(cuts), high / len(cuts))
        return jnp.repeat(jnp.exp(draws), extent[position] // parts).reshape((-1,) + (1,) * (len(extent) - position - 1))

    factor_of = one(*cuts[0])
    for cut in cuts[1:]:
        factor_of = factor_of * one(*cut)
    return factor_of


def gaussian(stream_key, extent, scale, bound, cuts=(), kind=jnp.bfloat16):
    entries = scale * jax.random.normal(stream_key, extent, jnp.float32)
    if cuts:
        entries = entries * block_scale(stream_key, extent, cuts, -0.22, 0.18)
    return jnp.clip(entries, -bound, bound).astype(kind)


def setup_inputs(seed: int = 0) -> dict:
    streams_of = jax.random.split(jax.random.key(seed), 22)
    features = gaussian(streams_of[0], (UTTERANCES, LEN, D), 1.0, 6.0, ((0, 4), (1, 8)))
    lengths = draw_lengths(jax.random.fold_in(streams_of[21], 71), 0)
    cotangent = gaussian(streams_of[2], (UTTERANCES, LEN, D), 1.0, 6.0, ((0, 4), (1, 8)))
    front_gain = jnp.clip(1.0 + 0.1 * jax.random.normal(streams_of[3], (D,), jnp.float32), 0.5, 1.5).astype(jnp.bfloat16)
    front_in = gaussian(streams_of[4], (D, FF), D ** -0.5, 0.25, ((0, 4),))
    front_out = gaussian(streams_of[5], (FF, D), (FF // 4) ** -0.5, 0.25, ((0, 4),))
    mixer_gain = jnp.clip(1.0 + 0.1 * jax.random.normal(streams_of[6], (D,), jnp.float32), 0.5, 1.5).astype(jnp.bfloat16)
    query_weight = gaussian(streams_of[7], (D, D), D ** -0.5, 0.25, ((0, 4),))
    key_weight = gaussian(streams_of[8], (D, D), D ** -0.5, 0.25, ((0, 4),))
    value_weight = gaussian(streams_of[9], (D, D), D ** -0.5, 0.25, ((0, 4),))
    output_weight = gaussian(streams_of[10], (D, D), (D // 16) ** -0.5, 1.0, ((0, 4),))
    conv_gain = jnp.clip(1.0 + 0.1 * jax.random.normal(streams_of[11], (D,), jnp.float32), 0.5, 1.5).astype(jnp.bfloat16)
    expand_weight = gaussian(streams_of[12], (D, 2 * D), D ** -0.5, 0.25, ((0, 4),))
    depth_weight = gaussian(streams_of[13], (D, KERNEL), KERNEL ** -0.5, 1.0, ((0, 4),))
    batch_gain = jnp.clip(1.0 + 0.1 * jax.random.normal(streams_of[14], (D,), jnp.float32), 0.5, 1.5).astype(jnp.bfloat16)
    batch_bias = gaussian(streams_of[15], (D,), 0.5, 3.0, ((0, 4),))
    project_weight = gaussian(streams_of[16], (D, D), D ** -0.5, 0.25, ((0, 4),))
    back_gain = jnp.clip(1.0 + 0.1 * jax.random.normal(streams_of[17], (D,), jnp.float32), 0.5, 1.5).astype(jnp.bfloat16)
    back_in = gaussian(streams_of[18], (D, FF), D ** -0.5, 0.25, ((0, 4),))
    back_out = gaussian(streams_of[19], (FF, D), (FF // 4) ** -0.5, 0.25, ((0, 4),))
    final_gain = jnp.clip(1.0 + 0.1 * jax.random.normal(streams_of[20], (D,), jnp.float32), 0.5, 1.5).astype(jnp.bfloat16)
    return dict(features=features, lengths=lengths, cotangent=cotangent, front_gain=front_gain, front_in=front_in, front_out=front_out, mixer_gain=mixer_gain, query_weight=query_weight, key_weight=key_weight, value_weight=value_weight, output_weight=output_weight, conv_gain=conv_gain, expand_weight=expand_weight, depth_weight=depth_weight, batch_gain=batch_gain, batch_bias=batch_bias, project_weight=project_weight, back_gain=back_gain, back_in=back_in, back_out=back_out, final_gain=final_gain)


@jax.custom_vjp
def low(v):
    return lax.optimization_barrier(v.astype(jnp.bfloat16)).astype(jnp.float32)

@jax.custom_vjp
def low_back(v):
    return v

def low_keep(v):
    return (low(v), None)

def low_pass(kept, grad):
    return (grad,)

def back_keep(v):
    return (v, None)

def back_low(kept, grad):
    return (low(grad),)
low.defvjp(low_keep, low_pass)
low_back.defvjp(back_keep, back_low)
EPSILON = 1e-05
HIGHEST_PRECISION = lax.Precision.HIGHEST

def layer_norm(inputs, norm_gain):
    centred = inputs - lax.optimization_barrier(jnp.mean(inputs, -1, keepdims=True))
    spread = lax.optimization_barrier(jnp.mean(centred * centred, -1, keepdims=True))
    return centred * lax.rsqrt(spread + EPSILON) * norm_gain

def matmul(left_side, right_side):
    return jnp.dot(left_side, right_side, precision=HIGHEST_PRECISION)

def feed_forward(residual_rows, norm_gain, w_in, w_out):
    normed = low(layer_norm(residual_rows, norm_gain))
    hidden = low(jax.nn.silu(low_back(matmul(normed, w_in))))
    return residual_rows + 0.5 * low_back(matmul(hidden, w_out))

def attend_one(inputs):
    queries, key_rows, value_rows, length = inputs
    score_scale = 1.0 / math.sqrt(HEAD_DIM)
    places = jnp.arange(LEN, dtype=jnp.int32)
    slopes = 64.0 * 2.0 ** (-jnp.arange(HEADS).astype(jnp.float32)) / LEN
    distance = jnp.abs(places[:, None] - places[None, :]).astype(jnp.float32)
    raw_scores = jnp.einsum('qhd,khd->hqk', queries, key_rows, precision=HIGHEST_PRECISION)
    scores = low_back(raw_scores) * score_scale - slopes[:, None, None] * distance
    usable = (places < length)[None, None, :]
    scores = jnp.where(usable, scores, -1e+30)
    row_max = lax.optimization_barrier(jnp.max(scores, -1, keepdims=True))
    unnormed = jnp.where(usable, jnp.exp(scores - row_max), 0.0)
    probs = unnormed / lax.optimization_barrier(jnp.sum(unnormed, -1, keepdims=True))
    return jnp.einsum('hqk,khd->qhd', low(probs), value_rows, precision=HIGHEST_PRECISION)

def mixer(residual_rows, lengths, norm_gain, w_query, w_key, w_value, w_output):
    normed = low(layer_norm(residual_rows, norm_gain))
    shape_heads = (residual_rows.shape[0], LEN, HEADS, HEAD_DIM)
    queries = low(low_back(matmul(normed, w_query))).reshape(shape_heads)
    key_rows = low(low_back(matmul(normed, w_key))).reshape(shape_heads)
    value_rows = low(low_back(matmul(normed, w_value))).reshape(shape_heads)
    attended = lax.map(jax.checkpoint(attend_one), (queries, key_rows, value_rows, lengths))
    mixture = low(low_back(attended.reshape(residual_rows.shape)))
    return residual_rows + low_back(matmul(mixture, w_output))

def convolve(residual_rows, frame_mask, norm_gain, w_expand, w_depth, b_gain, b_bias, w_project):
    normed = low(layer_norm(residual_rows, norm_gain))
    expand = low_back(matmul(normed, w_expand))
    linear_half = expand[..., :D]
    gate_half = expand[..., D:]
    gated = low(low_back(linear_half * jax.nn.sigmoid(gate_half) * frame_mask[..., None]))
    padded = jnp.pad(gated, ((0, 0), (HALF, HALF), (0, 0)))
    filtered = padded[:, 0:LEN, :] * w_depth[:, 0]
    for kernel_tap in range(1, KERNEL):
        filtered = filtered + padded[:, kernel_tap:kernel_tap + LEN, :] * w_depth[:, kernel_tap]
    mask_cells = frame_mask[..., None]
    frames_total = jnp.sum(frame_mask)
    middle = lax.optimization_barrier(jnp.sum(filtered * mask_cells, axis=(0, 1))) / frames_total
    offset = filtered - middle
    spread = lax.optimization_barrier(jnp.sum(mask_cells * offset * offset, axis=(0, 1))) / frames_total
    batch_normed = offset * lax.rsqrt(spread + EPSILON) * b_gain + b_bias
    swish = low(jax.nn.silu(batch_normed))
    return residual_rows + low_back(matmul(swish, w_project))

def reference(features, lengths, cotangent, front_gain, front_in, front_out, mixer_gain, query_weight, key_weight, value_weight, output_weight, conv_gain, expand_weight, depth_weight, batch_gain, batch_bias, project_weight, back_gain, back_in, back_out, final_gain):
    params = tuple((item.astype(jnp.float32) for item in (front_gain, front_in, front_out, mixer_gain, query_weight, key_weight, value_weight, output_weight, conv_gain, expand_weight, depth_weight, batch_gain, batch_bias, project_weight, back_gain, back_in, back_out, final_gain)))
    inputs_f32 = features.astype(jnp.float32)
    frame_mask = (jnp.arange(LEN, dtype=jnp.int32)[None, :] < lengths[:, None]).astype(jnp.float32)

    def forward(frames, weights):
        after_front = feed_forward(frames, weights[0], weights[1], weights[2])
        after_mixer = mixer(after_front, lengths, weights[3], weights[4], weights[5], weights[6], weights[7])
        after_conv = convolve(after_mixer, frame_mask, weights[8], weights[9], weights[10], weights[11], weights[12], weights[13])
        after_back = feed_forward(after_conv, weights[14], weights[15], weights[16])
        return layer_norm(after_back, weights[17])
    result, pullback = jax.vjp(forward, inputs_f32, params)
    grad_inputs, grads = pullback(cotangent.astype(jnp.float32))
    return (result.astype(jnp.bfloat16), grad_inputs.astype(jnp.bfloat16), grads[0], grads[1], grads[2], grads[3], grads[4], grads[5], grads[6], grads[7], grads[8], grads[9], grads[10], grads[11], grads[12], grads[13], grads[14], grads[15], grads[16], grads[17])
```

```python
import functools
import math

import jax
import jax.numpy as jnp
from jax import lax
from jax.experimental import pallas as pl
from jax.experimental.pallas import tpu as pltpu
from jax.sharding import PartitionSpec as P

HEADS = 8


EPSILON = 1e-05
MESH = pl.DeviceIdType.MESH
KEY_BLOCK = 256
QUERY_BLOCK = 256
MASKED = -1e30
HALO = 16
CORE_PAIRS = [(0, 1), (1, 0), (2, 3), (3, 2)]


def remote(src, dst, send_sem, recv_sem, where):
    return pltpu.make_async_remote_copy(
        src_ref=src,
        dst_ref=dst,
        send_sem=send_sem,
        recv_sem=recv_sem,
        device_id=where,
        device_id_type=MESH,
    )


def entry_kernel(count, *refs):
    feat, shards = refs[0], refs[1 : 1 + count]
    feat_out, fulls = refs[1 + count], refs[2 + count : 2 + 2 * count]
    (a_send, a_recv, y_send, y_recv, c_send, c_recv, f_send, f_recv, local) = refs[2 + 2 * count :]
    me, n = lax.axis_index("tm"), lax.axis_size("tm")
    s = lax.axis_index("slots")
    sibling = s + 1 - 2 * lax.rem(s, 2)
    across = lax.rem(s + 2, 4)
    frames = feat.shape[1]

    barrier = pltpu.get_barrier_semaphore()
    for k in range(1, n):
        pl.semaphore_signal(
            barrier, inc=1, device_id={"tm": lax.rem(me + k, n)}, device_id_type=MESH
        )
    pl.semaphore_signal(barrier, inc=1, device_id={"slots": sibling}, device_id_type=MESH)
    pl.semaphore_signal(barrier, inc=1, device_id={"slots": across}, device_id_type=MESH)
    pl.semaphore_wait(barrier, n + 1)

    def block(ref, shard, owner):
        rows = shard.shape[0]
        return ref.at[pl.ds(owner * rows, rows)]

    y_copies, c_copies, locals_ = [], [], []
    for i in range(count):
        mine = block(fulls[i], shards[i], s)
        y_copies.append(remote(shards[i], mine, y_send.at[i], y_recv.at[i], {"slots": across}))
        y_copies[-1].start()
    a_copies = []
    for k in sorted(range(1, n), key=lambda k: abs(k - n / 2)):
        to = lax.rem(me + k, n)
        a_copies.append(
            remote(
                feat.at[to],
                feat_out.at[pl.ds(me * frames, frames)],
                a_send.at[k],
                a_recv.at[k],
                {"tm": to},
            )
        )
        a_copies[-1].start()
    for i in range(count):
        mine = block(fulls[i], shards[i], s)
        c_copies.append(remote(shards[i], mine, c_send.at[i], c_recv.at[i], {"slots": sibling}))
        c_copies[-1].start()
        locals_.append(pltpu.make_async_copy(shards[i], mine, local.at[i]))
        locals_[-1].start()
    locals_.append(
        pltpu.make_async_copy(
            feat.at[me], feat_out.at[pl.ds(me * frames, frames)], local.at[count]
        )
    )
    locals_[-1].start()
    f_copies = []
    for i in range(count):
        y_copies[i].wait_recv()
        theirs = block(fulls[i], shards[i], across)
        f_copies.append(remote(theirs, theirs, f_send.at[i], f_recv.at[i], {"slots": sibling}))
        f_copies[-1].start()
    for copy in y_copies:
        copy.wait_send()
    for copy in c_copies + f_copies + a_copies + locals_:
        copy.wait()


def entry_exchange(feat, shards):
    n, frames, width = feat.shape
    count = len(shards)
    dma = pltpu.SemaphoreType.DMA
    return pl.pallas_call(
        functools.partial(entry_kernel, count),
        out_shape=[jax.ShapeDtypeStruct((n * frames, width), feat.dtype)]
        + [jax.ShapeDtypeStruct((4 * w.shape[0],) + w.shape[1:], w.dtype) for w in shards],
        in_specs=[pl.BlockSpec(memory_space=pltpu.VMEM)] * (1 + count),
        out_specs=[pl.BlockSpec(memory_space=pl.ANY)] * (1 + count),
        scratch_shapes=[dma((n,)), dma((n,))] + [dma((count,))] * 6 + [dma((count + 1,))],
        compiler_params=pltpu.CompilerParams(collective_id=0, has_side_effects=True),
        name="entry_exchange",
    )(feat, *shards)


def stats_kernel(combine, x_ref, o_ref, near, far, mid, send, recv):
    t, s = lax.axis_index("tm"), lax.axis_index("slots")
    n, m = lax.axis_size("tm"), lax.axis_size("slots")
    barrier = pltpu.get_barrier_semaphore()
    slot_places = [{"slots": lax.rem(s + k, m)} for k in range(1, m)]
    tm_places = [{"tm": lax.rem(t + k, n)} for k in range(1, n)]
    for place in slot_places + tm_places:
        pl.semaphore_signal(barrier, inc=1, device_id=place, device_id_type=MESH)
    pl.semaphore_wait(barrier, n + m - 2)

    def share(source, landing, places, first):
        copies = []
        for i, place in enumerate(places):
            copies.append(
                remote(source, landing.at[i], send.at[first + i], recv.at[first + i], place)
            )
            copies[-1].start()
        for copy in copies:
            copy.wait()
        return combine([source[...]] + [landing[i] for i in range(len(places))])

    mid[...] = share(x_ref, near, slot_places, 0)
    o_ref[...] = share(mid, far, tm_places, m - 1)


def add_blocks(blocks):
    total = blocks[0]
    for block in blocks[1:]:
        total = total + block
    return total


def merge_spreads(blocks):
    sums = add_blocks([b[0:1] for b in blocks])
    counts = add_blocks([b[2:3] for b in blocks])
    mean = sums / counts
    squares = add_blocks(
        [b[1:2] + b[2:3] * (b[0:1] / b[2:3] - mean) * (b[0:1] / b[2:3] - mean) for b in blocks]
    )
    return jnp.concatenate((sums, squares, counts, jnp.zeros((5,) + sums.shape[1:], sums.dtype)), 0)


def share_stats(block, combine, collective_id):
    n, m = lax.axis_size("tm"), lax.axis_size("slots")
    return pl.pallas_call(
        functools.partial(stats_kernel, combine),
        out_shape=jax.ShapeDtypeStruct(block.shape, block.dtype),
        in_specs=[pl.BlockSpec(memory_space=pltpu.VMEM)],
        out_specs=pl.BlockSpec(memory_space=pltpu.VMEM),
        scratch_shapes=[
            pltpu.VMEM((m - 1,) + block.shape, block.dtype),
            pltpu.VMEM((n - 1,) + block.shape, block.dtype),
            pltpu.VMEM(block.shape, block.dtype),
            pltpu.SemaphoreType.DMA((n + m - 2,)),
            pltpu.SemaphoreType.DMA((n + m - 2,)),
        ],
        compiler_params=pltpu.CompilerParams(collective_id=collective_id, has_side_effects=True),
        name="share_stats",
    )(block)


def permute_kernel(places, x_ref, o_ref, held, load, store):
    n = x_ref.shape[0]
    loads = [pltpu.make_async_copy(x_ref.at[places[i]], held.at[i], load.at[i]) for i in range(n)]
    stores = [pltpu.make_async_copy(held.at[i], o_ref.at[i], store.at[i]) for i in range(n)]
    for copy in loads:
        copy.start()
    for i in range(n):
        loads[i].wait()
        stores[i].start()
    for copy in stores:
        copy.wait()


def take_slots(x, places):
    n = x.shape[0]
    return pl.pallas_call(
        permute_kernel,
        out_shape=jax.ShapeDtypeStruct(x.shape, x.dtype),
        grid_spec=pltpu.PrefetchScalarGridSpec(
            num_scalar_prefetch=1,
            grid=(1,),
            in_specs=[pl.BlockSpec(memory_space=pl.ANY)],
            out_specs=pl.BlockSpec(memory_space=pl.ANY),
            scratch_shapes=[
                pltpu.VMEM(x.shape, x.dtype),
                pltpu.SemaphoreType.DMA((n,)),
                pltpu.SemaphoreType.DMA((n,)),
            ],
        ),
        cost_estimate=pl.CostEstimate(flops=0, bytes_accessed=2 * x.size * 2, transcendentals=0),
        name="take_slots",
    )(places, x)


def split_parts(x):
    high = x.astype(jnp.bfloat16).astype(jnp.float32)
    rest = x - high
    middle = rest.astype(jnp.bfloat16).astype(jnp.float32)
    return high, middle, rest - middle


def dot_nn(a, b):
    return jnp.dot(a, b, preferred_element_type=jnp.float32)


def dot_nt(a, b):
    return lax.dot_general(a, b, (((1,), (1,)), ((), ())), preferred_element_type=jnp.float32)


def fill_bias(table, slope, blocks, span):
    rows = lax.broadcasted_iota(jnp.int32, (KEY_BLOCK, KEY_BLOCK), 0)
    lanes = lax.broadcasted_iota(jnp.int32, (KEY_BLOCK, KEY_BLOCK), 1)
    relative = (rows - lanes + (span - KEY_BLOCK)).astype(jnp.float32)

    def fill(c, carry):
        at = pl.multiple_of(c * KEY_BLOCK, KEY_BLOCK)
        table[:, pl.ds(at, KEY_BLOCK)] = slope * jnp.abs(relative - at.astype(jnp.float32))
        return carry

    lax.fori_loop(span // KEY_BLOCK - blocks, 2 * span // KEY_BLOCK - 1, fill, 0)


def lane_rows(span):
    lane = lax.broadcasted_iota(jnp.int32, (1, 128), 1)
    first = (lane < 64).astype(jnp.float32)
    return (first, 1.0 - first), lax.rem(lane, 64)


def one_hot(place, low, high):
    return ((place >= low) & (place < high)).astype(jnp.float32)


def key_tile(k, sel, place, length):
    row = lax.broadcasted_iota(jnp.int32, (k.shape[0], 1), 0)
    masked = jnp.where(row < length, 0.0, MASKED)
    extra = (1.0 - sel) * (one_hot(place, 1, 4) + masked * one_hot(place, 0, 1))
    return k * sel.astype(jnp.bfloat16) + extra.astype(jnp.bfloat16)


def block_count(length):
    return (length + KEY_BLOCK - 1) // KEY_BLOCK


def attend_kernel(
    lengths, slopes, *refs
):
    qkv, (own_att, near_att, own_qa, near_qa) = (refs[0:3], refs[3:6]), refs[6:10]
    table, qa, ka, vt, acc, top = refs[10:]
    span = own_att.shape[0]
    pair = pl.program_id(0)
    sels, place = lane_rows(span)
    counts = [block_count(lengths[u]) for u in range(2)]
    most = jnp.maximum(counts[0], counts[1])
    for h in range(2):
        fill_bias(table.at[h], slopes[2 * pair + h], most, span)
    ones = jnp.ones((16, span), jnp.bfloat16)
    for u in range(2):
        q, k, v = (r[...] for r in qkv[u])
        v_turned = jnp.transpose(v)
        for h in range(2):
            query_extra = (1.0 - sels[h]) * one_hot(place, 0, 1)
            qa[u, h] = q * (sels[h] * 0.125).astype(jnp.bfloat16) + query_extra.astype(jnp.bfloat16)
            ka[u, h] = key_tile(k, sels[h], place, lengths[u])
            vt[u, h, 0:64] = v_turned[64 * h : 64 * h + 64]
            vt[u, h, 64:80] = ones
    acc[...] = jnp.zeros_like(acc)
    top[...] = jnp.full_like(top, -3e38)

    def step(i, carry):
        u = (i >= counts[0]).astype(jnp.int32)
        at = pl.multiple_of((i - u * counts[0]) * KEY_BLOCK, KEY_BLOCK)
        x0 = pl.multiple_of((span - KEY_BLOCK) - at, KEY_BLOCK)
        for h in range(2):
            s = dot_nt(ka[u, h, pl.ds(at, KEY_BLOCK), :], qa[u, h]) - table[h, :, pl.ds(x0, span)]
            old = top[u, h, 0:1]
            new = jnp.maximum(old, jnp.max(s, axis=0, keepdims=True))
            p = jnp.exp(s - new).astype(jnp.bfloat16)
            top[u, h, 0:1] = new
            acc[u, h] = acc[u, h] * jnp.exp(old - new) + dot_nn(
                vt[u, h, :, pl.ds(at, KEY_BLOCK)], p
            )
        return carry

    lax.fori_loop(0, counts[0] + counts[1], step, 0)
    for u, att, qa_out in ((0, own_att, own_qa), (1, near_att, near_qa)):
        attended, extras = [], []
        for h in range(2):
            total = acc[u, h, 64:65, :]
            attended.append((acc[u, h, 0:64, :] / total).astype(jnp.bfloat16))
            parts = split_parts(-(top[u, h, 0:1, :] + jnp.log(total)))
            extras.append(
                jnp.concatenate(
                    (jnp.zeros_like(total),) + parts + (jnp.zeros((60, span), jnp.float32),), 0
                ).astype(jnp.bfloat16)
            )
        att[...] = jnp.transpose(jnp.concatenate(attended, 0))
        query_extra = jnp.transpose(jnp.concatenate((extras[1], extras[0]), 0))
        for h in range(2):
            qa_out[h] = qa[u, h] + query_extra * (1.0 - sels[h]).astype(jnp.bfloat16)


def pair_columns(span, pairs, which):
    return pl.BlockSpec((span, 128), lambda p, *_: (0, which * pairs + p))


def attend(own_qkv, near_qkv, lengths, slopes):
    span, columns = own_qkv.shape
    pairs = columns // 384
    cells = span * span * pairs * 2
    table_width = 2 * span - KEY_BLOCK
    columns3 = [pair_columns(span, pairs, i) for i in range(3)]
    tall = pl.BlockSpec((span, 128), lambda p, *_: (0, p))
    heads = pl.BlockSpec((2, span, 128), lambda p, *_: (p, 0, 0))
    return pl.pallas_call(
        attend_kernel,
        out_shape=[jax.ShapeDtypeStruct((span, pairs * 128), jnp.bfloat16)] * 2
        + [jax.ShapeDtypeStruct((2 * pairs, span, 128), jnp.bfloat16)] * 2,
        grid_spec=pltpu.PrefetchScalarGridSpec(
            num_scalar_prefetch=2,
            grid=(pairs,),
            in_specs=columns3 * 2,
            out_specs=[tall, tall, heads, heads],
            scratch_shapes=[
                pltpu.VMEM((2, KEY_BLOCK, table_width), jnp.float32),
                pltpu.VMEM((2, 2, span, 128), jnp.bfloat16),
                pltpu.VMEM((2, 2, span, 128), jnp.bfloat16),
                pltpu.VMEM((2, 2, 80, span), jnp.bfloat16),
                pltpu.VMEM((2, 2, 80, span), jnp.float32),
                pltpu.VMEM((2, 2, 8, span), jnp.float32),
            ],
        ),
        compiler_params=pltpu.CompilerParams(vmem_limit_bytes=56 << 20),
        cost_estimate=pl.CostEstimate(
            flops=cells * 4 * 256, bytes_accessed=span * columns * 8, transcendentals=cells
        ),
        name="attend",
    )(lengths, slopes, *([own_qkv] * 3), *([near_qkv] * 3))


def attend_back_kernel(lengths, slopes, *refs):
    inputs, outputs = (refs[0:5], refs[5:10]), (refs[10:13], refs[13:16])
    table, qa, ka, va, ga, kt, dqt, dk_out, dv_out = refs[16:]
    span = refs[1].shape[0]
    pair = pl.program_id(0)
    sels, place = lane_rows(span)
    counts = [block_count(lengths[u]) for u in range(2)]
    most = jnp.maximum(counts[0], counts[1])
    for h in range(2):
        fill_bias(table.at[h], slopes[2 * pair + h], most, span)
    side = lax.broadcasted_iota(jnp.int32, (128, 128), 0) < 64
    other = lax.broadcasted_iota(jnp.int32, (128, 128), 1) >= 64
    gather = jnp.where(side == other, 1.0, 0.0).astype(jnp.bfloat16)
    for u in range(2):
        qa_in, k_in, v_in, g_in, att_in = inputs[u]
        k, v, g = k_in[...], v_in[...], g_in[...]
        product = g.astype(jnp.float32) * att_in[...].astype(jnp.float32)
        high = product.astype(jnp.bfloat16)
        low = (product - high.astype(jnp.float32)).astype(jnp.bfloat16)
        delta = split_parts(dot_nn(high, gather) + dot_nn(low, gather))
        grad_extra = sum(
            delta[i].astype(jnp.bfloat16) * one_hot(place, i, i + 1).astype(jnp.bfloat16)
            for i in range(3)
        )
        kt[u] = jnp.transpose(k)
        for h in range(2):
            sel = sels[h].astype(jnp.bfloat16)
            rest = (1.0 - sels[h]).astype(jnp.bfloat16)
            qa[u, h] = qa_in[h]
            ka[u, h] = key_tile(k, sels[h], place, lengths[u])
            va[u, h] = v * sel - ((1.0 - sels[h]) * one_hot(place, 0, 3)).astype(jnp.bfloat16)
            ga[u, h] = g * sel + grad_extra * rest
    dqt[...] = jnp.zeros_like(dqt)
    block_lane = lax.broadcasted_iota(jnp.int32, (KEY_BLOCK, 128), 1)

    def step(i, carry):
        u = (i >= counts[0]).astype(jnp.int32)
        at = pl.multiple_of((i - u * counts[0]) * KEY_BLOCK, KEY_BLOCK)
        keys = pl.ds(at, KEY_BLOCK)
        x0 = pl.multiple_of((span - KEY_BLOCK) - at, KEY_BLOCK)
        dk, dv = [], []
        for h in range(2):
            query_rows, grad_rows = qa[u, h], ga[u, h]
            s = dot_nt(ka[u, h, keys, :], query_rows)
            p = jnp.exp(s - table[h, :, pl.ds(x0, span)])
            d = (p * dot_nt(va[u, h, keys, :], grad_rows)).astype(jnp.bfloat16)
            dv.append(dot_nn(p.astype(jnp.bfloat16), grad_rows))
            dk.append(dot_nn(d, query_rows))
            rows = slice(64 * h, 64 * h + 64)
            dqt[u, rows] += dot_nn(kt[u, rows, keys], d)
        dk_out[u, keys, :] = jnp.where(block_lane < 64, dk[0], dk[1]).astype(jnp.bfloat16)
        dv_out[u, keys, :] = jnp.where(block_lane < 64, dv[0], dv[1]).astype(jnp.bfloat16)
        return carry

    lax.fori_loop(0, counts[0] + counts[1], step, 0)
    for u in range(2):

        def blank(b, carry, u=u):
            keys = pl.ds(pl.multiple_of(b * KEY_BLOCK, KEY_BLOCK), KEY_BLOCK)
            dk_out[u, keys, :] = jnp.zeros((KEY_BLOCK, 128), jnp.bfloat16)
            dv_out[u, keys, :] = jnp.zeros((KEY_BLOCK, 128), jnp.bfloat16)
            return carry

        lax.fori_loop(counts[u], span // KEY_BLOCK, blank, 0)
        dq_ref, dk_ref, dv_ref = outputs[u]
        dk_ref[...] = dk_out[u]
        dv_ref[...] = dv_out[u]
        dq_ref[...] = jnp.transpose((dqt[u] * 0.125).astype(jnp.bfloat16))


def attend_back(own, near, lengths, slopes):
    span, columns = own[1].shape
    pairs = columns // 384
    cells = span * span * pairs * 2
    table_width = 2 * span - KEY_BLOCK
    tall = pl.BlockSpec((span, 128), lambda p, *_: (0, p))
    heads = pl.BlockSpec((2, span, 128), lambda p, *_: (p, 0, 0))
    specs = [heads, pair_columns(span, pairs, 1), pair_columns(span, pairs, 2), tall, tall]
    tile = pltpu.VMEM((2, 2, span, 128), jnp.bfloat16)
    grads = pl.pallas_call(
        attend_back_kernel,
        out_shape=[jax.ShapeDtypeStruct((span, pairs * 128), jnp.bfloat16)] * 6,
        grid_spec=pltpu.PrefetchScalarGridSpec(
            num_scalar_prefetch=2,
            grid=(pairs,),
            in_specs=specs * 2,
            out_specs=[tall] * 6,
            scratch_shapes=[
                pltpu.VMEM((2, KEY_BLOCK, table_width), jnp.float32),
                tile,
                tile,
                tile,
                tile,
                pltpu.VMEM((2, 128, span), jnp.bfloat16),
                pltpu.VMEM((2, 128, span), jnp.float32),
                pltpu.VMEM((2, span, 128), jnp.bfloat16),
                pltpu.VMEM((2, span, 128), jnp.bfloat16),
            ],
        ),
        compiler_params=pltpu.CompilerParams(vmem_limit_bytes=56 << 20),
        cost_estimate=pl.CostEstimate(
            flops=cells * 10 * 256, bytes_accessed=span * columns * 16, transcendentals=cells
        ),
        name="attend_back",
    )(
        lengths, slopes,
        own[0], own[1], own[1], own[2], own[3],
        near[0], near[1], near[1], near[2], near[3],
    )
    return grads[:3], grads[3:]


CHUNK = 64


def filter_kernel(taps_count, scalars, gated_ref, taps_ref, out_ref, stats_ref, padded):
    span = gated_ref.shape[0]
    half = taps_count // 2
    length = scalars[0]
    padded[0:HALO] = jnp.zeros((HALO, 128), jnp.float32)
    padded[HALO + span : HALO + span + HALO] = jnp.zeros((HALO, 128), jnp.float32)
    padded[HALO : HALO + span] = gated_ref[...].astype(jnp.float32)

    def chunk(c, total):
        at = pl.multiple_of(c * CHUNK, CHUNK)
        value = jnp.zeros((CHUNK, 128), jnp.float32)
        for k in range(taps_count):
            value = value + padded[pl.ds(at + (HALO - half + k), CHUNK), :] * taps_ref[k : k + 1, :]
        out_ref[pl.ds(at, CHUNK), :] = value
        row = lax.broadcasted_iota(jnp.int32, (CHUNK, 128), 0) + at
        return total + jnp.sum(jnp.where(row < length, value, 0.0), axis=0, keepdims=True)

    total = lax.fori_loop(0, span // CHUNK, chunk, jnp.zeros((1, 128), jnp.float32))
    mean = total / length.astype(jnp.float32)

    def deviate(c, squares):
        at = pl.multiple_of(c * CHUNK, CHUNK)
        row = lax.broadcasted_iota(jnp.int32, (CHUNK, 128), 0) + at
        off = jnp.where(row < length, out_ref[pl.ds(at, CHUNK), :] - mean, 0.0)
        return squares + jnp.sum(off * off, axis=0, keepdims=True)

    squares = lax.fori_loop(0, span // CHUNK, deviate, jnp.zeros((1, 128), jnp.float32))
    stats_ref[...] = jnp.concatenate((total, squares, jnp.zeros((6, 128), jnp.float32)), 0)


def filter_frames(gated, taps, length):
    span, width = gated.shape
    return pl.pallas_call(
        functools.partial(filter_kernel, taps.shape[0]),
        out_shape=[
            jax.ShapeDtypeStruct((span, width), jnp.float32),
            jax.ShapeDtypeStruct((8, width), jnp.float32),
        ],
        grid_spec=pltpu.PrefetchScalarGridSpec(
            num_scalar_prefetch=1,
            grid=(width // 128,),
            in_specs=[
                pl.BlockSpec((span, 128), lambda c, *_: (0, c)),
                pl.BlockSpec((taps.shape[0], 128), lambda c, *_: (0, c)),
            ],
            out_specs=[
                pl.BlockSpec((span, 128), lambda c, *_: (0, c)),
                pl.BlockSpec((8, 128), lambda c, *_: (0, c)),
            ],
            scratch_shapes=[pltpu.VMEM((span + 2 * HALO, 128), jnp.float32)],
        ),
        cost_estimate=pl.CostEstimate(
            flops=64 * span * width, bytes_accessed=6 * span * width, transcendentals=0
        ),
        name="filter_frames",
    )(length, gated, taps)


def filter_back_kernel(
    taps_count, scalars, filtered_ref, dbn_ref, gated_ref, taps_ref, rows_ref, dgated_ref, dtaps_ref,
    padded, gpadded,
):
    span = gated_ref.shape[0]
    half = taps_count // 2
    length = scalars[0]
    for ref in (padded, gpadded):
        ref[0:HALO] = jnp.zeros((HALO, 128), jnp.float32)
        ref[HALO + span : HALO + span + HALO] = jnp.zeros((HALO, 128), jnp.float32)
    gpadded[HALO : HALO + span] = gated_ref[...].astype(jnp.float32)
    row = lax.broadcasted_iota(jnp.int32, (span, 128), 0)
    unit = (filtered_ref[...] - rows_ref[0:1, :]) * rows_ref[1:2, :]
    shift = rows_ref[3:4, :] + unit * rows_ref[4:5, :]
    padded[HALO : HALO + span] = rows_ref[1:2, :] * (
        dbn_ref[...] * rows_ref[2:3, :] - jnp.where(row < length, shift, 0.0)
    )

    def chunk(c, carry):
        at = pl.multiple_of(c * CHUNK, CHUNK)
        value = jnp.zeros((CHUNK, 128), jnp.float32)
        for k in range(taps_count):
            value = value + padded[pl.ds(at + (HALO + half - k), CHUNK), :] * taps_ref[k : k + 1, :]
        dgated_ref[pl.ds(at, CHUNK), :] = value.astype(jnp.bfloat16)
        return carry

    lax.fori_loop(0, span // CHUNK, chunk, 0)

    def tally(c, sums):
        at = pl.multiple_of(c * CHUNK, CHUNK)
        grad = padded[pl.ds(at + HALO, CHUNK), :]
        added = []
        for k in range(taps_count):
            term = grad * gpadded[pl.ds(at + (HALO - half + k), CHUNK), :]
            folded = term[0:8]
            for r in range(8, CHUNK, 8):
                folded = folded + term[r : r + 8]
            added.append(sums[k] + folded)
        return tuple(added)

    sums = lax.fori_loop(
        0, span // CHUNK, tally, tuple(jnp.zeros((8, 128), jnp.float32) for _ in range(taps_count))
    )
    pad = dtaps_ref.shape[0] - taps_count
    dtaps_ref[...] = jnp.concatenate(
        [jnp.sum(x, axis=0, keepdims=True) for x in sums] + [jnp.zeros((pad, 128), jnp.float32)], 0
    )


def filter_back(filtered, dbn, gated, taps, rows, length):
    span, width = gated.shape
    count = taps.shape[0]
    held = (count + 7) // 8 * 8
    tall = pl.BlockSpec((span, 128), lambda c, *_: (0, c))
    return pl.pallas_call(
        functools.partial(filter_back_kernel, count),
        out_shape=[
            jax.ShapeDtypeStruct((span, width), jnp.bfloat16),
            jax.ShapeDtypeStruct((held, width), jnp.float32),
        ],
        grid_spec=pltpu.PrefetchScalarGridSpec(
            num_scalar_prefetch=1,
            grid=(width // 128,),
            in_specs=[
                tall,
                tall,
                tall,
                pl.BlockSpec((count, 128), lambda c, *_: (0, c)),
                pl.BlockSpec((8, 128), lambda c, *_: (0, c)),
            ],
            out_specs=[tall, pl.BlockSpec((held, 128), lambda c, *_: (0, c))],
            scratch_shapes=[pltpu.VMEM((span + 2 * HALO, 128), jnp.float32)] * 2,
        ),
        cost_estimate=pl.CostEstimate(
            flops=128 * span * width, bytes_accessed=12 * span * width, transcendentals=0
        ),
        name="filter_back",
    )(length, filtered, dbn, gated, taps, rows)


def dot_tn(a, b):
    return lax.dot_general(a, b, (((0,), (0,)), ((), ())), preferred_element_type=jnp.float32)


def sigmoid(x):
    return 0.5 * jnp.tanh(0.5 * x) + 0.5


def silu_parts(x):
    s = sigmoid(x)
    value = x * s
    return value, s + value * (1.0 - s)


def normed_parts(x):
    centred = x - jnp.mean(x, -1, keepdims=True)
    scale = lax.rsqrt(jnp.mean(centred * centred, -1, keepdims=True) + EPSILON)
    return centred * scale, scale


def normed_back(n, scale, e):
    return scale * (e - jnp.mean(e, -1, keepdims=True) - n * jnp.mean(e * n, -1, keepdims=True))


def column_sum(x):
    return jnp.sum(x, axis=0, keepdims=True)


def add_rows(ref, rows):
    @pl.when(pl.program_id(0) == 0)
    def _():
        ref[...] = jnp.zeros_like(ref)

    width = ref.shape[1]
    ref[...] += jnp.concatenate(list(rows) + [jnp.zeros((8 - len(rows), width), jnp.float32)], 0)


def row_call(kernel, name, scalars, tall, whole, outs, sums, block, flops):
    span = tall[0].shape[0]

    def rows(columns):
        return pl.BlockSpec((block, columns), lambda i, *_: (i, 0))

    def kept(x):
        return pl.BlockSpec(x.shape, lambda i, *_: (0,) * x.ndim, pipeline_mode=pl.Buffered(1))

    width = whole[0].shape[-1]
    moved = sum(x.size * x.dtype.itemsize for x in tall + whole)
    moved += sum(span * c * jnp.dtype(d).itemsize for c, d in outs)
    return pl.pallas_call(
        kernel,
        out_shape=[jax.ShapeDtypeStruct((span, c), d) for c, d in outs]
        + [jax.ShapeDtypeStruct((8, width), jnp.float32)] * sums,
        grid_spec=pltpu.PrefetchScalarGridSpec(
            num_scalar_prefetch=1,
            grid=(span // block,),
            in_specs=[rows(x.shape[1]) for x in tall] + [kept(x) for x in whole],
            out_specs=[rows(c) for c, _ in outs]
            + [pl.BlockSpec((8, width), lambda i, *_: (0, 0))] * sums,
        ),
        compiler_params=pltpu.CompilerParams(vmem_limit_bytes=60 << 20),
        cost_estimate=pl.CostEstimate(
            flops=flops * span, bytes_accessed=moved, transcendentals=span * 2048
        ),
        name=name,
    )(scalars, *tall, *whole)


def head_columns(ref, which, width):
    return ref[:, pl.ds(pl.multiple_of(which * width, width), width)]


def head_rows(ref, which, width):
    return ref[pl.ds(pl.multiple_of(which * width, width), width), :]


def front_kernel(
    scalars, x_ref, gains, w_in, w_out, wq, wk, wv,
    normed_out, hidden_out, slope_out, after_out, mixer_out, own_out, far_out,
):
    core = scalars[0]
    x = x_ref[...].astype(jnp.float32)
    n, _ = normed_parts(x)
    normed = (n * gains[0:1]).astype(jnp.bfloat16)
    normed_out[...] = normed
    value, slope = silu_parts(dot_nn(normed, w_in[...]))
    hidden = value.astype(jnp.bfloat16)
    hidden_out[...] = hidden
    slope_out[...] = slope.astype(jnp.bfloat16)
    after = x + 0.5 * dot_nn(hidden, w_out[...])
    after_out[...] = after
    n, _ = normed_parts(after)
    mixer = (n * gains[1:2]).astype(jnp.bfloat16)
    mixer_out[...] = mixer
    half = wq.shape[1] // 2
    for out, which in ((far_out, 1 - core), (own_out, core)):
        for i, w in enumerate((wq, wk, wv)):
            out[:, i * half : (i + 1) * half] = dot_nn(mixer, head_columns(w, which, half)).astype(
                jnp.bfloat16
            )


def expand_kernel(
    scalars, own_ref, far_ref, after_ref, gains, w_output, w_expand,
    after_out, normed_out, gated_out, slope_out,
):
    core, length = scalars[0], scalars[1]
    block, half = own_ref.shape
    after = (
        after_ref[...]
        + dot_nn(own_ref[...], head_rows(w_output, core, half))
        + dot_nn(far_ref[...], head_rows(w_output, 1 - core, half))
    )
    after_out[...] = after
    n, _ = normed_parts(after)
    normed = (n * gains[0:1]).astype(jnp.bfloat16)
    normed_out[...] = normed
    expand = dot_nn(normed, w_expand[...])
    width = expand.shape[1] // 2
    row = lax.broadcasted_iota(jnp.int32, (block, width), 0) + pl.program_id(0) * block
    gate = sigmoid(expand[:, width:])
    live = jnp.where(row < length, gate, 0.0)
    gated = expand[:, :width] * live
    gated_out[...] = gated.astype(jnp.bfloat16)
    slope_out[:, :width] = live.astype(jnp.bfloat16)
    slope_out[:, width:] = (gated * (1.0 - gate)).astype(jnp.bfloat16)


def back_kernel(
    scalars, filtered_ref, after_ref, cot_ref, params, w_project, w_in, w_out,
    output_out, grad_out, dbn_out, swish_out, top_out, hidden_out, dpre_out, normed_out, half_out,
    sums,
):
    unit = (filtered_ref[...] - params[0:1]) * params[1:2]
    value, slope_bn = silu_parts(unit * params[2:3] + params[3:4])
    swish = value.astype(jnp.bfloat16)
    swish_out[...] = swish
    after_conv = after_ref[...] + dot_nn(swish, w_project[...])
    n1, r1 = normed_parts(after_conv)
    normed = (n1 * params[4:5]).astype(jnp.bfloat16)
    normed_out[...] = normed
    value, slope = silu_parts(dot_nn(normed, w_in[...]))
    hidden = value.astype(jnp.bfloat16)
    hidden_out[...] = hidden
    n2, r2 = normed_parts(after_conv + 0.5 * dot_nn(hidden, w_out[...]))
    output_out[...] = (n2 * params[5:6]).astype(jnp.bfloat16)

    cot = cot_ref[...].astype(jnp.float32)
    grad = normed_back(n2, r2, cot * params[5:6])
    half_grad = (0.5 * grad).astype(jnp.bfloat16)
    half_out[...] = half_grad
    dpre = (dot_nt(half_grad, w_out[...]) * slope).astype(jnp.bfloat16)
    dpre_out[...] = dpre
    dnormed = dot_nt(dpre, w_in[...])
    grad = grad + normed_back(n1, r1, dnormed * params[4:5])
    grad_out[...] = grad
    top = grad.astype(jnp.bfloat16)
    top_out[...] = top
    dbn = dot_nt(top, w_project[...]) * slope_bn
    dbn_out[...] = dbn
    add_rows(
        sums,
        [column_sum(dbn), column_sum(dbn * unit), column_sum(cot * n2), column_sum(dnormed * n1)],
    )


def glu_back_kernel(
    scalars, dgated_ref, slope_ref, grad_ref, after_ref, gains, w_expand, w_output,
    dexpand_out, grad_out, top_out, own_out, far_out, sums,
):
    core = scalars[0]
    dgated = dgated_ref[...].astype(jnp.float32)
    width = dgated.shape[1]
    slopes = slope_ref[...].astype(jnp.float32)
    dexpand = jnp.concatenate((dgated * slopes[:, :width], dgated * slopes[:, width:]), 1)
    dexpand = dexpand.astype(jnp.bfloat16)
    dexpand_out[...] = dexpand
    dnormed = dot_nt(dexpand, w_expand[...])
    n, r = normed_parts(after_ref[...])
    grad = grad_ref[...] + normed_back(n, r, dnormed * gains[0:1])
    grad_out[...] = grad
    top = grad.astype(jnp.bfloat16)
    top_out[...] = top
    half = own_out.shape[1]
    far_out[...] = dot_nt(top, head_rows(w_output, 1 - core, half)).astype(jnp.bfloat16)
    own_out[...] = dot_nt(top, head_rows(w_output, core, half)).astype(jnp.bfloat16)
    add_rows(sums, [column_sum(dnormed * n)])


def front_back_kernel(
    scalars, dq, dk, dv, fq, fk, fv, grad_ref, after_ref, x_ref, slope_ref,
    gains, w_in, w_out, wq, wk, wv, half_out, dpre_out, rows_out, sums,
):
    core = scalars[0]
    half = dq.shape[1]
    dnormed = None
    for which, grads in ((core, (dq, dk, dv)), (1 - core, (fq, fk, fv))):
        for d, w in zip(grads, (wq, wk, wv)):
            term = dot_nt(d[...], head_columns(w, which, half))
            dnormed = term if dnormed is None else dnormed + term
    n, r = normed_parts(after_ref[...])
    mixer_sum = column_sum(dnormed * n)
    grad = grad_ref[...] + normed_back(n, r, dnormed * gains[1:2])
    half_grad = (0.5 * grad).astype(jnp.bfloat16)
    half_out[...] = half_grad
    slope = slope_ref[...].astype(jnp.float32)
    dpre = (dot_nt(half_grad, w_out[...]) * slope).astype(jnp.bfloat16)
    dpre_out[...] = dpre
    dnormed = dot_nt(dpre, w_in[...])
    n, r = normed_parts(x_ref[...].astype(jnp.float32))
    rows_out[...] = (grad + normed_back(n, r, dnormed * gains[0:1])).astype(jnp.bfloat16)
    add_rows(sums, [column_sum(dnormed * n), mixer_sum])


def back_weights_kernel(hidden, half_grad, normed, dpre, swish, top, out):
    width = half_grad.shape[1]
    shard = width // 4
    quarter = hidden.shape[1]
    j = pl.program_id(0)
    out[j, 0:quarter] = dot_tn(hidden[...], half_grad[...]).astype(jnp.bfloat16)
    total = dot_tn(normed[...], dpre[...]).astype(jnp.bfloat16)
    out[:, pl.ds(pl.multiple_of(quarter + j * shard, shard), shard)] = total.reshape(4, shard, width)

    @pl.when(j == 0)
    def _():
        total = dot_tn(swish[...], top[...]).astype(jnp.bfloat16)
        out[:, quarter + 4 * shard :] = total.reshape(4, shard, width)


def back_weights(hidden, half_grad, normed, dpre, swish, top):
    span, width = half_grad.shape
    ff = hidden.shape[1]
    held = ff // 4 + ff * width // 4 // width + width // 4
    wide = pl.BlockSpec((span, ff // 4), lambda j: (0, j))
    whole = pl.BlockSpec((span, width), lambda j: (0, 0), pipeline_mode=pl.Buffered(1))
    return pl.pallas_call(
        back_weights_kernel,
        out_shape=jax.ShapeDtypeStruct((4, held, width), jnp.bfloat16),
        grid=(4,),
        in_specs=[wide, whole, whole, wide, whole, whole],
        out_specs=pl.BlockSpec((4, held, width), lambda j: (0, 0, 0)),
        compiler_params=pltpu.CompilerParams(vmem_limit_bytes=60 << 20),
        cost_estimate=pl.CostEstimate(
            flops=4 * span * ff * width + 2 * span * width * width,
            bytes_accessed=4 * span * (ff + 2 * width) + 8 * held * width,
            transcendentals=0,
        ),
        name="back_weights",
    )(hidden, half_grad, normed, dpre, swish, top)


def middle_weights_kernel(core_ref, normed, dexpand, own, far, top, out):
    width = top.shape[1]
    shard = width // 4
    core = core_ref[0]
    for j in range(2):
        total = dot_tn(normed[...], dexpand[:, j * width : (j + 1) * width]).astype(jnp.bfloat16)
        out[:, j * shard : (j + 1) * shard] = total.reshape(4, shard, width)
    for which, att in ((core, own), (1 - core, far)):
        total = dot_tn(att[...], top[...]).astype(jnp.bfloat16)
        out[pl.ds(2 * which, 2), 2 * shard :] = total.reshape(2, shard, width)


def middle_weights(core, normed, dexpand, own, far, top):
    span, width = top.shape
    whole = [pl.BlockSpec(x.shape, lambda i, *_: (0, 0)) for x in (normed, dexpand, own, far, top)]
    return pl.pallas_call(
        middle_weights_kernel,
        out_shape=jax.ShapeDtypeStruct((4, 3 * width // 4, width), jnp.bfloat16),
        grid_spec=pltpu.PrefetchScalarGridSpec(
            num_scalar_prefetch=1,
            grid=(1,),
            in_specs=whole,
            out_specs=pl.BlockSpec((4, 3 * width // 4, width), lambda i, *_: (0, 0, 0)),
        ),
        compiler_params=pltpu.CompilerParams(vmem_limit_bytes=60 << 20),
        cost_estimate=pl.CostEstimate(
            flops=6 * span * width * width, bytes_accessed=12 * span * width, transcendentals=0
        ),
        name="middle_weights",
    )(core, normed, dexpand, own, far, top)


def with_halo(block, sides, width):
    for axis, dim in sides:
        count = lax.axis_size(axis)
        forward = [(i, i + 1) for i in range(count - 1)]
        backward = [(target, source) for source, target in forward]
        low = lax.ppermute(
            lax.slice_in_dim(block, block.shape[dim] - width, None, axis=dim), axis, forward
        )
        high = lax.ppermute(lax.slice_in_dim(block, 0, width, axis=dim), axis, backward)
        block = jnp.concatenate([low, block, high], axis=dim)
    return block


def layer_norm(inputs, norm_gain):
    centred = inputs - jnp.mean(inputs, -1, keepdims=True)
    spread = jnp.mean(centred * centred, -1, keepdims=True)
    return centred * lax.rsqrt(spread + EPSILON) * norm_gain


def norm_back(inputs, norm_gain, incoming):
    result, pullback = jax.vjp(layer_norm, inputs, norm_gain)
    return pullback(incoming)


def matmul(left_side, right_side):
    return jnp.dot(left_side, right_side, preferred_element_type=jnp.float32)


def matmul_tn(left_side, right_side):
    return lax.dot_general(
        left_side, right_side, (((0,), (0,)), ((), ())), preferred_element_type=jnp.float32
    )


def matmul_nt(left_side, right_side):
    return lax.dot_general(
        left_side, right_side, (((1,), (1,)), ((), ())), preferred_element_type=jnp.float32
    )


def silu_slope(inputs):
    sigmoid_gate = jax.nn.sigmoid(inputs)
    return sigmoid_gate * (1.0 + inputs * (1.0 - sigmoid_gate))


def feed_forward(residual_rows, norm_gain, w_in, w_out):
    normed = layer_norm(residual_rows, norm_gain).astype(jnp.bfloat16)
    before_act = matmul(normed, w_in)
    hidden = jax.nn.silu(before_act).astype(jnp.bfloat16)
    return (residual_rows + 0.5 * matmul(hidden, w_out), (normed, before_act, hidden))


def feed_back(residual_rows, norm_gain, w_in, w_out, kept, incoming):
    normed, before_act, hidden = kept
    grad_top = (0.5 * incoming).astype(jnp.bfloat16)
    grad_w_out = matmul_tn(hidden, grad_top)
    grad_before = (matmul_nt(grad_top, w_out) * silu_slope(before_act)).astype(jnp.bfloat16)
    grad_w_in = matmul_tn(normed, grad_before)
    grad_normed = matmul_nt(grad_before, w_in)
    grad_rows, grad_gain = norm_back(residual_rows, norm_gain, grad_normed)
    return (incoming + grad_rows, grad_gain, grad_w_in, grad_w_out)


class Chunk:
    def __init__(self, rows, width, dtype):
        self.rows, self.width, self.dtype = rows, width, dtype

    def scratch(self):
        r, w = self.rows, self.width
        shapes = [(4, r, w), (2, r, w), (2, r, w), (r, w), (r, w), (r // 2, w), (r // 2, w)]
        shapes += [(3, r // 8, w), (r, w)]
        return [pltpu.VMEM(s, self.dtype) for s in shapes]


SCRATCH = 9
LAGS = (0, 1, 3, 5, 7, 9, 11)


def closing_kernel(chunks, feeds, produce, finish, n_out, *refs):
    inputs, rows_in = refs[:feeds], refs[feeds]
    outs, rows_out = refs[feeds + 1 : feeds + 1 + n_out], refs[feeds + 1 + n_out]
    rest = refs[feeds + 2 + n_out :]
    held, rest = rest[:feeds], rest[feeds:]
    count = len(chunks)
    bufs = [rest[SCRATCH * c : SCRATCH * (c + 1)] for c in range(count)]
    load, a_send, a_recv, one_send, one_recv, z_send, z_recv, g_send, g_recv, local = rest[
        SCRATCH * count :
    ]
    me, n = lax.axis_index("tm"), lax.axis_size("tm")
    s = lax.axis_index("slots")
    core, y = lax.rem(s, 2), lax.div(s, 2)
    x, z = lax.rem(me, 2), lax.div(me, 2)
    sibling, across = {"slots": s + 1 - 2 * core}, {"slots": lax.rem(s + 2, 4)}
    beside = {"tm": me + 1 - 2 * x}
    along = [{"tm": lax.rem(me + 2 * k, n)} for k in range(1, 4)]
    frames = rows_in.shape[0] // n

    loads = [pltpu.make_async_copy(inputs[i], held[i], load.at[i]) for i in range(feeds)]
    for copy in loads:
        copy.start()
    barrier = pltpu.get_barrier_semaphore()
    for k in range(1, n):
        pl.semaphore_signal(
            barrier, inc=1, device_id={"tm": lax.rem(me + k, n)}, device_id_type=MESH
        )
    pl.semaphore_signal(barrier, inc=1, device_id=sibling, device_id_type=MESH)
    pl.semaphore_signal(barrier, inc=1, device_id=across, device_id_type=MESH)
    pl.semaphore_wait(barrier, n + 1)

    a_copies = []
    for k in sorted(range(1, n), key=lambda k: abs(k - n / 2)):
        to = lax.rem(me + k, n)
        a_copies.append(
            remote(
                rows_in.at[pl.ds(to * frames, frames)],
                rows_out.at[me],
                a_send.at[k],
                a_recv.at[k],
                {"tm": to},
            )
        )
        a_copies[-1].start()
    own_rows = pltpu.make_async_copy(
        rows_in.at[pl.ds(me * frames, frames)], rows_out.at[me], local.at[0]
    )
    own_rows.start()

    sent = []
    going = [{} for _ in chunks]

    def start(c, name, copies):
        for copy in copies:
            copy.start()
            sent.append(copy)
        going[c][name] = copies

    def arrive(c, name):
        for copy in going[c][name]:
            copy.wait_recv()

    waited = set()

    def need(i):
        if i not in waited:
            loads[i].wait()
            waited.add(i)
        return held[i]

    def add(*terms):
        total = terms[0].astype(jnp.float32)
        for term in terms[1:]:
            total = total + term.astype(jnp.float32)
        return total

    def stage(c, k):
        part, core_in, core_sum, y_in, y_sum, x_in, x_sum, z_in, final = bufs[c]
        r = chunks[c].rows
        kind = chunks[c].dtype
        half, piece = r // 2, r // 8
        if k == 0:
            produce(c, need, part, core)
            start(c, "core", [
                remote(part.at[2 * i + 1 - core], core_in.at[i], one_send.at[c, i], one_recv.at[c, i], sibling)
                for i in range(2)
            ])
        elif k == 1:
            arrive(c, "core")
            for i in range(2):
                core_sum[i] = add(part[2 * i + core], core_in[i]).astype(kind)
            start(c, "y", [
                remote(core_sum.at[1 - y], y_in, one_send.at[c, 2], one_recv.at[c, 2], across)
            ])
        elif k == 2:
            arrive(c, "y")
            y_sum[...] = add(core_sum[y], y_in[...]).astype(kind)
            start(c, "x", [
                remote(
                    y_sum.at[pl.ds(pl.multiple_of((1 - x) * half, half), half)],
                    x_in, one_send.at[c, 3], one_recv.at[c, 3], beside,
                )
            ])
        elif k == 3:
            arrive(c, "x")
            x_sum[...] = add(y_sum[pl.ds(pl.multiple_of(x * half, half), half)], x_in[...]).astype(
                kind
            )
            start(c, "z", [
                remote(
                    x_sum.at[pl.ds(pl.multiple_of(lax.rem(z + i + 1, 4) * piece, piece), piece)],
                    z_in.at[i], z_send.at[c, i], z_recv.at[c, i], along[i],
                )
                for i in range(3)
            ])
        elif k == 4:
            arrive(c, "z")
            own = x_sum[pl.ds(pl.multiple_of(z * piece, piece), piece)]
            place = pl.ds(pl.multiple_of(x * half + z * piece, piece), piece)
            final[place] = add(own, z_in[0], z_in[1], z_in[2]).astype(kind)
            start(c, "g", [
                remote(final.at[place], final.at[place], g_send.at[c, i], g_recv.at[c, i], along[i])
                for i in range(3)
            ])
        elif k == 5:
            arrive(c, "g")
            mine = final.at[pl.ds(pl.multiple_of(x * half, half), half)]
            start(c, "h", [remote(mine, mine, one_send.at[c, 4], one_recv.at[c, 4], beside)])
        else:
            arrive(c, "h")
            finish(c, final, outs)

    for tick in range(count + LAGS[-1]):
        for k in range(6, -1, -1):
            if 0 <= tick - LAGS[k] < count:
                stage(tick - LAGS[k], k)
    for copy in sent:
        copy.wait_send()
    for copy in a_copies:
        copy.wait()
    own_rows.wait()


def closing_exchange(chunks, inputs, produce, finish, out_shapes, rows, n, collective_id, flops):
    dma = pltpu.SemaphoreType.DMA
    anywhere = pl.BlockSpec(memory_space=pl.ANY)
    count, feeds = len(chunks), len(inputs)
    scratch = [pltpu.VMEM(x.shape, x.dtype) for x in inputs]
    for chunk in chunks:
        scratch += chunk.scratch()
    scratch += [dma((feeds,)), dma((n,)), dma((n,)), dma((count, 5)), dma((count, 5))]
    scratch += [dma((count, 3))] * 4 + [dma((1,))]
    return pl.pallas_call(
        functools.partial(
            closing_kernel, chunks, feeds, produce, finish, len(out_shapes)
        ),
        out_shape=[jax.ShapeDtypeStruct(s, jnp.float32) for s in out_shapes]
        + [jax.ShapeDtypeStruct((n, rows.shape[0] // n, rows.shape[1]), rows.dtype)],
        in_specs=[anywhere] * (feeds + 1),
        out_specs=[pl.BlockSpec(memory_space=pltpu.VMEM)] * len(out_shapes) + [anywhere],
        scratch_shapes=scratch,
        compiler_params=pltpu.CompilerParams(
            collective_id=collective_id, has_side_effects=True, vmem_limit_bytes=60 << 20
        ),
        cost_estimate=pl.CostEstimate(
            flops=flops, bytes_accessed=sum(x.size * 2 for x in inputs), transcendentals=0
        ),
        name="closing_exchange",
    )(*inputs, rows)


def closing(hidden, grad_top, normed, grad_before, mixer_normed, own_grads, far_grads, gains, rows, n):
    width = normed.shape[1]
    shard, ff = width // 4, hidden.shape[1]
    inputs = [hidden, grad_top, normed, grad_before, mixer_normed, *own_grads, *far_grads, gains]
    quarter, half = ff // 4, width // 2
    chunks, makers, takers = [], [], []
    small = 256
    for j in range(quarter // small):

        def make_out(need, part, core, j=j):
            a, b = need(0), need(1)
            for o in range(4):
                at = o * quarter + j * small
                part[o] = dot_tn(a[:, at : at + small], b[...]).astype(jnp.bfloat16)

        def take_out(final, outs, j=j):
            outs[1][j * small : (j + 1) * small] = final[...].astype(jnp.float32)

        chunks.append(Chunk(small, width, jnp.bfloat16))
        makers.append(make_out)
        takers.append(take_out)
    for j in range(ff // width):

        def make_in(need, part, core, j=j):
            total = dot_tn(need(2)[...], need(3)[:, j * width : (j + 1) * width])
            part[...] = total.astype(jnp.bfloat16).reshape(part.shape)

        def take_in(final, outs, j=j):
            outs[0][:, j * width : (j + 1) * width] = final[...].astype(jnp.float32)

        chunks.append(Chunk(shard, width, jnp.bfloat16))
        makers.append(make_in)
        takers.append(take_in)
    for j in range(3):

        def make_head(need, part, core, j=j):
            for which, i in ((core, 5 + j), (1 - core, 8 + j)):
                total = dot_tn(need(4)[...], need(i)[...]).astype(jnp.bfloat16)
                part[:, :, pl.ds(pl.multiple_of(which * half, half), half)] = total.reshape(
                    4, shard, half
                )

        def take_head(final, outs, j=j):
            outs[2 + j][...] = final[...].astype(jnp.float32)

        chunks.append(Chunk(shard, width, jnp.bfloat16))
        makers.append(make_head)
        takers.append(take_head)

    def make_gains(need, part, core):
        part[...] = need(11)[...]

    def take_gains(final, outs):
        outs[5][...] = final[...]

    chunks.append(Chunk(gains.shape[1], gains.shape[2], jnp.float32))
    makers.append(make_gains)
    takers.append(take_gains)

    def produce(c, need, part, core):
        makers[c](need, part, core)

    def finish(c, final, outs):
        takers[c](final, outs)

    out_shapes = [(shard, ff), (quarter, width)] + [(shard, width)] * 3 + [gains.shape[1:]]
    flops = 2 * normed.shape[0] * (2 * ff * width + 3 * width * width)
    return closing_exchange(chunks, inputs, produce, finish, out_shapes, rows, n, 3, flops)


def exchange(x, pairs=CORE_PAIRS):
    return lax.ppermute(x, "slots", pairs)


def on_device_fast(
    features, lengths, cotangent, front_gain, front_in, front_out, mixer_gain, query_weight,
    key_weight, value_weight, output_weight, conv_gain, expand_weight, depth_weight, batch_gain,
    batch_bias, project_weight, back_gain, back_in, back_out, final_gain,
):
    slot_count, frames_dev, width = features.shape
    full_length = slot_count * frames_dev
    head_dim = width // HEADS
    half = width // 2
    tm, slots = lax.axis_index("tm"), lax.axis_index("slots")
    core = lax.rem(slots, 2)
    shard = front_gain.shape[0]
    taps_count = depth_weight.shape[1]

    def ordered(group_lengths, backward):
        numbers = jnp.arange(slot_count, dtype=jnp.int32)
        mine, theirs = group_lengths[:, None], group_lengths[None, :]
        ahead = (theirs > mine) | ((theirs == mine) & (numbers[None, :] < numbers[:, None]))
        rank = jnp.sum(ahead.astype(jnp.int32), 1)
        rank = jnp.where(backward, slot_count - 1 - rank, rank)
        order = jnp.sum(jnp.where(rank[:, None] == numbers[None, :], numbers[:, None], 0), 0)
        return rank, order

    rank, order = ordered(lengths, core == 1)
    small = [front_gain, mixer_gain, conv_gain, batch_gain, batch_bias, back_gain, final_gain]
    pack = jnp.concatenate(
        [x.astype(jnp.float32)[None] for x in small]
        + [depth_weight.astype(jnp.float32).T]
        + [jnp.pad(lengths.astype(jnp.float32), (0, shard - slot_count))[None]],
        0,
    )
    pack = jnp.pad(pack, ((0, -pack.shape[0] % 8), (0, 0)))
    pack_rows = pack.shape[0]
    rows_bf16, full_front_in, full_front_out, full_query, full_key, full_value, packs = (
        entry_exchange(
            take_slots(features, order),
            [front_in, front_out, query_weight, key_weight, value_weight, pack],
        )
    )
    cot_rows = lax.all_to_all(take_slots(cotangent, order), "tm", 0, 1, tiled=True)[0]
    gather = functools.partial(lax.all_gather, axis_name="slots", axis=0, tiled=True)
    full_output, full_expand, full_project = (
        gather(output_weight),
        gather(expand_weight),
        gather(project_weight),
    )
    full_back_in, full_back_out = gather(back_in), gather(back_out)

    packs = packs.reshape(-1, pack_rows, shard)
    params = jnp.transpose(packs, (1, 0, 2)).reshape(pack_rows, width)
    (front_norm_gain, mixer_norm_gain, conv_norm_gain, batch_scale, batch_shift, back_norm_gain,
     final_norm_gain) = (params[i] for i in range(7))
    depth_taps = params[7 : 7 + taps_count]
    all_lengths = packs[:, 7 + taps_count, :slot_count].astype(jnp.int32)
    frames_total = jnp.sum(all_lengths).astype(jnp.float32)
    length = jnp.sum(jnp.where(jnp.arange(slot_count) == tm, lengths[order], 0))
    near = lax.dynamic_index_in_dim(all_lengths, slots + 1 - 2 * core, 0, False)
    near_order = ordered(near, core == 0)[1]
    near_length = jnp.sum(jnp.where(jnp.arange(slot_count) == tm, near[near_order], 0))
    length, near_length = length.reshape(1), near_length.reshape(1)
    head_numbers = (jnp.arange(HEADS // 2, dtype=jnp.int32) + core * (HEADS // 2)).astype(jnp.float32)
    slopes = 64.0 * 2.0 ** (-head_numbers) / full_length
    def stack(*rows):
        return jnp.concatenate(
            [r[None] for r in rows] + [jnp.zeros((8 - len(rows), width), jnp.float32)], 0
        )

    bf16, f32 = jnp.bfloat16, jnp.float32
    ff = front_in.shape[1]
    scalars = jnp.concatenate([core.reshape(1), length])
    front_gains = stack(front_norm_gain, mixer_norm_gain)
    front_normed, front_hidden, front_slope, after_front, mixer_normed, own_qkv, far_qkv = row_call(
        front_kernel, "front", scalars, [rows_bf16],
        [front_gains, full_front_in, full_front_out, full_query, full_key, full_value],
        [(width, bf16), (ff, bf16), (ff, bf16), (width, f32), (width, bf16), (3 * half, bf16), (3 * half, bf16)],
        0, 512, 4 * width * ff + 6 * width * width,
    )
    near_qkv = exchange(far_qkv)
    both_lengths = jnp.concatenate([length, near_length])
    own_att, near_att, own_qa, near_qa = attend(own_qkv, near_qkv, both_lengths, slopes)
    far_att = exchange(near_att)
    conv_gains = stack(conv_norm_gain)
    after_mixer, conv_normed, gated, glu_slope = row_call(
        expand_kernel, "expand", scalars, [own_att, far_att, after_front],
        [conv_gains, full_output, full_expand],
        [(width, f32), (width, bf16), (width, bf16), (2 * width, bf16)],
        0, 512, 6 * width * width,
    )
    filtered, stats = filter_frames(gated, depth_taps, length)
    counted = jnp.concatenate(
        [stats[:2], jnp.full((1, width), length.astype(f32)[0]), stats[3:]], 0
    )
    shared = share_stats(counted, merge_spreads, 1)
    middle = shared[0] / frames_total
    spread = shared[1] / frames_total
    inverse_spread = lax.rsqrt(spread + EPSILON)

    params8 = stack(
        middle, inverse_spread, batch_scale, batch_shift, back_norm_gain, final_norm_gain
    )
    (output_rows, grad_rows, dbn, swish, conv_top, back_hidden, back_dpre, back_normed, back_half,
     back_sums) = row_call(
        back_kernel, "back", scalars, [filtered, after_mixer, cot_rows],
        [params8, full_project, full_back_in, full_back_out],
        [(width, bf16), (width, f32), (width, f32), (width, bf16), (width, bf16), (ff, bf16),
         (ff, bf16), (width, bf16), (width, bf16)],
        1, 256, 8 * width * ff + 4 * width * width,
    )
    sums = share_stats(back_sums, add_blocks, 2)
    grad_batch_shift, grad_batch_scale = sums[0], sums[1]
    rows5 = stack(
        middle,
        inverse_spread,
        batch_scale,
        batch_scale * grad_batch_shift / frames_total,
        batch_scale * grad_batch_scale / frames_total,
    )
    weights_back = back_weights(back_hidden, back_half, back_normed, back_dpre, swish, conv_top)

    def send_back(rows):
        parts = lax.all_to_all(
            rows.reshape(slot_count, frames_dev, width), "tm", 0, 0, tiled=True
        )
        return take_slots(parts, rank)

    def scattered(joined):
        return lax.psum_scatter(joined, "slots", scatter_dimension=0, tiled=True)[0]

    output_rows, weights_back, _ = lax.optimization_barrier((output_rows, weights_back, sums))
    weights_back = lax.psum(scattered(weights_back), "tm")
    output = send_back(output_rows)
    dgated, grad_depth = filter_back(filtered, dbn, gated, depth_taps, rows5, length)
    dexpand, grad_rows, mix_top, own_grad, far_grad, conv_sums = row_call(
        glu_back_kernel, "glu_back", scalars, [dgated, glu_slope, grad_rows, after_mixer],
        [conv_gains, full_expand, full_output],
        [(2 * width, bf16), (width, f32), (width, bf16), (half, bf16), (half, bf16)],
        1, 512, 6 * width * width,
    )
    near_grad = exchange(far_grad)
    weights_middle = middle_weights(
        core.reshape(1), conv_normed, dexpand, own_att, far_att, mix_top
    )
    own_dqkv, near_dqkv = attend_back(
        (own_qa, own_qkv, own_grad, own_att),
        (near_qa, near_qkv, near_grad, near_att),
        both_lengths,
        slopes,
    )
    far_dqkv = [exchange(x) for x in near_dqkv]
    weights_middle = scattered(weights_middle)
    weights_middle, _ = lax.optimization_barrier((weights_middle, weights_back))
    weights_middle = lax.psum(weights_middle, "tm")
    front_half, front_dpre, home_rows, front_sums = row_call(
        front_back_kernel, "front_back", scalars,
        [*own_dqkv, *far_dqkv, grad_rows, after_front, rows_bf16, front_slope],
        [front_gains, full_front_in, full_front_out, full_query, full_key, full_value],
        [(width, bf16), (ff, bf16), (width, bf16)],
        1, 256, 4 * width * ff + 6 * width * width,
    )
    gains = jnp.concatenate(
        [front_sums[:2], conv_sums[:1], back_sums[3:4], back_sums[2:3], grad_depth[:taps_count]], 0
    )
    gains = jnp.pad(gains, ((0, -gains.shape[0] % 64), (0, 0)))
    gains = jnp.transpose(gains.reshape(-1, 4, shard), (1, 0, 2))
    part_front_in, part_front_out, part_query, part_key, part_value, gains, parts = closing(
        front_hidden, front_half, front_normed, front_dpre, mixer_normed, own_dqkv, far_dqkv,
        gains, home_rows, slot_count,
    )
    grad_features = take_slots(parts, rank)

    def side_by_side(rows, count):
        rows = rows.astype(f32).reshape(count, shard, width)
        return jnp.transpose(rows, (1, 0, 2)).reshape(shard, count * width)

    quarter = ff // 4
    part_back_out = weights_back[:quarter].astype(f32)
    part_back_in = side_by_side(weights_back[quarter : quarter + 4 * shard], 4)
    part_project = weights_back[quarter + 4 * shard :].astype(f32)
    part_expand = side_by_side(weights_middle[: 2 * shard], 2)
    part_output = weights_middle[2 * shard :].astype(f32)

    def own_part(row):
        return lax.dynamic_slice_in_dim(row, slots * shard, shard, 0)

    part_depth = gains[5 : 5 + taps_count].T
    return (
        output,
        grad_features,
        gains[0],
        part_front_in,
        part_front_out,
        gains[1],
        part_query,
        part_key,
        part_value,
        part_output,
        gains[2],
        part_expand,
        part_depth,
        own_part(grad_batch_scale),
        own_part(grad_batch_shift),
        part_project,
        gains[3],
        part_back_in,
        part_back_out,
        gains[4],
    )


def on_device(features, *rest):
    whole = features.shape[0] == lax.axis_size("tm") and lax.axis_size("slots") == 4
    return (on_device_fast if whole else on_device_general)(features, *rest)


def on_device_general(
    features,
    lengths,
    cotangent,
    front_gain,
    front_in,
    front_out,
    mixer_gain,
    query_weight,
    key_weight,
    value_weight,
    output_weight,
    conv_gain,
    expand_weight,
    depth_weight,
    batch_gain,
    batch_bias,
    project_weight,
    back_gain,
    back_in,
    back_out,
    final_gain,
):
    gathered = (
        lax.all_gather(front_gain, "slots", axis=0, tiled=True),
        lax.all_gather(front_in, "slots", axis=0, tiled=True),
        lax.all_gather(front_out, "slots", axis=0, tiled=True),
        lax.all_gather(mixer_gain, "slots", axis=0, tiled=True),
        lax.all_gather(query_weight, "slots", axis=0, tiled=True),
        lax.all_gather(key_weight, "slots", axis=0, tiled=True),
        lax.all_gather(value_weight, "slots", axis=0, tiled=True),
        lax.all_gather(output_weight, "slots", axis=0, tiled=True),
        lax.all_gather(conv_gain, "slots", axis=0, tiled=True),
        lax.all_gather(expand_weight, "slots", axis=0, tiled=True),
        lax.all_gather(depth_weight, "slots", axis=0, tiled=True),
        lax.all_gather(batch_gain, "slots", axis=0, tiled=True),
        lax.all_gather(batch_bias, "slots", axis=0, tiled=True),
        lax.all_gather(project_weight, "slots", axis=0, tiled=True),
        lax.all_gather(back_gain, "slots", axis=0, tiled=True),
        lax.all_gather(back_in, "slots", axis=0, tiled=True),
        lax.all_gather(back_out, "slots", axis=0, tiled=True),
        lax.all_gather(final_gain, "slots", axis=0, tiled=True),
    )
    (
        full_front_gain,
        full_front_in,
        full_front_out,
        full_mixer_gain,
        full_query,
        full_key,
        full_value,
        full_output,
        full_conv_gain,
        full_expand,
        full_depth,
        full_batch_gain,
        full_batch_bias,
        full_project,
        full_back_gain,
        full_back_in,
        full_back_out,
        full_final_gain,
    ) = gathered
    front_norm_gain = full_front_gain.astype(jnp.float32)
    mixer_norm_gain = full_mixer_gain.astype(jnp.float32)
    conv_norm_gain = full_conv_gain.astype(jnp.float32)
    batch_scale = full_batch_gain.astype(jnp.float32)
    batch_shift = full_batch_bias.astype(jnp.float32)
    back_norm_gain = full_back_gain.astype(jnp.float32)
    final_norm_gain = full_final_gain.astype(jnp.float32)
    depth_taps = full_depth.astype(jnp.float32)
    slot_count, frames_dev, width = features.shape
    row_count = slot_count * frames_dev
    full_length = frames_dev * lax.axis_size("tm")
    head_dim = width // HEADS
    taps_count = full_depth.shape[1]
    half_width = taps_count // 2
    score_scale = 1.0 / math.sqrt(head_dim)
    head_numbers = jnp.arange(HEADS, dtype=jnp.int32)
    frame_index = lax.axis_index("tm") * frames_dev + jnp.arange(frames_dev, dtype=jnp.int32)
    frame_mask = (frame_index[None, :] < lengths[:, None]).astype(jnp.float32).reshape(row_count, 1)
    residual_rows = features.astype(jnp.float32).reshape(row_count, width)
    after_front, front_kept = feed_forward(
        residual_rows, front_norm_gain, full_front_in, full_front_out
    )
    mixer_normed = layer_norm(after_front, mixer_norm_gain).astype(jnp.bfloat16)
    query_rows = (
        matmul(mixer_normed, full_query).astype(jnp.bfloat16).reshape(slot_count, frames_dev, width)
    )
    key_rows = (
        matmul(mixer_normed, full_key).astype(jnp.bfloat16).reshape(slot_count, frames_dev, width)
    )
    value_rows = (
        matmul(mixer_normed, full_value).astype(jnp.bfloat16).reshape(slot_count, frames_dev, width)
    )

    def head_scores(head_index, key_part):
        span_keys = key_part.shape[1]
        query_head = lax.dynamic_slice_in_dim(query_rows, head_index * head_dim, head_dim, 2)
        key_head = lax.dynamic_slice_in_dim(key_part, head_index * head_dim, head_dim, 2)
        products = jnp.einsum(
            "ucd,und->ucn", query_head, key_head, preferred_element_type=jnp.float32
        )
        key_index = jnp.arange(span_keys, dtype=jnp.int32)
        slope_head = 64.0 * 2.0 ** (-head_index.astype(jnp.float32)) / full_length
        distance = jnp.abs(frame_index[:, None] - key_index[None, :]).astype(jnp.float32)
        scores = products * score_scale - slope_head * distance
        usable = key_index[None, None, :] < lengths[:, None, None]
        return (scores, usable, query_head, key_head)

    start_state = (
        jnp.full((HEADS, slot_count, frames_dev), -1e30, jnp.float32),
        jnp.zeros((HEADS, slot_count, frames_dev), jnp.float32),
        jnp.zeros((HEADS, slot_count, frames_dev, head_dim), jnp.float32),
    )
    key_part = lax.all_gather(key_rows, "tm", axis=1, tiled=True)
    value_part = lax.all_gather(value_rows, "tm", axis=1, tiled=True)

    def absorb_per_head(inputs):
        head_index, run_max, run_sum, accumulator = inputs
        scores, usable, query_head, key_head = head_scores(head_index, key_part)
        value_head = lax.dynamic_slice_in_dim(value_part, head_index * head_dim, head_dim, 2)
        new_max = jnp.maximum(run_max, jnp.max(jnp.where(usable, scores, -1e30), -1))
        weights_now = jnp.where(usable, jnp.exp(scores - new_max[..., None]), 0.0)
        factor = jnp.exp(run_max - new_max)
        new_sum = run_sum * factor + jnp.sum(weights_now, -1)
        new_accum = accumulator * factor[..., None] + jnp.einsum(
            "ucn,und->ucd",
            weights_now.astype(jnp.bfloat16),
            value_head,
            preferred_element_type=jnp.float32,
        )
        return (new_max, new_sum, new_accum)

    run_max, run_sum, accumulator = lax.map(absorb_per_head, (head_numbers,) + tuple(start_state))
    attended = accumulator / run_sum[..., None]
    log_total = run_max + jnp.log(run_sum)
    mixture = jnp.transpose(attended, (1, 2, 0, 3)).reshape(row_count, width).astype(jnp.bfloat16)
    after_mixer = after_front + matmul(mixture, full_output)
    conv_normed = layer_norm(after_mixer, conv_norm_gain).astype(jnp.bfloat16)
    expand = matmul(conv_normed, full_expand)
    linear_half = expand[:, :width]
    sigmoid_gate = jax.nn.sigmoid(expand[:, width:])
    gated = (
        (linear_half * sigmoid_gate * frame_mask)
        .astype(jnp.bfloat16)
        .reshape(slot_count, frames_dev, width)
    )
    padded = with_halo(gated, (("tm", 1),), half_width)
    filtered = padded[:, 0:frames_dev, :] * depth_taps[:, 0]
    for kernel_tap in range(1, taps_count):
        filtered = (
            filtered
            + padded[:, kernel_tap : kernel_tap + frames_dev, :] * depth_taps[:, kernel_tap]
        )
    filtered = filtered.reshape(row_count, width)
    mask_total, frames_total = lax.psum(
        (jnp.sum(filtered * frame_mask, 0), jnp.sum(frame_mask)), ("tm", "slots")
    )
    middle = mask_total / frames_total
    offset = filtered - middle
    spread = lax.psum(jnp.sum(frame_mask * offset * offset, 0), ("tm", "slots")) / frames_total
    inverse_spread = lax.rsqrt(spread + EPSILON)
    unit_conv = offset * inverse_spread
    batch_normed = unit_conv * batch_scale + batch_shift
    swish = jax.nn.silu(batch_normed).astype(jnp.bfloat16)
    after_conv = after_mixer + matmul(swish, full_project)
    after_back, back_kept = feed_forward(after_conv, back_norm_gain, full_back_in, full_back_out)
    output = (
        layer_norm(after_back, final_norm_gain)
        .astype(jnp.bfloat16)
        .reshape(slot_count, frames_dev, width)
    )
    incoming = cotangent.astype(jnp.float32).reshape(row_count, width)
    grad_rows, grad_final = norm_back(after_back, final_norm_gain, incoming)
    grad_rows, grad_back_gain, grad_back_in, grad_back_out = feed_back(
        after_conv, back_norm_gain, full_back_in, full_back_out, back_kept, grad_rows
    )
    grad_conv_top = grad_rows.astype(jnp.bfloat16)
    grad_project = matmul_tn(swish, grad_conv_top)
    grad_batch_normed = matmul_nt(grad_conv_top, full_project) * silu_slope(batch_normed)
    grad_batch_scale = jnp.sum(grad_batch_normed * unit_conv, 0)
    grad_batch_shift = jnp.sum(grad_batch_normed, 0)
    grad_unit = grad_batch_normed * batch_scale
    sum_plain, sum_scaled = lax.psum(
        (jnp.sum(grad_unit, 0), jnp.sum(grad_unit * unit_conv, 0)), ("tm", "slots")
    )
    grad_filtered = inverse_spread * (
        grad_unit - frame_mask * (sum_plain + unit_conv * sum_scaled) / frames_total
    )
    grad_grid = grad_filtered.reshape(slot_count, frames_dev, width)
    grad_padded = with_halo(grad_grid.astype(jnp.bfloat16), (("tm", 1),), half_width).astype(
        grad_grid.dtype
    )
    grad_gated = jnp.zeros((slot_count, frames_dev, width), jnp.float32)
    taps_grad = []
    for kernel_tap in range(taps_count):
        lead = 2 * half_width - kernel_tap
        grad_gated = (
            grad_gated + depth_taps[:, kernel_tap] * grad_padded[:, lead : lead + frames_dev, :]
        )
        taps_grad.append(
            jnp.sum(grad_grid * padded[:, kernel_tap : kernel_tap + frames_dev, :], axis=(0, 1))
        )
    grad_depth = jnp.stack(taps_grad, axis=1)
    grad_gated_low = lax.optimization_barrier(
        grad_gated.reshape(row_count, width).astype(jnp.bfloat16)
    ).astype(jnp.float32)
    grad_masked = grad_gated_low * frame_mask
    grad_linear = grad_masked * sigmoid_gate
    grad_gate = grad_masked * linear_half * sigmoid_gate * (1.0 - sigmoid_gate)
    grad_expand = jnp.concatenate([grad_linear, grad_gate], 1).astype(jnp.bfloat16)
    grad_expand_weight = matmul_tn(conv_normed, grad_expand)
    grad_conv_normed = matmul_nt(grad_expand, full_expand)
    delta_rows, grad_conv_gain = norm_back(after_mixer, conv_norm_gain, grad_conv_normed)
    grad_rows = grad_rows + delta_rows
    grad_mix_top = grad_rows.astype(jnp.bfloat16)
    grad_output_weight = matmul_tn(mixture, grad_mix_top)
    grad_mixture = matmul_nt(grad_mix_top, full_output).astype(jnp.bfloat16)
    grad_heads = jnp.transpose(
        grad_mixture.reshape(slot_count, frames_dev, HEADS, head_dim), (2, 0, 1, 3)
    )
    delta_heads = jnp.sum(grad_heads.astype(jnp.float32) * attended, -1)
    start_grads = (
        jnp.zeros((HEADS, slot_count, frames_dev, head_dim), jnp.float32),
        jnp.zeros((HEADS, slot_count, full_length, head_dim), jnp.float32),
        jnp.zeros((HEADS, slot_count, full_length, head_dim), jnp.float32),
    )
    collect_key_part = lax.all_gather(key_rows, "tm", axis=1, tiled=True)
    collect_value_part = lax.all_gather(value_rows, "tm", axis=1, tiled=True)
    span_keys = collect_key_part.shape[1]

    def collect_per_head(inputs):
        head_index, grad_query, key_sums, value_sums, total_log, delta_head, grad_head = inputs
        scores, usable, query_head, key_head = head_scores(head_index, collect_key_part)
        value_head = lax.dynamic_slice_in_dim(
            collect_value_part, head_index * head_dim, head_dim, 2
        )
        probs = jnp.where(usable, jnp.exp(scores - total_log[..., None]), 0.0)
        grad_probs = jnp.einsum(
            "ucd,und->ucn", grad_head, value_head, preferred_element_type=jnp.float32
        )
        grad_raw = (probs * (grad_probs - delta_head[..., None]) * score_scale).astype(jnp.bfloat16)
        grad_query = grad_query + jnp.einsum(
            "ucn,und->ucd", grad_raw, key_head, preferred_element_type=jnp.float32
        )
        key_term = jnp.einsum(
            "ucn,ucd->und", grad_raw, query_head, preferred_element_type=jnp.float32
        )
        value_term = jnp.einsum(
            "ucn,ucd->und",
            probs.astype(jnp.bfloat16),
            grad_head,
            preferred_element_type=jnp.float32,
        )
        key_sums = key_sums + key_term
        value_sums = value_sums + value_term
        return (grad_query, key_sums, value_sums)

    folded = lax.map(
        collect_per_head,
        (head_numbers,) + tuple(start_grads) + (log_total, delta_heads, grad_heads),
    )
    grad_query_heads, key_sums, value_sums = folded
    grad_key_heads, grad_value_heads = (
        lax.psum_scatter(
            key_sums.astype(jnp.bfloat16), "tm", scatter_dimension=2, tiled=True
        ).astype(jnp.float32),
        lax.psum_scatter(
            value_sums.astype(jnp.bfloat16), "tm", scatter_dimension=2, tiled=True
        ).astype(jnp.float32),
    )

    def to_rows(heads_array):
        return (
            jnp.transpose(heads_array, (1, 2, 0, 3)).reshape(row_count, width).astype(jnp.bfloat16)
        )

    grad_query_rows = to_rows(grad_query_heads)
    grad_key_rows = to_rows(grad_key_heads)
    grad_value_rows = to_rows(grad_value_heads)
    grad_query_weight = matmul_tn(mixer_normed, grad_query_rows)
    grad_key_weight = matmul_tn(mixer_normed, grad_key_rows)
    grad_value_weight = matmul_tn(mixer_normed, grad_value_rows)
    grad_mixer_normed = (
        matmul_nt(grad_query_rows, full_query)
        + matmul_nt(grad_key_rows, full_key)
        + matmul_nt(grad_value_rows, full_value)
    )
    delta_rows, grad_mixer_gain = norm_back(after_front, mixer_norm_gain, grad_mixer_normed)
    grad_rows = grad_rows + delta_rows
    grad_rows, grad_front_gain, grad_front_in, grad_front_out = feed_back(
        residual_rows, front_norm_gain, full_front_in, full_front_out, front_kept, grad_rows
    )
    grad_features = grad_rows.astype(jnp.bfloat16).reshape(slot_count, frames_dev, width)
    partial_rows = (
        lax.psum_scatter(
            grad_front_gain.astype(jnp.bfloat16), "slots", scatter_dimension=0, tiled=True
        ).astype(jnp.float32),
        lax.psum_scatter(
            grad_front_in.astype(jnp.bfloat16), "slots", scatter_dimension=0, tiled=True
        ).astype(jnp.float32),
        lax.psum_scatter(
            grad_front_out.astype(jnp.bfloat16), "slots", scatter_dimension=0, tiled=True
        ).astype(jnp.float32),
        lax.psum_scatter(
            grad_mixer_gain.astype(jnp.bfloat16), "slots", scatter_dimension=0, tiled=True
        ).astype(jnp.float32),
        lax.psum_scatter(
            grad_query_weight.astype(jnp.bfloat16), "slots", scatter_dimension=0, tiled=True
        ).astype(jnp.float32),
        lax.psum_scatter(
            grad_key_weight.astype(jnp.bfloat16), "slots", scatter_dimension=0, tiled=True
        ).astype(jnp.float32),
        lax.psum_scatter(
            grad_value_weight.astype(jnp.bfloat16), "slots", scatter_dimension=0, tiled=True
        ).astype(jnp.float32),
        lax.psum_scatter(
            grad_output_weight.astype(jnp.bfloat16), "slots", scatter_dimension=0, tiled=True
        ).astype(jnp.float32),
        lax.psum_scatter(
            grad_conv_gain.astype(jnp.bfloat16), "slots", scatter_dimension=0, tiled=True
        ).astype(jnp.float32),
        lax.psum_scatter(
            grad_expand_weight.astype(jnp.bfloat16), "slots", scatter_dimension=0, tiled=True
        ).astype(jnp.float32),
        lax.psum_scatter(
            grad_depth.astype(jnp.bfloat16), "slots", scatter_dimension=0, tiled=True
        ).astype(jnp.float32),
        lax.psum_scatter(
            grad_batch_scale.astype(jnp.bfloat16), "slots", scatter_dimension=0, tiled=True
        ).astype(jnp.float32),
        lax.psum_scatter(
            grad_batch_shift.astype(jnp.bfloat16), "slots", scatter_dimension=0, tiled=True
        ).astype(jnp.float32),
        lax.psum_scatter(
            grad_project.astype(jnp.bfloat16), "slots", scatter_dimension=0, tiled=True
        ).astype(jnp.float32),
        lax.psum_scatter(
            grad_back_gain.astype(jnp.bfloat16), "slots", scatter_dimension=0, tiled=True
        ).astype(jnp.float32),
        lax.psum_scatter(
            grad_back_in.astype(jnp.bfloat16), "slots", scatter_dimension=0, tiled=True
        ).astype(jnp.float32),
        lax.psum_scatter(
            grad_back_out.astype(jnp.bfloat16), "slots", scatter_dimension=0, tiled=True
        ).astype(jnp.float32),
        lax.psum_scatter(
            grad_final.astype(jnp.bfloat16), "slots", scatter_dimension=0, tiled=True
        ).astype(jnp.float32),
    )
    (
        part_front_gain,
        part_front_in,
        part_front_out,
        part_mixer_gain,
        part_query,
        part_key,
        part_value,
        part_output,
        part_conv_gain,
        part_expand,
        part_depth,
        part_batch_gain,
        part_batch_bias,
        part_project,
        part_back_gain,
        part_back_in,
        part_back_out,
        part_final_gain,
    ) = partial_rows
    shards = (
        lax.psum(part_front_gain.astype(jnp.bfloat16), "tm").astype(jnp.float32),
        lax.psum(part_front_in.astype(jnp.bfloat16), "tm").astype(jnp.float32),
        lax.psum(part_front_out.astype(jnp.bfloat16), "tm").astype(jnp.float32),
        lax.psum(part_mixer_gain.astype(jnp.bfloat16), "tm").astype(jnp.float32),
        lax.psum(part_query.astype(jnp.bfloat16), "tm").astype(jnp.float32),
        lax.psum(part_key.astype(jnp.bfloat16), "tm").astype(jnp.float32),
        lax.psum(part_value.astype(jnp.bfloat16), "tm").astype(jnp.float32),
        lax.psum(part_output.astype(jnp.bfloat16), "tm").astype(jnp.float32),
        lax.psum(part_conv_gain.astype(jnp.bfloat16), "tm").astype(jnp.float32),
        lax.psum(part_expand.astype(jnp.bfloat16), "tm").astype(jnp.float32),
        lax.psum(part_depth.astype(jnp.bfloat16), "tm").astype(jnp.float32),
        lax.psum(part_batch_gain.astype(jnp.bfloat16), "tm").astype(jnp.float32),
        lax.psum(part_batch_bias.astype(jnp.bfloat16), "tm").astype(jnp.float32),
        lax.psum(part_project.astype(jnp.bfloat16), "tm").astype(jnp.float32),
        lax.psum(part_back_gain.astype(jnp.bfloat16), "tm").astype(jnp.float32),
        lax.psum(part_back_in.astype(jnp.bfloat16), "tm").astype(jnp.float32),
        lax.psum(part_back_out.astype(jnp.bfloat16), "tm").astype(jnp.float32),
        lax.psum(part_final_gain.astype(jnp.bfloat16), "tm").astype(jnp.float32),
    )
    return (output, grad_features) + tuple(shards)


def solution(mesh):
    in_specs = (
        P("slots", "tm", None),
        P("slots"),
        P("slots", "tm", None),
        P("slots"),
        P("slots", None),
        P("slots", None),
        P("slots"),
        P("slots", None),
        P("slots", None),
        P("slots", None),
        P("slots", None),
        P("slots"),
        P("slots", None),
        P("slots", None),
        P("slots"),
        P("slots"),
        P("slots", None),
        P("slots"),
        P("slots", None),
        P("slots", None),
        P("slots"),
    )
    out_specs = (
        P("slots", "tm", None),
        P("slots", "tm", None),
        P("slots"),
        P("slots", None),
        P("slots", None),
        P("slots"),
        P("slots", None),
        P("slots", None),
        P("slots", None),
        P("slots", None),
        P("slots"),
        P("slots", None),
        P("slots", None),
        P("slots"),
        P("slots"),
        P("slots", None),
        P("slots"),
        P("slots", None),
        P("slots", None),
        P("slots"),
    )
    return jax.shard_map(
        on_device, mesh=mesh, in_specs=in_specs, out_specs=out_specs, check_vma=False
    )
```

```python
import functools
import math

import jax
import jax.numpy as jnp
from jax import lax
from jax.experimental import pallas as pl
from jax.experimental.pallas import tpu as pltpu
from jax.sharding import PartitionSpec as P

HEADS = 8


EPSILON = 1e-05
MESH = pl.DeviceIdType.MESH
KEY_BLOCK = 256
QUERY_BLOCK = 256
MASKED = -1e30
HALO = 16
CORE_PAIRS = [(0, 1), (1, 0), (2, 3), (3, 2)]


def remote(src, dst, send_sem, recv_sem, where):
    return pltpu.make_async_remote_copy(
        src_ref=src,
        dst_ref=dst,
        send_sem=send_sem,
        recv_sem=recv_sem,
        device_id=where,
        device_id_type=MESH,
    )


def entry_kernel(count, *refs):
    feat, shards = refs[0], refs[1 : 1 + count]
    feat_out, fulls = refs[1 + count], refs[2 + count : 2 + 2 * count]
    (a_send, a_recv, y_send, y_recv, c_send, c_recv, f_send, f_recv, local) = refs[2 + 2 * count :]
    me, n = lax.axis_index("tm"), lax.axis_size("tm")
    s = lax.axis_index("slots")
    sibling = s + 1 - 2 * lax.rem(s, 2)
    across = lax.rem(s + 2, 4)
    frames = feat.shape[1]

    barrier = pltpu.get_barrier_semaphore()
    for k in range(1, n):
        pl.semaphore_signal(
            barrier, inc=1, device_id={"tm": lax.rem(me + k, n)}, device_id_type=MESH
        )
    pl.semaphore_signal(barrier, inc=1, device_id={"slots": sibling}, device_id_type=MESH)
    pl.semaphore_signal(barrier, inc=1, device_id={"slots": across}, device_id_type=MESH)
    pl.semaphore_wait(barrier, n + 1)

    def block(ref, shard, owner):
        rows = shard.shape[0]
        return ref.at[pl.ds(owner * rows, rows)]

    y_copies, c_copies, locals_ = [], [], []
    for i in range(count):
        mine = block(fulls[i], shards[i], s)
        y_copies.append(remote(shards[i], mine, y_send.at[i], y_recv.at[i], {"slots": across}))
        y_copies[-1].start()
    a_copies = []
    for k in sorted(range(1, n), key=lambda k: abs(k - n / 2)):
        to = lax.rem(me + k, n)
        a_copies.append(
            remote(
                feat.at[to],
                feat_out.at[pl.ds(me * frames, frames)],
                a_send.at[k],
                a_recv.at[k],
                {"tm": to},
            )
        )
        a_copies[-1].start()
    for i in range(count):
        mine = block(fulls[i], shards[i], s)
        c_copies.append(remote(shards[i], mine, c_send.at[i], c_recv.at[i], {"slots": sibling}))
        c_copies[-1].start()
        locals_.append(pltpu.make_async_copy(shards[i], mine, local.at[i]))
        locals_[-1].start()
    locals_.append(
        pltpu.make_async_copy(
            feat.at[me], feat_out.at[pl.ds(me * frames, frames)], local.at[count]
        )
    )
    locals_[-1].start()
    f_copies = []
    for i in range(count):
        y_copies[i].wait_recv()
        theirs = block(fulls[i], shards[i], across)
        f_copies.append(remote(theirs, theirs, f_send.at[i], f_recv.at[i], {"slots": sibling}))
        f_copies[-1].start()
    for copy in y_copies:
        copy.wait_send()
    for copy in c_copies + f_copies + a_copies + locals_:
        copy.wait()


def entry_exchange(feat, shards):
    n, frames, width = feat.shape
    count = len(shards)
    dma = pltpu.SemaphoreType.DMA
    return pl.pallas_call(
        functools.partial(entry_kernel, count),
        out_shape=[jax.ShapeDtypeStruct((n * frames, width), feat.dtype)]
        + [jax.ShapeDtypeStruct((4 * w.shape[0],) + w.shape[1:], w.dtype) for w in shards],
        in_specs=[pl.BlockSpec(memory_space=pltpu.VMEM)] * (1 + count),
        out_specs=[pl.BlockSpec(memory_space=pl.ANY)] * (1 + count),
        scratch_shapes=[dma((n,)), dma((n,))] + [dma((count,))] * 6 + [dma((count + 1,))],
        compiler_params=pltpu.CompilerParams(collective_id=0, has_side_effects=True),
        name="entry_exchange",
    )(feat, *shards)


def stats_kernel(combine, x_ref, o_ref, near, far, mid, send, recv):
    t, s = lax.axis_index("tm"), lax.axis_index("slots")
    n, m = lax.axis_size("tm"), lax.axis_size("slots")
    barrier = pltpu.get_barrier_semaphore()
    slot_places = [{"slots": lax.rem(s + k, m)} for k in range(1, m)]
    tm_places = [{"tm": lax.rem(t + k, n)} for k in range(1, n)]
    for place in slot_places + tm_places:
        pl.semaphore_signal(barrier, inc=1, device_id=place, device_id_type=MESH)
    pl.semaphore_wait(barrier, n + m - 2)

    def share(source, landing, places, first):
        copies = []
        for i, place in enumerate(places):
            copies.append(
                remote(source, landing.at[i], send.at[first + i], recv.at[first + i], place)
            )
            copies[-1].start()
        for copy in copies:
            copy.wait()
        return combine([source[...]] + [landing[i] for i in range(len(places))])

    mid[...] = share(x_ref, near, slot_places, 0)
    o_ref[...] = share(mid, far, tm_places, m - 1)


def add_blocks(blocks):
    total = blocks[0]
    for block in blocks[1:]:
        total = total + block
    return total


def merge_spreads(blocks):
    sums = add_blocks([b[0:1] for b in blocks])
    counts = add_blocks([b[2:3] for b in blocks])
    mean = sums / counts
    squares = add_blocks(
        [b[1:2] + b[2:3] * (b[0:1] / b[2:3] - mean) * (b[0:1] / b[2:3] - mean) for b in blocks]
    )
    return jnp.concatenate((sums, squares, counts, jnp.zeros((5,) + sums.shape[1:], sums.dtype)), 0)


def share_stats(block, combine, collective_id):
    n, m = lax.axis_size("tm"), lax.axis_size("slots")
    return pl.pallas_call(
        functools.partial(stats_kernel, combine),
        out_shape=jax.ShapeDtypeStruct(block.shape, block.dtype),
        in_specs=[pl.BlockSpec(memory_space=pltpu.VMEM)],
        out_specs=pl.BlockSpec(memory_space=pltpu.VMEM),
        scratch_shapes=[
            pltpu.VMEM((m - 1,) + block.shape, block.dtype),
            pltpu.VMEM((n - 1,) + block.shape, block.dtype),
            pltpu.VMEM(block.shape, block.dtype),
            pltpu.SemaphoreType.DMA((n + m - 2,)),
            pltpu.SemaphoreType.DMA((n + m - 2,)),
        ],
        compiler_params=pltpu.CompilerParams(collective_id=collective_id, has_side_effects=True),
        name="share_stats",
    )(block)


def permute_kernel(places, x_ref, o_ref, held, load, store):
    n = x_ref.shape[0]
    loads = [pltpu.make_async_copy(x_ref.at[places[i]], held.at[i], load.at[i]) for i in range(n)]
    stores = [pltpu.make_async_copy(held.at[i], o_ref.at[i], store.at[i]) for i in range(n)]
    for copy in loads:
        copy.start()
    for i in range(n):
        loads[i].wait()
        stores[i].start()
    for copy in stores:
        copy.wait()


def take_slots(x, places):
    n = x.shape[0]
    return pl.pallas_call(
        permute_kernel,
        out_shape=jax.ShapeDtypeStruct(x.shape, x.dtype),
        grid_spec=pltpu.PrefetchScalarGridSpec(
            num_scalar_prefetch=1,
            grid=(1,),
            in_specs=[pl.BlockSpec(memory_space=pl.ANY)],
            out_specs=pl.BlockSpec(memory_space=pl.ANY),
            scratch_shapes=[
                pltpu.VMEM(x.shape, x.dtype),
                pltpu.SemaphoreType.DMA((n,)),
                pltpu.SemaphoreType.DMA((n,)),
            ],
        ),
        cost_estimate=pl.CostEstimate(flops=0, bytes_accessed=2 * x.size * 2, transcendentals=0),
        name="take_slots",
    )(places, x)


def split_parts(x):
    high = x.astype(jnp.bfloat16).astype(jnp.float32)
    rest = x - high
    middle = rest.astype(jnp.bfloat16).astype(jnp.float32)
    return high, middle, rest - middle


def dot_nn(a, b):
    return jnp.dot(a, b, preferred_element_type=jnp.float32)


def dot_nt(a, b):
    return lax.dot_general(a, b, (((1,), (1,)), ((), ())), preferred_element_type=jnp.float32)


def fill_bias(table, slope, blocks, span):
    rows = lax.broadcasted_iota(jnp.int32, (KEY_BLOCK, KEY_BLOCK), 0)
    lanes = lax.broadcasted_iota(jnp.int32, (KEY_BLOCK, KEY_BLOCK), 1)
    relative = (rows - lanes + (span - KEY_BLOCK)).astype(jnp.float32)

    def fill(c, carry):
        at = pl.multiple_of(c * KEY_BLOCK, KEY_BLOCK)
        table[:, pl.ds(at, KEY_BLOCK)] = slope * jnp.abs(relative - at.astype(jnp.float32))
        return carry

    lax.fori_loop(span // KEY_BLOCK - blocks, 2 * span // KEY_BLOCK - 1, fill, 0)


def lane_rows(span):
    lane = lax.broadcasted_iota(jnp.int32, (1, 128), 1)
    first = (lane < 64).astype(jnp.float32)
    return (first, 1.0 - first), lax.rem(lane, 64)


def one_hot(place, low, high):
    return ((place >= low) & (place < high)).astype(jnp.float32)


def key_tile(k, sel, place, length):
    row = lax.broadcasted_iota(jnp.int32, (k.shape[0], 1), 0)
    masked = jnp.where(row < length, 0.0, MASKED)
    extra = (1.0 - sel) * (one_hot(place, 1, 4) + masked * one_hot(place, 0, 1))
    return k * sel.astype(jnp.bfloat16) + extra.astype(jnp.bfloat16)


def block_count(length):
    return (length + KEY_BLOCK - 1) // KEY_BLOCK


def attend_kernel(
    lengths, slopes, *refs
):
    qkv, (own_att, near_att, own_qa, near_qa) = (refs[0:3], refs[3:6]), refs[6:10]
    table, qa, ka, vt, acc, top = refs[10:]
    span = own_att.shape[0]
    pair = pl.program_id(0)
    sels, place = lane_rows(span)
    counts = [block_count(lengths[u]) for u in range(2)]
    most = jnp.maximum(counts[0], counts[1])
    for h in range(2):
        fill_bias(table.at[h], slopes[2 * pair + h], most, span)
    ones = jnp.ones((16, span), jnp.bfloat16)
    for u in range(2):
        q, k, v = (r[...] for r in qkv[u])
        v_turned = jnp.transpose(v)
        for h in range(2):
            query_extra = (1.0 - sels[h]) * one_hot(place, 0, 1)
            qa[u, h] = q * (sels[h] * 0.125).astype(jnp.bfloat16) + query_extra.astype(jnp.bfloat16)
            ka[u, h] = key_tile(k, sels[h], place, lengths[u])
            vt[u, h, 0:64] = v_turned[64 * h : 64 * h + 64]
            vt[u, h, 64:80] = ones
    acc[...] = jnp.zeros_like(acc)
    top[...] = jnp.full_like(top, -3e38)

    def step(i, carry):
        u = (i >= counts[0]).astype(jnp.int32)
        at = pl.multiple_of((i - u * counts[0]) * KEY_BLOCK, KEY_BLOCK)
        x0 = pl.multiple_of((span - KEY_BLOCK) - at, KEY_BLOCK)
        for h in range(2):
            s = dot_nt(ka[u, h, pl.ds(at, KEY_BLOCK), :], qa[u, h]) - table[h, :, pl.ds(x0, span)]
            old = top[u, h, 0:1]
            new = jnp.maximum(old, jnp.max(s, axis=0, keepdims=True))
            p = jnp.exp(s - new).astype(jnp.bfloat16)
            top[u, h, 0:1] = new
            acc[u, h] = acc[u, h] * jnp.exp(old - new) + dot_nn(
                vt[u, h, :, pl.ds(at, KEY_BLOCK)], p
            )
        return carry

    lax.fori_loop(0, counts[0] + counts[1], step, 0)
    for u, att, qa_out in ((0, own_att, own_qa), (1, near_att, near_qa)):
        attended, extras = [], []
        for h in range(2):
            total = acc[u, h, 64:65, :]
            attended.append((acc[u, h, 0:64, :] / total).astype(jnp.bfloat16))
            parts = split_parts(-(top[u, h, 0:1, :] + jnp.log(total)))
            extras.append(
                jnp.concatenate(
                    (jnp.zeros_like(total),) + parts + (jnp.zeros((60, span), jnp.float32),), 0
                ).astype(jnp.bfloat16)
            )
        att[...] = jnp.transpose(jnp.concatenate(attended, 0))
        query_extra = jnp.transpose(jnp.concatenate((extras[1], extras[0]), 0))
        for h in range(2):
            qa_out[h] = qa[u, h] + query_extra * (1.0 - sels[h]).astype(jnp.bfloat16)


def pair_columns(span, pairs, which):
    return pl.BlockSpec((span, 128), lambda p, *_: (0, which * pairs + p))


def attend(own_qkv, near_qkv, lengths, slopes):
    span, columns = own_qkv.shape
    pairs = columns // 384
    cells = span * span * pairs * 2
    table_width = 2 * span - KEY_BLOCK
    columns3 = [pair_columns(span, pairs, i) for i in range(3)]
    tall = pl.BlockSpec((span, 128), lambda p, *_: (0, p))
    heads = pl.BlockSpec((2, span, 128), lambda p, *_: (p, 0, 0))
    return pl.pallas_call(
        attend_kernel,
        out_shape=[jax.ShapeDtypeStruct((span, pairs * 128), jnp.bfloat16)] * 2
        + [jax.ShapeDtypeStruct((2 * pairs, span, 128), jnp.bfloat16)] * 2,
        grid_spec=pltpu.PrefetchScalarGridSpec(
            num_scalar_prefetch=2,
            grid=(pairs,),
            in_specs=columns3 * 2,
            out_specs=[tall, tall, heads, heads],
            scratch_shapes=[
                pltpu.VMEM((2, KEY_BLOCK, table_width), jnp.float32),
                pltpu.VMEM((2, 2, span, 128), jnp.bfloat16),
                pltpu.VMEM((2, 2, span, 128), jnp.bfloat16),
                pltpu.VMEM((2, 2, 80, span), jnp.bfloat16),
                pltpu.VMEM((2, 2, 80, span), jnp.float32),
                pltpu.VMEM((2, 2, 8, span), jnp.float32),
            ],
        ),
        compiler_params=pltpu.CompilerParams(vmem_limit_bytes=56 << 20),
        cost_estimate=pl.CostEstimate(
            flops=cells * 4 * 256, bytes_accessed=span * columns * 8, transcendentals=cells
        ),
        name="attend",
    )(lengths, slopes, *([own_qkv] * 3), *([near_qkv] * 3))


def attend_back_kernel(lengths, slopes, *refs):
    inputs, outputs = (refs[0:5], refs[5:10]), (refs[10:13], refs[13:16])
    table, qa, ka, va, ga, kt, dqt, dk_out, dv_out = refs[16:]
    span = refs[1].shape[0]
    pair = pl.program_id(0)
    sels, place = lane_rows(span)
    counts = [block_count(lengths[u]) for u in range(2)]
    most = jnp.maximum(counts[0], counts[1])
    for h in range(2):
        fill_bias(table.at[h], slopes[2 * pair + h], most, span)
    side = lax.broadcasted_iota(jnp.int32, (128, 128), 0) < 64
    other = lax.broadcasted_iota(jnp.int32, (128, 128), 1) >= 64
    gather = jnp.where(side == other, 1.0, 0.0).astype(jnp.bfloat16)
    for u in range(2):
        qa_in, k_in, v_in, g_in, att_in = inputs[u]
        k, v, g = k_in[...], v_in[...], g_in[...]
        product = g.astype(jnp.float32) * att_in[...].astype(jnp.float32)
        high = product.astype(jnp.bfloat16)
        low = (product - high.astype(jnp.float32)).astype(jnp.bfloat16)
        delta = split_parts(dot_nn(high, gather) + dot_nn(low, gather))
        grad_extra = sum(
            delta[i].astype(jnp.bfloat16) * one_hot(place, i, i + 1).astype(jnp.bfloat16)
            for i in range(3)
        )
        kt[u] = jnp.transpose(k)
        for h in range(2):
            sel = sels[h].astype(jnp.bfloat16)
            rest = (1.0 - sels[h]).astype(jnp.bfloat16)
            qa[u, h] = qa_in[h]
            ka[u, h] = key_tile(k, sels[h], place, lengths[u])
            va[u, h] = v * sel - ((1.0 - sels[h]) * one_hot(place, 0, 3)).astype(jnp.bfloat16)
            ga[u, h] = g * sel + grad_extra * rest
    dqt[...] = jnp.zeros_like(dqt)
    block_lane = lax.broadcasted_iota(jnp.int32, (KEY_BLOCK, 128), 1)

    def step(i, carry):
        u = (i >= counts[0]).astype(jnp.int32)
        at = pl.multiple_of((i - u * counts[0]) * KEY_BLOCK, KEY_BLOCK)
        keys = pl.ds(at, KEY_BLOCK)
        x0 = pl.multiple_of((span - KEY_BLOCK) - at, KEY_BLOCK)
        dk, dv = [], []
        for h in range(2):
            query_rows, grad_rows = qa[u, h], ga[u, h]
            s = dot_nt(ka[u, h, keys, :], query_rows)
            p = jnp.exp(s - table[h, :, pl.ds(x0, span)])
            d = (p * dot_nt(va[u, h, keys, :], grad_rows)).astype(jnp.bfloat16)
            dv.append(dot_nn(p.astype(jnp.bfloat16), grad_rows))
            dk.append(dot_nn(d, query_rows))
            rows = slice(64 * h, 64 * h + 64)
            dqt[u, rows] += dot_nn(kt[u, rows, keys], d)
        dk_out[u, keys, :] = jnp.where(block_lane < 64, dk[0], dk[1]).astype(jnp.bfloat16)
        dv_out[u, keys, :] = jnp.where(block_lane < 64, dv[0], dv[1]).astype(jnp.bfloat16)
        return carry

    lax.fori_loop(0, counts[0] + counts[1], step, 0)
    for u in range(2):

        def blank(b, carry, u=u):
            keys = pl.ds(pl.multiple_of(b * KEY_BLOCK, KEY_BLOCK), KEY_BLOCK)
            dk_out[u, keys, :] = jnp.zeros((KEY_BLOCK, 128), jnp.bfloat16)
            dv_out[u, keys, :] = jnp.zeros((KEY_BLOCK, 128), jnp.bfloat16)
            return carry

        lax.fori_loop(counts[u], span // KEY_BLOCK, blank, 0)
        dq_ref, dk_ref, dv_ref = outputs[u]
        dk_ref[...] = dk_out[u]
        dv_ref[...] = dv_out[u]
        dq_ref[...] = jnp.transpose((dqt[u] * 0.125).astype(jnp.bfloat16))


def attend_back(own, near, lengths, slopes):
    span, columns = own[1].shape
    pairs = columns // 384
    cells = span * span * pairs * 2
    table_width = 2 * span - KEY_BLOCK
    tall = pl.BlockSpec((span, 128), lambda p, *_: (0, p))
    heads = pl.BlockSpec((2, span, 128), lambda p, *_: (p, 0, 0))
    specs = [heads, pair_columns(span, pairs, 1), pair_columns(span, pairs, 2), tall, tall]
    tile = pltpu.VMEM((2, 2, span, 128), jnp.bfloat16)
    grads = pl.pallas_call(
        attend_back_kernel,
        out_shape=[jax.ShapeDtypeStruct((span, pairs * 128), jnp.bfloat16)] * 6,
        grid_spec=pltpu.PrefetchScalarGridSpec(
            num_scalar_prefetch=2,
            grid=(pairs,),
            in_specs=specs * 2,
            out_specs=[tall] * 6,
            scratch_shapes=[
                pltpu.VMEM((2, KEY_BLOCK, table_width), jnp.float32),
                tile,
                tile,
                tile,
                tile,
                pltpu.VMEM((2, 128, span), jnp.bfloat16),
                pltpu.VMEM((2, 128, span), jnp.float32),
                pltpu.VMEM((2, span, 128), jnp.bfloat16),
                pltpu.VMEM((2, span, 128), jnp.bfloat16),
            ],
        ),
        compiler_params=pltpu.CompilerParams(vmem_limit_bytes=56 << 20),
        cost_estimate=pl.CostEstimate(
            flops=cells * 10 * 256, bytes_accessed=span * columns * 16, transcendentals=cells
        ),
        name="attend_back",
    )(
        lengths, slopes,
        own[0], own[1], own[1], own[2], own[3],
        near[0], near[1], near[1], near[2], near[3],
    )
    return grads[:3], grads[3:]


CHUNK = 64


def filter_kernel(taps_count, scalars, gated_ref, taps_ref, out_ref, stats_ref, padded):
    span = gated_ref.shape[0]
    half = taps_count // 2
    length = scalars[0]
    padded[0:HALO] = jnp.zeros((HALO, 128), jnp.float32)
    padded[HALO + span : HALO + span + HALO] = jnp.zeros((HALO, 128), jnp.float32)
    padded[HALO : HALO + span] = gated_ref[...].astype(jnp.float32)

    def chunk(c, total):
        at = pl.multiple_of(c * CHUNK, CHUNK)
        value = jnp.zeros((CHUNK, 128), jnp.float32)
        for k in range(taps_count):
            value = value + padded[pl.ds(at + (HALO - half + k), CHUNK), :] * taps_ref[k : k + 1, :]
        out_ref[pl.ds(at, CHUNK), :] = value
        row = lax.broadcasted_iota(jnp.int32, (CHUNK, 128), 0) + at
        return total + jnp.sum(jnp.where(row < length, value, 0.0), axis=0, keepdims=True)

    total = lax.fori_loop(0, span // CHUNK, chunk, jnp.zeros((1, 128), jnp.float32))
    mean = total / length.astype(jnp.float32)

    def deviate(c, squares):
        at = pl.multiple_of(c * CHUNK, CHUNK)
        row = lax.broadcasted_iota(jnp.int32, (CHUNK, 128), 0) + at
        off = jnp.where(row < length, out_ref[pl.ds(at, CHUNK), :] - mean, 0.0)
        return squares + jnp.sum(off * off, axis=0, keepdims=True)

    squares = lax.fori_loop(0, span // CHUNK, deviate, jnp.zeros((1, 128), jnp.float32))
    stats_ref[...] = jnp.concatenate((total, squares, jnp.zeros((6, 128), jnp.float32)), 0)


def filter_frames(gated, taps, length):
    span, width = gated.shape
    return pl.pallas_call(
        functools.partial(filter_kernel, taps.shape[0]),
        out_shape=[
            jax.ShapeDtypeStruct((span, width), jnp.float32),
            jax.ShapeDtypeStruct((8, width), jnp.float32),
        ],
        grid_spec=pltpu.PrefetchScalarGridSpec(
            num_scalar_prefetch=1,
            grid=(width // 128,),
            in_specs=[
                pl.BlockSpec((span, 128), lambda c, *_: (0, c)),
                pl.BlockSpec((taps.shape[0], 128), lambda c, *_: (0, c)),
            ],
            out_specs=[
                pl.BlockSpec((span, 128), lambda c, *_: (0, c)),
                pl.BlockSpec((8, 128), lambda c, *_: (0, c)),
            ],
            scratch_shapes=[pltpu.VMEM((span + 2 * HALO, 128), jnp.float32)],
        ),
        cost_estimate=pl.CostEstimate(
            flops=64 * span * width, bytes_accessed=6 * span * width, transcendentals=0
        ),
        name="filter_frames",
    )(length, gated, taps)


def filter_turned(taps_count, padded, taps_ref, out_ref, cut):
    span = out_ref.shape[0]
    half = taps_count // 2

    def chunk(c, carry):
        at = pl.multiple_of(c * CHUNK, CHUNK)
        value = jnp.zeros((CHUNK, 128), jnp.float32)
        for k in range(taps_count):
            tap = taps_ref[k : k + 1, cut]
            value = value + padded[pl.ds(at + (HALO + half - k), CHUNK), :] * tap
        out_ref[pl.ds(at, CHUNK), cut] = value.astype(jnp.bfloat16)
        return carry

    lax.fori_loop(0, span // CHUNK, chunk, 0)


def filter_taps(taps_count, span, padded, gpadded, held):
    half = taps_count // 2

    def tally(c, sums):
        at = pl.multiple_of(c * CHUNK, CHUNK)
        grad = padded[pl.ds(at + HALO, CHUNK), :]
        added = []
        for k in range(taps_count):
            term = grad * gpadded[pl.ds(at + (HALO - half + k), CHUNK), :]
            folded = term[0:8]
            for r in range(8, CHUNK, 8):
                folded = folded + term[r : r + 8]
            added.append(sums[k] + folded)
        return tuple(added)

    blank = tuple(jnp.zeros((8, 128), jnp.float32) for _ in range(taps_count))
    sums = lax.fori_loop(0, span // CHUNK, tally, blank)
    rest = jnp.zeros((held - taps_count, 128), jnp.float32)
    return jnp.concatenate([column_sum(x) for x in sums] + [rest], 0)


def dot_tn(a, b):
    return lax.dot_general(a, b, (((0,), (0,)), ((), ())), preferred_element_type=jnp.float32)


def sigmoid(x):
    return 0.5 * jnp.tanh(0.5 * x) + 0.5


def silu_parts(x):
    s = sigmoid(x)
    value = x * s
    return value, s + value * (1.0 - s)


def normed_parts(x):
    centred = x - jnp.mean(x, -1, keepdims=True)
    scale = lax.rsqrt(jnp.mean(centred * centred, -1, keepdims=True) + EPSILON)
    return centred * scale, scale


def normed_back(n, scale, e):
    return scale * (e - jnp.mean(e, -1, keepdims=True) - n * jnp.mean(e * n, -1, keepdims=True))


def column_sum(x):
    return jnp.sum(x, axis=0, keepdims=True)


def add_rows(ref, rows):
    @pl.when(pl.program_id(0) == 0)
    def _():
        ref[...] = jnp.zeros_like(ref)

    width = ref.shape[1]
    ref[...] += jnp.concatenate(list(rows) + [jnp.zeros((8 - len(rows), width), jnp.float32)], 0)


def row_call(kernel, name, scalars, tall, whole, outs, sums, block, flops):
    span = tall[0].shape[0]

    def rows(columns):
        return pl.BlockSpec((block, columns), lambda i, *_: (i, 0))

    def kept(x):
        return pl.BlockSpec(x.shape, lambda i, *_: (0,) * x.ndim, pipeline_mode=pl.Buffered(1))

    width = whole[0].shape[-1]
    moved = sum(x.size * x.dtype.itemsize for x in tall + whole)
    moved += sum(span * c * jnp.dtype(d).itemsize for c, d in outs)
    return pl.pallas_call(
        kernel,
        out_shape=[jax.ShapeDtypeStruct((span, c), d) for c, d in outs]
        + [jax.ShapeDtypeStruct((8, width), jnp.float32)] * sums,
        grid_spec=pltpu.PrefetchScalarGridSpec(
            num_scalar_prefetch=1,
            grid=(span // block,),
            in_specs=[rows(x.shape[1]) for x in tall] + [kept(x) for x in whole],
            out_specs=[rows(c) for c, _ in outs]
            + [pl.BlockSpec((8, width), lambda i, *_: (0, 0))] * sums,
        ),
        compiler_params=pltpu.CompilerParams(vmem_limit_bytes=60 << 20),
        cost_estimate=pl.CostEstimate(
            flops=flops * span, bytes_accessed=moved, transcendentals=span * 2048
        ),
        name=name,
    )(scalars, *tall, *whole)


def head_columns(ref, which, width):
    return ref[:, pl.ds(pl.multiple_of(which * width, width), width)]


def head_rows(ref, which, width):
    return ref[pl.ds(pl.multiple_of(which * width, width), width), :]


def front_kernel(
    scalars, x_ref, gains, w_in, w_out, wq, wk, wv,
    normed_out, hidden_out, slope_out, after_out, mixer_out, own_out, far_out,
):
    core = scalars[0]
    x = x_ref[...].astype(jnp.float32)
    n, _ = normed_parts(x)
    normed = (n * gains[0:1]).astype(jnp.bfloat16)
    normed_out[...] = normed
    value, slope = silu_parts(dot_nn(normed, w_in[...]))
    hidden = value.astype(jnp.bfloat16)
    hidden_out[...] = hidden
    slope_out[...] = slope.astype(jnp.bfloat16)
    after = x + 0.5 * dot_nn(hidden, w_out[...])
    after_out[...] = after
    n, _ = normed_parts(after)
    mixer = (n * gains[1:2]).astype(jnp.bfloat16)
    mixer_out[...] = mixer
    half = wq.shape[1] // 2
    for out, which in ((far_out, 1 - core), (own_out, core)):
        for i, w in enumerate((wq, wk, wv)):
            out[:, i * half : (i + 1) * half] = dot_nn(mixer, head_columns(w, which, half)).astype(
                jnp.bfloat16
            )


def expand_kernel(
    scalars, own_ref, far_ref, after_ref, gains, w_output, w_expand,
    after_out, normed_out, gated_out, slope_out,
):
    core, length = scalars[0], scalars[1]
    block, half = own_ref.shape
    after = (
        after_ref[...]
        + dot_nn(own_ref[...], head_rows(w_output, core, half))
        + dot_nn(far_ref[...], head_rows(w_output, 1 - core, half))
    )
    after_out[...] = after
    n, _ = normed_parts(after)
    normed = (n * gains[0:1]).astype(jnp.bfloat16)
    normed_out[...] = normed
    expand = dot_nn(normed, w_expand[...])
    width = expand.shape[1] // 2
    row = lax.broadcasted_iota(jnp.int32, (block, width), 0) + pl.program_id(0) * block
    gate = sigmoid(expand[:, width:])
    live = jnp.where(row < length, gate, 0.0)
    gated = expand[:, :width] * live
    gated_out[...] = gated.astype(jnp.bfloat16)
    slope_out[:, :width] = live.astype(jnp.bfloat16)
    slope_out[:, width:] = (gated * (1.0 - gate)).astype(jnp.bfloat16)


def back_kernel(
    scalars, filtered_ref, after_ref, cot_ref, params, w_project, w_in, w_out,
    output_out, grad_out, dbn_out, swish_out, top_out, hidden_out, dpre_out, normed_out, half_out,
    sums,
):
    unit = (filtered_ref[...] - params[0:1]) * params[1:2]
    value, slope_bn = silu_parts(unit * params[2:3] + params[3:4])
    swish = value.astype(jnp.bfloat16)
    swish_out[...] = swish
    after_conv = after_ref[...] + dot_nn(swish, w_project[...])
    n1, r1 = normed_parts(after_conv)
    normed = (n1 * params[4:5]).astype(jnp.bfloat16)
    normed_out[...] = normed
    value, slope = silu_parts(dot_nn(normed, w_in[...]))
    hidden = value.astype(jnp.bfloat16)
    hidden_out[...] = hidden
    n2, r2 = normed_parts(after_conv + 0.5 * dot_nn(hidden, w_out[...]))
    output_out[...] = (n2 * params[5:6]).astype(jnp.bfloat16)

    cot = cot_ref[...].astype(jnp.float32)
    grad = normed_back(n2, r2, cot * params[5:6])
    half_grad = (0.5 * grad).astype(jnp.bfloat16)
    half_out[...] = half_grad
    dpre = (dot_nt(half_grad, w_out[...]) * slope).astype(jnp.bfloat16)
    dpre_out[...] = dpre
    dnormed = dot_nt(dpre, w_in[...])
    grad = grad + normed_back(n1, r1, dnormed * params[4:5])
    grad_out[...] = grad
    top = grad.astype(jnp.bfloat16)
    top_out[...] = top
    dbn = dot_nt(top, w_project[...]) * slope_bn
    dbn_out[...] = dbn
    add_rows(
        sums,
        [column_sum(dbn), column_sum(dbn * unit), column_sum(cot * n2), column_sum(dnormed * n1)],
    )


CORE_PACE, PAIR_PACE = 1.5, 22.0
HOP = 2.0
CHUNK_BUFFERS = 8
STAGES = 8


def chunk_scratch(chunks):
    dma = pltpu.SemaphoreType.DMA
    scratch = []
    for r, w, kind in chunks:
        shapes = [(2, r, w), (2, r, w), (2, r, w), (r, w), (r // 2, w), (r // 4, w), (r // 8, w), (r, w)]
        scratch += [pltpu.VMEM(shape, kind) for shape in shapes]
    n = len(chunks)
    return scratch + [dma((n, STAGES)), dma((n, STAGES))]


class Flow:
    def __init__(self, chunks, refs, finish, stages=None):
        count = len(chunks)
        self.stages = stages or [STAGES] * count
        self.chunks, self.finish = chunks, finish
        self.buffers = [refs[CHUNK_BUFFERS * c : CHUNK_BUFFERS * (c + 1)] for c in range(count)]
        self.send_sems, self.recv_sems = refs[CHUNK_BUFFERS * count :]
        me, n = lax.axis_index("tm"), lax.axis_size("tm")
        s = lax.axis_index("slots")
        self.core, self.y = lax.rem(s, 2), lax.div(s, 2)
        self.x, self.z = lax.rem(me, 2), lax.div(me, 2)
        self.sibling, self.across = {"slots": s + 1 - 2 * self.core}, {"slots": lax.rem(s + 2, 4)}
        self.beside = {"tm": me + 1 - 2 * self.x}
        self.low, self.high = lax.rem(self.z, 2), lax.div(self.z, 2)
        self.next, self.beyond = {"tm": me + 2 - 4 * self.low}, {"tm": me + 4 - 8 * self.high}
        self.sent = []
        self.going = {}
        self.clock, self.waiting, self.busy = 0.0, [], {}

    def put(self, c, y, even, odd):
        send, total = self.buffers[c][0], self.buffers[c][1]
        total[y] = jnp.where(self.core == 0, even, odd)
        send[y] = jnp.where(self.core == 0, odd, even)

    def put_all(self, c, terms):
        for y in range(2):
            self.put(c, y, terms[2 * y], terms[2 * y + 1])

    def stage(self, c, k):
        send, total, core_in, y_in, x_in, low_in, high_in, final = self.buffers[c]
        r, _, kind = self.chunks[c]
        x, y, low, high = self.x, self.y, self.low, self.high

        def add(ref, place, arrived):
            value = ref[place].astype(jnp.float32) + arrived.astype(jnp.float32)
            return value.astype(kind)

        def part(start, rows):
            return pl.ds(pl.multiple_of(start, rows), rows)

        half, quarter, piece = r // 2, r // 4, r // 8
        at_half = x * half
        at_quarter = at_half + low * quarter
        at_piece = at_quarter + high * piece
        if k:
            self.going[c].wait_recv()
        if k == 0:
            copy = (send, core_in, self.sibling)
        elif k == 1:
            for i in range(2):
                total[i] = add(total, i, core_in[i])
            copy = (total.at[1 - y], y_in, self.across)
        elif k == 2:
            total[y] = add(total, y, y_in[...])
            copy = (total.at[y, part((1 - x) * half, half)], x_in, self.beside)
        elif k == 3:
            mine = (y, part(at_half, half))
            total[mine] = add(total, mine, x_in[...])
            copy = (total.at[y, part(at_half + (1 - low) * quarter, quarter)], low_in, self.next)
        elif k == 4:
            mine = (y, part(at_quarter, quarter))
            total[mine] = add(total, mine, low_in[...])
            copy = (total.at[y, part(at_quarter + (1 - high) * piece, piece)], high_in, self.beyond)
        elif k == 5:
            mine = part(at_piece, piece)
            final[mine] = add(total, (y, mine), high_in[...])
            copy = (final.at[mine], final.at[mine], self.beyond)
        elif k == 6:
            mine = part(at_quarter, quarter)
            copy = (final.at[mine], final.at[mine], self.next)
        elif k == 7:
            mine = part(at_half, half)
            copy = (final.at[mine], final.at[mine], self.beside)
        if k == self.stages[c]:
            return
        source, target, where = copy
        copy = remote(source, target, self.send_sems.at[c, k], self.recv_sems.at[c, k], where)
        copy.start()
        self.sent.append(copy)
        self.going[c] = copy

    def occupy(self, link, time):
        self.busy[link] = max(self.busy.get(link, 0.0), self.clock) + time
        return self.busy[link] + HOP

    def step(self, c, k):
        self.stage(c, k)
        r, w, kind = self.chunks[c]
        size = r * w * jnp.dtype(kind).itemsize / 1e6
        half, quarter, piece = (size / cut * PAIR_PACE for cut in (2, 4, 8))
        pace = (
            ("core", 2 * size * CORE_PACE), ("y", size * PAIR_PACE), ("x", half), ("z", quarter),
            ("z", 2 * piece), ("z", 2 * piece), ("z", quarter), ("x", half),
        )
        if k < self.stages[c]:
            self.waiting.append((self.occupy(*pace[k]), c, k + 1))
        else:
            self.finish(c, self.buffers[c])
        self.clock += size

    def begin(self, c):
        self.step(c, 0)

    def spend(self, time):
        self.clock += time
        while self.waiting and min(self.waiting)[0] <= self.clock:
            first = min(self.waiting)
            self.waiting.remove(first)
            self.step(*first[1:])

    def drain(self):
        while self.waiting:
            self.spend(max(min(self.waiting)[0] - self.clock, 0.0))
        for copy in self.sent:
            copy.wait_send()


def greet(places):
    barrier = pltpu.get_barrier_semaphore()
    for place in places:
        pl.semaphore_signal(barrier, inc=1, device_id=place, device_id_type=MESH)
    pl.semaphore_wait(barrier, len(places))


class Named:
    def __init__(self, names, refs):
        self.__dict__.update(zip(names, refs))


def named_call(kernel, name, inputs, outputs, scratch, extra, collective_id, flops):
    names = [*inputs, *outputs, *scratch]

    def body(*refs):
        kernel(Named(names, refs), refs[len(names) :])

    results = pl.pallas_call(
        body,
        out_shape=[jax.ShapeDtypeStruct(shape, kind) for shape, kind, _ in outputs.values()],
        in_specs=[pl.BlockSpec(memory_space=space) for _, space in inputs.values()],
        out_specs=[pl.BlockSpec(memory_space=space) for _, _, space in outputs.values()],
        scratch_shapes=[*scratch.values(), *extra],
        compiler_params=pltpu.CompilerParams(
            collective_id=collective_id, has_side_effects=True, vmem_limit_bytes=62 << 20
        ),
        cost_estimate=pl.CostEstimate(
            flops=flops, bytes_accessed=sum(2 * x.size for x, _ in inputs.values()), transcendentals=0
        ),
        name=name,
    )(*(x for x, _ in inputs.values()))
    return Named(outputs, results)


class Stream:
    def __init__(self, sources, slots, semaphores, blocks):
        self.copies = [
            [
                pltpu.make_async_copy(ref.at[block], held.at[i % 2], semaphores.at[i % 2, j])
                for j, (ref, held) in enumerate(zip(sources, slots))
            ]
            for i, block in enumerate(blocks)
        ]

    def begin(self, i):
        if i < len(self.copies):
            for copy in self.copies[i]:
                copy.start()

    def take(self, i):
        self.begin(i + 1)
        for copy in self.copies[i]:
            copy.wait()


ROWS = 256


def middle_kernel(chunks, taps_count, r, flow_refs):
    t, s = lax.axis_index("tm"), lax.axis_index("slots")
    n, m = lax.axis_size("tm"), lax.axis_size("slots")
    span, width = r.half.shape
    shard = width // 4
    quarter, half = r.hidden.shape[1] // 4, width // 2
    back_chunks = len(chunks) - 3
    length = r.length[0]
    core = lax.rem(s, 2)
    wanted = ("half", "hidden", "normed", "dpre", "swish", "top")
    loads = {
        name: pltpu.make_async_copy(getattr(r, name), getattr(r, "held_" + name), r.load.at[i])
        for i, name in enumerate(wanted)
    }
    for load in loads.values():
        load.start()
    everything = slice(None)
    columns = Stream(
        [r.filtered, r.dbn, r.gated],
        [r.filtered_slots, r.dbn_slots, r.gated_slots],
        r.column_load,
        [(everything, slice(128 * c, 128 * c + 128)) for c in range(width // 128)],
    )
    rows = Stream(
        [r.glu_slope, r.grad, r.after],
        [r.slope_slots, r.grad_slots, r.after_slots],
        r.row_load,
        [(slice(i * ROWS, (i + 1) * ROWS), everything) for i in range(span // ROWS)],
    )
    columns.begin(0)
    rows.begin(0)

    slot_places = [{"slots": lax.rem(s + k, m)} for k in range(1, m)]
    tm_places = [{"tm": lax.rem(t + k, n)} for k in range(1, n)]
    greet(slot_places + tm_places)

    def share(source, landing, places, first):
        copies = [
            remote(source, landing.at[i], r.stat_send.at[first + i], r.stat_recv.at[first + i], place)
            for i, place in enumerate(places)
        ]
        for copy in copies:
            copy.start()
        return copies

    def gathered(copies, source, landing):
        for copy in copies:
            copy.wait()
        return add_blocks([source[...]] + [landing[i] for i in range(len(copies))])

    held = {}

    def need(name):
        if name not in held:
            loads[name].wait()
            held[name] = getattr(r, "held_" + name)
        return held[name]

    def finish(c, buffers):
        if c >= back_chunks:
            cut = slice((c - back_chunks) * shard, (c - back_chunks + 1) * shard)
            r.part_middle[cut] = buffers[1][flow.y]
            return
        value = buffers[-1][...].astype(jnp.float32)
        if c < 2:
            rows_here = chunks[0][0]
            r.part_out[c * rows_here : (c + 1) * rows_here] = value
        elif c < back_chunks - 1:
            r.part_in[:, (c - 2) * width : (c - 1) * width] = value
        else:
            r.part_project[...] = value

    flow = Flow(chunks, flow_refs, finish, [STAGES] * back_chunks + [2] * (len(chunks) - back_chunks))

    def make(c):
        if c < 2:
            a, b = need("hidden"), need("half")
            rows_here = chunks[0][0]
            terms = []
            for o in range(4):
                at = o * quarter + c * rows_here
                terms.append(dot_tn(a[:, at : at + rows_here], b[...]).astype(jnp.bfloat16))
        elif c < back_chunks - 1:
            b = need("dpre")[:, (c - 2) * width : (c - 1) * width]
            terms = dot_tn(need("normed")[...], b).astype(jnp.bfloat16).reshape(4, shard, width)
        else:
            terms = dot_tn(need("swish")[...], need("top")[...]).astype(jnp.bfloat16)
            terms = terms.reshape(4, shard, width)
        flow.put_all(c, terms)
        flow.begin(c)
        flow.spend(2.6 if c < 2 else 1.4)

    first = share(r.sums_in, r.stat_near, slot_places, 0)
    make(0)
    r.stat_mid[...] = gathered(first, r.sums_in, r.stat_near)
    second = share(r.stat_mid, r.stat_far, tm_places, m - 1)
    make(1)
    make(2)
    r.sums_out[...] = gathered(second, r.stat_mid, r.stat_far)
    for c in range(3, back_chunks):
        make(c)
    later = [
        pltpu.make_async_copy(source, target, r.load.at[i])
        for i, (source, target) in enumerate((
            (r.conv_normed, r.held_normed),
            (r.own_att, r.held_half.at[:, 0:half]),
            (r.far_att, r.held_half.at[:, half:width]),
        ))
    ]
    for copy in later:
        copy.start()

    halo = jnp.zeros((HALO, 128), jnp.float32)
    for ref in (r.padded, r.gpadded):
        ref[0:HALO] = halo
        ref[HALO + span : HALO + span + HALO] = halo
    for c in range(width // 128):
        columns.take(c)
        cut = slice(128 * c, 128 * c + 128)
        middle, inverse, gain = (r.params[i : i + 1, cut] for i in range(3))
        over = r.params[4:5, cut]
        shift_sum, scale_sum = r.sums_out[0:1, cut], r.sums_out[1:2, cut]
        r.gpadded[HALO : HALO + span] = r.gated_slots[c % 2].astype(jnp.float32)
        row = lax.broadcasted_iota(jnp.int32, (span, 128), 0)
        unit = (r.filtered_slots[c % 2] - middle) * inverse
        shift = (gain * shift_sum + unit * (gain * scale_sum)) * over
        r.padded[HALO : HALO + span] = inverse * (
            r.dbn_slots[c % 2] * gain - jnp.where(row < length, shift, 0.0)
        )
        filter_turned(taps_count, r.padded, r.taps, r.held_swish, cut)
        flow.spend(2.3)
        r.grad_taps[:, cut] = filter_taps(taps_count, span, r.padded, r.gpadded, r.grad_taps.shape[0])
        flow.spend(2.7)

    conv_sum = jnp.zeros((1, width), jnp.float32)
    outgoing, stores = [], []
    for i in range(span // ROWS):
        rows.take(i)
        cut = slice(i * ROWS, (i + 1) * ROWS)
        if i >= 2:
            for copy in stores[i - 2]:
                copy.wait()
        dgated = r.held_swish[cut].astype(jnp.float32)
        slopes = r.slope_slots[i % 2].astype(jnp.float32)
        dexpand = jnp.concatenate((dgated * slopes[:, :width], dgated * slopes[:, width:]), 1)
        dexpand = dexpand.astype(jnp.bfloat16)
        r.held_dpre[cut, 0 : 2 * width] = dexpand
        dnormed = dot_nt(dexpand, r.w_expand[...])
        normed, scale = normed_parts(r.after_slots[i % 2])
        grad = r.grad_slots[i % 2] + normed_back(normed, scale, dnormed * r.params[3:4])
        r.grad_store[i % 2] = grad
        top = grad.astype(jnp.bfloat16)
        r.held_top[cut] = top
        r.far_rows[cut] = dot_nt(top, head_rows(r.w_output, 1 - core, half)).astype(jnp.bfloat16)
        outgoing.append(
            remote(
                r.far_rows.at[cut], r.near_grad.at[cut], r.far_send.at[i], r.far_recv.at[i],
                flow.sibling,
            )
        )
        outgoing[-1].start()
        r.own_slots[i % 2] = dot_nt(top, head_rows(r.w_output, core, half)).astype(jnp.bfloat16)
        conv_sum = conv_sum + column_sum(dnormed * normed)
        stores.append([
            pltpu.make_async_copy(source.at[i % 2], target.at[cut], r.store.at[i % 2, j])
            for j, (source, target) in enumerate((
                (r.grad_store, r.grad_out),
                (r.own_slots, r.own_grad),
            ))
        ])
        for copy in stores[-1]:
            copy.start()
        flow.spend(2.0)
    r.conv_sums[...] = jnp.concatenate((conv_sum, jnp.zeros((7, width), jnp.float32)), 0)
    for copy in later:
        copy.wait()
    for j in range(2):
        b = r.held_dpre[:, j * width : (j + 1) * width]
        terms = dot_tn(r.held_normed[...], b).astype(jnp.bfloat16).reshape(4, shard, width)
        flow.put_all(back_chunks + j, terms)
        flow.begin(back_chunks + j)
        flow.spend(1.6)
    for which, lanes in ((core, slice(0, half)), (1 - core, slice(half, width))):
        terms = dot_tn(r.held_half[:, lanes], r.held_top[...]).astype(jnp.bfloat16)
        flow.put(back_chunks + 2, which, terms[:shard], terms[shard:])
    flow.begin(back_chunks + 2)
    flow.drain()
    for copy in outgoing + [copy for group in stores[-2:] for copy in group]:
        copy.wait()


def middle(length, sums, params, taps, w_expand, w_output, big, collective_id):
    bf16, f32 = jnp.bfloat16, jnp.float32
    anywhere, vmem = pl.ANY, pltpu.VMEM
    span, width = big["half"].shape
    ff = big["hidden"].shape[1]
    shard, quarter, half = width // 4, ff // 4, width // 2
    n, m = lax.axis_size("tm"), lax.axis_size("slots")
    dma = pltpu.SemaphoreType.DMA
    chunks = [(quarter // 2, width, bf16)] * 2 + [(shard, width, bf16)] * (ff // width + 4)
    held_taps = -(-taps.shape[0] // 8) * 8
    inputs = {"length": (length, pltpu.SMEM), "sums_in": (sums, vmem), "params": (params, vmem)}
    inputs |= {"taps": (taps, vmem), "w_expand": (w_expand, vmem), "w_output": (w_output, vmem)}
    inputs |= {name: (x, anywhere) for name, x in big.items()}
    outputs = {
        "part_in": ((shard, ff), f32, vmem),
        "part_out": ((quarter, width), f32, vmem),
        "part_project": ((shard, width), f32, vmem),
        "sums_out": ((8, width), f32, vmem),
        "conv_sums": ((8, width), f32, vmem),
        "grad_taps": ((held_taps, width), f32, vmem),
        "part_middle": ((3 * shard, width), bf16, vmem),
        "grad_out": ((span, width), f32, anywhere),
        "own_grad": ((span, half), bf16, anywhere),
        "near_grad": ((span, half), bf16, anywhere),
    }
    scratch = {
        "held_" + name: vmem(big[name].shape, bf16)
        for name in ("half", "hidden", "normed", "dpre", "swish", "top")
    }
    scratch |= {
        "load": dma((6,)),
        "filtered_slots": vmem((2, span, 128), f32),
        "dbn_slots": vmem((2, span, 128), f32),
        "gated_slots": vmem((2, span, 128), bf16),
        "column_load": dma((2, 3)),
        "slope_slots": vmem((2, ROWS, 2 * width), bf16),
        "grad_slots": vmem((2, ROWS, width), f32),
        "after_slots": vmem((2, ROWS, width), f32),
        "row_load": dma((2, 3)),
        "stat_near": vmem((m - 1, 8, width), f32),
        "stat_mid": vmem((8, width), f32),
        "stat_far": vmem((n - 1, 8, width), f32),
        "stat_send": dma((n + m - 2,)),
        "stat_recv": dma((n + m - 2,)),
        "padded": vmem((span + 2 * HALO, 128), f32),
        "gpadded": vmem((span + 2 * HALO, 128), f32),
        "grad_store": vmem((2, ROWS, width), f32),
        "own_slots": vmem((2, ROWS, half), bf16),
        "far_rows": vmem((span, half), bf16),
        "far_send": dma((span // ROWS,)),
        "far_recv": dma((span // ROWS,)),
        "store": dma((2, 2)),
    }
    return named_call(
        functools.partial(middle_kernel, chunks, taps.shape[0]), "middle", inputs, outputs, scratch,
        chunk_scratch(chunks), collective_id, span * (4 * ff * width + 8 * width * width),
    )


def closing_kernel(chunks, r, flow_refs):
    me, n = lax.axis_index("tm"), lax.axis_size("tm")
    core = lax.rem(lax.axis_index("slots"), 2)
    span, width = r.x.shape
    frames = span // n
    ff = r.hidden.shape[1]
    shard, quarter, half = width // 4, ff // 4, width // 2
    names = ("dq", "dk", "dv", "mixer", "hidden", "normed")
    loads = {
        name: pltpu.make_async_copy(getattr(r, name), getattr(r, "held_" + name), r.load.at[i])
        for i, name in enumerate(names)
    }
    for load in loads.values():
        load.start()
    order = sorted(range(1, n), key=lambda k: abs(k - n / 2)) + [0]
    homes = [lax.rem(me + k, n) for k in order]
    places = [pl.ds(pl.multiple_of(home * frames, frames), frames) for home in homes]
    rows = Stream(
        [r.grad, r.after, r.x, r.slope],
        [r.grad_slots, r.after_slots, r.x_slots, r.slope_slots],
        r.row_load,
        [(place, slice(None)) for place in places],
    )
    rows.begin(0)
    held = {}

    def need(name):
        if name not in held:
            loads[name].wait()
            held[name] = getattr(r, "held_" + name)
        return held[name]

    in_chunk = 3
    out_chunk = in_chunk + ff // width
    gain_chunk = len(chunks) - 1

    def finish(c, buffers):
        value = buffers[-1][...].astype(jnp.float32)
        if c < in_chunk:
            (r.part_query, r.part_key, r.part_value)[c][...] = value
        elif c < out_chunk:
            r.part_in[:, (c - in_chunk) * width : (c - in_chunk + 1) * width] = value
        elif c < gain_chunk:
            size = chunks[c][0]
            r.part_out[(c - out_chunk) * size : (c - out_chunk + 1) * size] = value
        else:
            r.part_gains[...] = value

    flow = Flow(chunks, flow_refs, finish)
    greet([{"tm": lax.rem(me + k, n)} for k in range(1, n)] + [flow.sibling, flow.across])
    heads = [
        remote(getattr(r, name), r.far.at[i], r.far_send.at[i], r.far_recv.at[i], flow.sibling)
        for i, name in enumerate(("near_dq", "near_dk", "near_dv"))
    ]
    for copy in heads:
        copy.start()

    sums = [jnp.zeros((1, width), jnp.float32)] * 2
    w_heads = (r.w_query, r.w_key, r.w_value)
    for i, name in enumerate(("dq", "dk", "dv")):
        mixer = need("mixer")[...]
        own = dot_tn(mixer, need(name)[...]).astype(jnp.bfloat16)
        heads[i].wait_recv()
        far = dot_tn(mixer, r.far[i]).astype(jnp.bfloat16)
        total = jnp.concatenate(
            (jnp.where(core == 0, own, far), jnp.where(core == 0, far, own)), 1
        )
        flow.put_all(i, total.reshape(4, shard, width))
        flow.begin(i)
        flow.spend(1.2)

    sends = []
    for i, place in enumerate(places):
        rows.take(i)
        dnormed = None
        for j, name in enumerate(("dq", "dk", "dv")):
            for which, d in ((core, need(name)[place]), (1 - core, r.far[j, place])):
                term = dot_nt(d, head_columns(w_heads[j], which, half))
                dnormed = term if dnormed is None else dnormed + term
        normed, scale = normed_parts(r.after_slots[i % 2])
        sums[1] = sums[1] + column_sum(dnormed * normed)
        grad = r.grad_slots[i % 2] + normed_back(normed, scale, dnormed * r.gains[1:2])
        half_grad = (0.5 * grad).astype(jnp.bfloat16)
        r.half_grad[place] = half_grad
        slope = r.slope_slots[i % 2].astype(jnp.float32)
        dpre = (dot_nt(half_grad, r.w_out[...]) * slope).astype(jnp.bfloat16)
        r.dpre[place] = dpre
        dnormed = dot_nt(dpre, r.w_in[...])
        normed, scale = normed_parts(r.x_slots[i % 2].astype(jnp.float32))
        sums[0] = sums[0] + column_sum(dnormed * normed)
        r.home_rows[place] = (
            grad + normed_back(normed, scale, dnormed * r.gains[0:1])
        ).astype(jnp.bfloat16)
        if order[i]:
            sends.append(
                remote(
                    r.home_rows.at[place], r.home.at[me], r.home_send.at[i], r.home_recv.at[i],
                    {"tm": homes[i]},
                )
            )
        else:
            sends.append(
                pltpu.make_async_copy(r.home_rows.at[place], r.home.at[me], r.home_send.at[i])
            )
        sends[-1].start()
        if order[i]:
            flow.occupy("z", 4.5)
            flow.occupy("x", 2.2)
        flow.spend(2.4)

    for j in range(ff // width):
        total = dot_tn(need("normed")[...], r.dpre[:, j * width : (j + 1) * width])
        flow.put_all(in_chunk + j, total.astype(jnp.bfloat16).reshape(4, shard, width))
        flow.begin(in_chunk + j)
        flow.spend(1.6)
    for j in range(gain_chunk - out_chunk):
        size = chunks[out_chunk + j][0]
        terms = []
        for o in range(4):
            at = o * quarter + j * size
            terms.append(
                dot_tn(need("hidden")[:, at : at + size], r.half_grad[...]).astype(jnp.bfloat16)
            )
        flow.put_all(out_chunk + j, terms)
        flow.begin(out_chunk + j)
        flow.spend(2.7)
    terms = []
    for o in range(4):
        lanes = slice(o * shard, (o + 1) * shard)
        terms.append(
            jnp.concatenate((sums[0][:, lanes], sums[1][:, lanes], r.small[o, 2:]), 0)
        )
    flow.put_all(gain_chunk, terms)
    flow.begin(gain_chunk)
    flow.drain()
    for copy in heads:
        copy.wait_send()
    for copy in sends:
        copy.wait()


def closing(gains, small, weights, big, collective_id):
    bf16, f32 = jnp.bfloat16, jnp.float32
    anywhere, vmem = pl.ANY, pltpu.VMEM
    dma = pltpu.SemaphoreType.DMA
    span, width = big["x"].shape
    ff = big["hidden"].shape[1]
    n = lax.axis_size("tm")
    shard, quarter, half, frames = width // 4, ff // 4, width // 2, span // n
    chunks = [(shard, width, bf16)] * (3 + ff // width)
    chunks += [(quarter // 2, width, bf16)] * 2 + [small.shape[1:] + (f32,)]
    inputs = {"gains": (gains, vmem), "small": (small, vmem)}
    inputs |= {name: (x, vmem) for name, x in weights.items()}
    inputs |= {name: (x, anywhere) for name, x in big.items()}
    outputs = {
        "part_in": ((shard, ff), f32, vmem),
        "part_out": ((quarter, width), f32, vmem),
        "part_query": ((shard, width), f32, vmem),
        "part_key": ((shard, width), f32, vmem),
        "part_value": ((shard, width), f32, vmem),
        "part_gains": (small.shape[1:], f32, vmem),
        "home": ((n, frames, width), bf16, anywhere),
    }
    scratch = {
        "held_" + name: vmem(big[name].shape, bf16)
        for name in ("dq", "dk", "dv", "mixer", "hidden", "normed")
    }
    scratch |= {
        "load": dma((6,)),
        "grad_slots": vmem((2, frames, width), f32),
        "after_slots": vmem((2, frames, width), f32),
        "x_slots": vmem((2, frames, width), bf16),
        "slope_slots": vmem((2, frames, ff), bf16),
        "row_load": dma((2, 4)),
        "far": vmem((3, span, half), bf16),
        "far_send": dma((3,)),
        "far_recv": dma((3,)),
        "half_grad": vmem((span, width), bf16),
        "dpre": vmem((span, ff), bf16),
        "home_rows": vmem((span, width), bf16),
        "home_send": dma((n,)),
        "home_recv": dma((n,)),
    }
    return named_call(
        functools.partial(closing_kernel, chunks), "closing", inputs, outputs, scratch,
        chunk_scratch(chunks), collective_id, span * (8 * ff * width + 12 * width * width),
    )


def with_halo(block, sides, width):
    for axis, dim in sides:
        count = lax.axis_size(axis)
        forward = [(i, i + 1) for i in range(count - 1)]
        backward = [(target, source) for source, target in forward]
        low = lax.ppermute(
            lax.slice_in_dim(block, block.shape[dim] - width, None, axis=dim), axis, forward
        )
        high = lax.ppermute(lax.slice_in_dim(block, 0, width, axis=dim), axis, backward)
        block = jnp.concatenate([low, block, high], axis=dim)
    return block


def layer_norm(inputs, norm_gain):
    centred = inputs - jnp.mean(inputs, -1, keepdims=True)
    spread = jnp.mean(centred * centred, -1, keepdims=True)
    return centred * lax.rsqrt(spread + EPSILON) * norm_gain


def norm_back(inputs, norm_gain, incoming):
    result, pullback = jax.vjp(layer_norm, inputs, norm_gain)
    return pullback(incoming)


def matmul(left_side, right_side):
    return jnp.dot(left_side, right_side, preferred_element_type=jnp.float32)


def matmul_tn(left_side, right_side):
    return lax.dot_general(
        left_side, right_side, (((0,), (0,)), ((), ())), preferred_element_type=jnp.float32
    )


def matmul_nt(left_side, right_side):
    return lax.dot_general(
        left_side, right_side, (((1,), (1,)), ((), ())), preferred_element_type=jnp.float32
    )


def silu_slope(inputs):
    sigmoid_gate = jax.nn.sigmoid(inputs)
    return sigmoid_gate * (1.0 + inputs * (1.0 - sigmoid_gate))


def feed_forward(residual_rows, norm_gain, w_in, w_out):
    normed = layer_norm(residual_rows, norm_gain).astype(jnp.bfloat16)
    before_act = matmul(normed, w_in)
    hidden = jax.nn.silu(before_act).astype(jnp.bfloat16)
    return (residual_rows + 0.5 * matmul(hidden, w_out), (normed, before_act, hidden))


def feed_back(residual_rows, norm_gain, w_in, w_out, kept, incoming):
    normed, before_act, hidden = kept
    grad_top = (0.5 * incoming).astype(jnp.bfloat16)
    grad_w_out = matmul_tn(hidden, grad_top)
    grad_before = (matmul_nt(grad_top, w_out) * silu_slope(before_act)).astype(jnp.bfloat16)
    grad_w_in = matmul_tn(normed, grad_before)
    grad_normed = matmul_nt(grad_before, w_in)
    grad_rows, grad_gain = norm_back(residual_rows, norm_gain, grad_normed)
    return (incoming + grad_rows, grad_gain, grad_w_in, grad_w_out)


def exchange(x, pairs=CORE_PAIRS):
    return lax.ppermute(x, "slots", pairs)


def on_device_fast(
    features, lengths, cotangent, front_gain, front_in, front_out, mixer_gain, query_weight,
    key_weight, value_weight, output_weight, conv_gain, expand_weight, depth_weight, batch_gain,
    batch_bias, project_weight, back_gain, back_in, back_out, final_gain,
):
    slot_count, frames_dev, width = features.shape
    full_length = slot_count * frames_dev
    head_dim = width // HEADS
    half = width // 2
    tm, slots = lax.axis_index("tm"), lax.axis_index("slots")
    core = lax.rem(slots, 2)
    shard = front_gain.shape[0]
    taps_count = depth_weight.shape[1]

    def ordered(group_lengths, backward):
        numbers = jnp.arange(slot_count, dtype=jnp.int32)
        mine, theirs = group_lengths[:, None], group_lengths[None, :]
        ahead = (theirs > mine) | ((theirs == mine) & (numbers[None, :] < numbers[:, None]))
        rank = jnp.sum(ahead.astype(jnp.int32), 1)
        rank = jnp.where(backward, slot_count - 1 - rank, rank)
        order = jnp.sum(jnp.where(rank[:, None] == numbers[None, :], numbers[:, None], 0), 0)
        return rank, order

    rank, order = ordered(lengths, core == 1)
    small = [front_gain, mixer_gain, conv_gain, batch_gain, batch_bias, back_gain, final_gain]
    pack = jnp.concatenate(
        [x.astype(jnp.float32)[None] for x in small]
        + [depth_weight.astype(jnp.float32).T]
        + [jnp.pad(lengths.astype(jnp.float32), (0, shard - slot_count))[None]],
        0,
    )
    pack = jnp.pad(pack, ((0, -pack.shape[0] % 8), (0, 0)))
    pack_rows = pack.shape[0]
    rows_bf16, full_front_in, full_front_out, full_query, full_key, full_value, packs = (
        entry_exchange(
            take_slots(features, order),
            [front_in, front_out, query_weight, key_weight, value_weight, pack],
        )
    )
    others = jnp.concatenate([output_weight, expand_weight, project_weight], 1)
    others, back_in, back_out, cotangent, _ = lax.optimization_barrier(
        (others, back_in, back_out, cotangent, packs)
    )
    gather = functools.partial(lax.all_gather, axis_name="slots", axis=0, tiled=True)
    full_others, full_back_in, full_back_out = gather(others), gather(back_in), gather(back_out)
    full_output = full_others[:, :width]
    full_expand = full_others[:, width : 3 * width]
    full_project = full_others[:, 3 * width :]
    cot_rows = lax.all_to_all(take_slots(cotangent, order), "tm", 0, 1, tiled=True)[0]

    packs = packs.reshape(-1, pack_rows, shard)
    params = jnp.transpose(packs, (1, 0, 2)).reshape(pack_rows, width)
    (front_norm_gain, mixer_norm_gain, conv_norm_gain, batch_scale, batch_shift, back_norm_gain,
     final_norm_gain) = (params[i] for i in range(7))
    depth_taps = params[7 : 7 + taps_count]
    all_lengths = packs[:, 7 + taps_count, :slot_count].astype(jnp.int32)
    frames_total = jnp.sum(all_lengths).astype(jnp.float32)
    length = jnp.sum(jnp.where(jnp.arange(slot_count) == tm, lengths[order], 0))
    near = lax.dynamic_index_in_dim(all_lengths, slots + 1 - 2 * core, 0, False)
    near_order = ordered(near, core == 0)[1]
    near_length = jnp.sum(jnp.where(jnp.arange(slot_count) == tm, near[near_order], 0))
    length, near_length = length.reshape(1), near_length.reshape(1)
    head_numbers = (jnp.arange(HEADS // 2, dtype=jnp.int32) + core * (HEADS // 2)).astype(jnp.float32)
    slopes = 64.0 * 2.0 ** (-head_numbers) / full_length
    def stack(*rows):
        return jnp.concatenate(
            [r[None] for r in rows] + [jnp.zeros((8 - len(rows), width), jnp.float32)], 0
        )

    bf16, f32 = jnp.bfloat16, jnp.float32
    ff = front_in.shape[1]
    scalars = jnp.concatenate([core.reshape(1), length])
    front_gains = stack(front_norm_gain, mixer_norm_gain)
    front_normed, front_hidden, front_slope, after_front, mixer_normed, own_qkv, far_qkv = row_call(
        front_kernel, "front", scalars, [rows_bf16],
        [front_gains, full_front_in, full_front_out, full_query, full_key, full_value],
        [(width, bf16), (ff, bf16), (ff, bf16), (width, f32), (width, bf16), (3 * half, bf16), (3 * half, bf16)],
        0, 512, 4 * width * ff + 6 * width * width,
    )
    near_qkv = exchange(far_qkv)
    both_lengths = jnp.concatenate([length, near_length])
    own_att, near_att, own_qa, near_qa = attend(own_qkv, near_qkv, both_lengths, slopes)
    far_att = exchange(near_att)
    conv_gains = stack(conv_norm_gain)
    after_mixer, conv_normed, gated, glu_slope = row_call(
        expand_kernel, "expand", scalars, [own_att, far_att, after_front],
        [conv_gains, full_output, full_expand],
        [(width, f32), (width, bf16), (width, bf16), (2 * width, bf16)],
        0, 512, 6 * width * width,
    )
    filtered, stats = filter_frames(gated, depth_taps, length)
    counted = jnp.concatenate(
        [stats[:2], jnp.full((1, width), length.astype(f32)[0]), stats[3:]], 0
    )
    shared = share_stats(counted, merge_spreads, 1)
    middle_row = shared[0] / frames_total
    spread = shared[1] / frames_total
    inverse_spread = lax.rsqrt(spread + EPSILON)

    params8 = stack(
        middle_row, inverse_spread, batch_scale, batch_shift, back_norm_gain, final_norm_gain
    )
    (output_rows, grad_rows, dbn, swish, conv_top, back_hidden, back_dpre, back_normed, back_half,
     back_sums) = row_call(
        back_kernel, "back", scalars, [filtered, after_mixer, cot_rows],
        [params8, full_project, full_back_in, full_back_out],
        [(width, bf16), (width, f32), (width, f32), (width, bf16), (width, bf16), (ff, bf16),
         (ff, bf16), (width, bf16), (width, bf16)],
        1, 256, 8 * width * ff + 4 * width * width,
    )
    params5 = stack(
        middle_row,
        inverse_spread,
        batch_scale,
        conv_norm_gain,
        jnp.full((width,), 1.0, f32) / frames_total,
    )
    mid = middle(
        length, back_sums, params5, depth_taps, full_expand, full_output,
        dict(hidden=back_hidden, dpre=back_dpre, half=back_half, normed=back_normed, swish=swish,
             top=conv_top, filtered=filtered, dbn=dbn, gated=gated, glu_slope=glu_slope,
             grad=grad_rows, after=after_mixer, conv_normed=conv_normed, own_att=own_att,
             far_att=far_att),
        2,
    )
    grad_batch_shift, grad_batch_scale = mid.sums_out[0], mid.sums_out[1]

    output_rows, _ = lax.optimization_barrier((output_rows, mid.sums_out))
    parts = lax.all_to_all(
        output_rows.reshape(slot_count, frames_dev, width), "tm", 0, 0, tiled=True
    )
    output = take_slots(parts, rank)
    part_middle = lax.psum(mid.part_middle, "tm").astype(f32)
    own_dqkv, near_dqkv = attend_back(
        (own_qa, own_qkv, mid.own_grad, own_att),
        (near_qa, near_qkv, mid.near_grad, near_att),
        both_lengths,
        slopes,
    )
    small = jnp.concatenate(
        [
            jnp.zeros((2, width), f32),
            mid.conv_sums[:1],
            back_sums[3:4],
            back_sums[2:3],
            mid.grad_taps[:taps_count],
        ],
        0,
    )
    small = jnp.pad(small, ((0, -small.shape[0] % 64), (0, 0)))
    small = jnp.transpose(small.reshape(-1, 4, shard), (1, 0, 2))
    last = closing(
        front_gains, small,
        dict(w_in=full_front_in, w_out=full_front_out, w_query=full_query, w_key=full_key,
             w_value=full_value),
        dict(dq=own_dqkv[0], dk=own_dqkv[1], dv=own_dqkv[2],
             near_dq=near_dqkv[0], near_dk=near_dqkv[1], near_dv=near_dqkv[2], mixer=mixer_normed,
             hidden=front_hidden, normed=front_normed, grad=mid.grad_out, after=after_front,
             x=rows_bf16, slope=front_slope),
        3,
    )
    grad_features = take_slots(last.home, rank)
    gains = last.part_gains

    def own_part(row):
        return lax.dynamic_slice_in_dim(row, slots * shard, shard, 0)

    part_depth = gains[5 : 5 + taps_count].T
    return (
        output,
        grad_features,
        gains[0],
        last.part_in,
        last.part_out,
        gains[1],
        last.part_query,
        last.part_key,
        last.part_value,
        part_middle[2 * shard :],
        gains[2],
        jnp.concatenate((part_middle[:shard], part_middle[shard : 2 * shard]), 1),
        part_depth,
        own_part(grad_batch_scale),
        own_part(grad_batch_shift),
        mid.part_project,
        gains[3],
        mid.part_in,
        mid.part_out,
        gains[4],
    )


def on_device(features, *rest):
    whole = features.shape[0] == lax.axis_size("tm") and lax.axis_size("slots") == 4
    return (on_device_fast if whole else on_device_general)(features, *rest)


def on_device_general(
    features,
    lengths,
    cotangent,
    front_gain,
    front_in,
    front_out,
    mixer_gain,
    query_weight,
    key_weight,
    value_weight,
    output_weight,
    conv_gain,
    expand_weight,
    depth_weight,
    batch_gain,
    batch_bias,
    project_weight,
    back_gain,
    back_in,
    back_out,
    final_gain,
):
    gathered = (
        lax.all_gather(front_gain, "slots", axis=0, tiled=True),
        lax.all_gather(front_in, "slots", axis=0, tiled=True),
        lax.all_gather(front_out, "slots", axis=0, tiled=True),
        lax.all_gather(mixer_gain, "slots", axis=0, tiled=True),
        lax.all_gather(query_weight, "slots", axis=0, tiled=True),
        lax.all_gather(key_weight, "slots", axis=0, tiled=True),
        lax.all_gather(value_weight, "slots", axis=0, tiled=True),
        lax.all_gather(output_weight, "slots", axis=0, tiled=True),
        lax.all_gather(conv_gain, "slots", axis=0, tiled=True),
        lax.all_gather(expand_weight, "slots", axis=0, tiled=True),
        lax.all_gather(depth_weight, "slots", axis=0, tiled=True),
        lax.all_gather(batch_gain, "slots", axis=0, tiled=True),
        lax.all_gather(batch_bias, "slots", axis=0, tiled=True),
        lax.all_gather(project_weight, "slots", axis=0, tiled=True),
        lax.all_gather(back_gain, "slots", axis=0, tiled=True),
        lax.all_gather(back_in, "slots", axis=0, tiled=True),
        lax.all_gather(back_out, "slots", axis=0, tiled=True),
        lax.all_gather(final_gain, "slots", axis=0, tiled=True),
    )
    (
        full_front_gain,
        full_front_in,
        full_front_out,
        full_mixer_gain,
        full_query,
        full_key,
        full_value,
        full_output,
        full_conv_gain,
        full_expand,
        full_depth,
        full_batch_gain,
        full_batch_bias,
        full_project,
        full_back_gain,
        full_back_in,
        full_back_out,
        full_final_gain,
    ) = gathered
    front_norm_gain = full_front_gain.astype(jnp.float32)
    mixer_norm_gain = full_mixer_gain.astype(jnp.float32)
    conv_norm_gain = full_conv_gain.astype(jnp.float32)
    batch_scale = full_batch_gain.astype(jnp.float32)
    batch_shift = full_batch_bias.astype(jnp.float32)
    back_norm_gain = full_back_gain.astype(jnp.float32)
    final_norm_gain = full_final_gain.astype(jnp.float32)
    depth_taps = full_depth.astype(jnp.float32)
    slot_count, frames_dev, width = features.shape
    row_count = slot_count * frames_dev
    full_length = frames_dev * lax.axis_size("tm")
    head_dim = width // HEADS
    taps_count = full_depth.shape[1]
    half_width = taps_count // 2
    score_scale = 1.0 / math.sqrt(head_dim)
    head_numbers = jnp.arange(HEADS, dtype=jnp.int32)
    frame_index = lax.axis_index("tm") * frames_dev + jnp.arange(frames_dev, dtype=jnp.int32)
    frame_mask = (frame_index[None, :] < lengths[:, None]).astype(jnp.float32).reshape(row_count, 1)
    residual_rows = features.astype(jnp.float32).reshape(row_count, width)
    after_front, front_kept = feed_forward(
        residual_rows, front_norm_gain, full_front_in, full_front_out
    )
    mixer_normed = layer_norm(after_front, mixer_norm_gain).astype(jnp.bfloat16)
    query_rows = (
        matmul(mixer_normed, full_query).astype(jnp.bfloat16).reshape(slot_count, frames_dev, width)
    )
    key_rows = (
        matmul(mixer_normed, full_key).astype(jnp.bfloat16).reshape(slot_count, frames_dev, width)
    )
    value_rows = (
        matmul(mixer_normed, full_value).astype(jnp.bfloat16).reshape(slot_count, frames_dev, width)
    )

    def head_scores(head_index, key_part):
        span_keys = key_part.shape[1]
        query_head = lax.dynamic_slice_in_dim(query_rows, head_index * head_dim, head_dim, 2)
        key_head = lax.dynamic_slice_in_dim(key_part, head_index * head_dim, head_dim, 2)
        products = jnp.einsum(
            "ucd,und->ucn", query_head, key_head, preferred_element_type=jnp.float32
        )
        key_index = jnp.arange(span_keys, dtype=jnp.int32)
        slope_head = 64.0 * 2.0 ** (-head_index.astype(jnp.float32)) / full_length
        distance = jnp.abs(frame_index[:, None] - key_index[None, :]).astype(jnp.float32)
        scores = products * score_scale - slope_head * distance
        usable = key_index[None, None, :] < lengths[:, None, None]
        return (scores, usable, query_head, key_head)

    start_state = (
        jnp.full((HEADS, slot_count, frames_dev), -1e30, jnp.float32),
        jnp.zeros((HEADS, slot_count, frames_dev), jnp.float32),
        jnp.zeros((HEADS, slot_count, frames_dev, head_dim), jnp.float32),
    )
    key_part = lax.all_gather(key_rows, "tm", axis=1, tiled=True)
    value_part = lax.all_gather(value_rows, "tm", axis=1, tiled=True)

    def absorb_per_head(inputs):
        head_index, run_max, run_sum, accumulator = inputs
        scores, usable, query_head, key_head = head_scores(head_index, key_part)
        value_head = lax.dynamic_slice_in_dim(value_part, head_index * head_dim, head_dim, 2)
        new_max = jnp.maximum(run_max, jnp.max(jnp.where(usable, scores, -1e30), -1))
        weights_now = jnp.where(usable, jnp.exp(scores - new_max[..., None]), 0.0)
        factor = jnp.exp(run_max - new_max)
        new_sum = run_sum * factor + jnp.sum(weights_now, -1)
        new_accum = accumulator * factor[..., None] + jnp.einsum(
            "ucn,und->ucd",
            weights_now.astype(jnp.bfloat16),
            value_head,
            preferred_element_type=jnp.float32,
        )
        return (new_max, new_sum, new_accum)

    run_max, run_sum, accumulator = lax.map(absorb_per_head, (head_numbers,) + tuple(start_state))
    attended = accumulator / run_sum[..., None]
    log_total = run_max + jnp.log(run_sum)
    mixture = jnp.transpose(attended, (1, 2, 0, 3)).reshape(row_count, width).astype(jnp.bfloat16)
    after_mixer = after_front + matmul(mixture, full_output)
    conv_normed = layer_norm(after_mixer, conv_norm_gain).astype(jnp.bfloat16)
    expand = matmul(conv_normed, full_expand)
    linear_half = expand[:, :width]
    sigmoid_gate = jax.nn.sigmoid(expand[:, width:])
    gated = (
        (linear_half * sigmoid_gate * frame_mask)
        .astype(jnp.bfloat16)
        .reshape(slot_count, frames_dev, width)
    )
    padded = with_halo(gated, (("tm", 1),), half_width)
    filtered = padded[:, 0:frames_dev, :] * depth_taps[:, 0]
    for kernel_tap in range(1, taps_count):
        filtered = (
            filtered
            + padded[:, kernel_tap : kernel_tap + frames_dev, :] * depth_taps[:, kernel_tap]
        )
    filtered = filtered.reshape(row_count, width)
    mask_total, frames_total = lax.psum(
        (jnp.sum(filtered * frame_mask, 0), jnp.sum(frame_mask)), ("tm", "slots")
    )
    middle = mask_total / frames_total
    offset = filtered - middle
    spread = lax.psum(jnp.sum(frame_mask * offset * offset, 0), ("tm", "slots")) / frames_total
    inverse_spread = lax.rsqrt(spread + EPSILON)
    unit_conv = offset * inverse_spread
    batch_normed = unit_conv * batch_scale + batch_shift
    swish = jax.nn.silu(batch_normed).astype(jnp.bfloat16)
    after_conv = after_mixer + matmul(swish, full_project)
    after_back, back_kept = feed_forward(after_conv, back_norm_gain, full_back_in, full_back_out)
    output = (
        layer_norm(after_back, final_norm_gain)
        .astype(jnp.bfloat16)
        .reshape(slot_count, frames_dev, width)
    )
    incoming = cotangent.astype(jnp.float32).reshape(row_count, width)
    grad_rows, grad_final = norm_back(after_back, final_norm_gain, incoming)
    grad_rows, grad_back_gain, grad_back_in, grad_back_out = feed_back(
        after_conv, back_norm_gain, full_back_in, full_back_out, back_kept, grad_rows
    )
    grad_conv_top = grad_rows.astype(jnp.bfloat16)
    grad_project = matmul_tn(swish, grad_conv_top)
    grad_batch_normed = matmul_nt(grad_conv_top, full_project) * silu_slope(batch_normed)
    grad_batch_scale = jnp.sum(grad_batch_normed * unit_conv, 0)
    grad_batch_shift = jnp.sum(grad_batch_normed, 0)
    grad_unit = grad_batch_normed * batch_scale
    sum_plain, sum_scaled = lax.psum(
        (jnp.sum(grad_unit, 0), jnp.sum(grad_unit * unit_conv, 0)), ("tm", "slots")
    )
    grad_filtered = inverse_spread * (
        grad_unit - frame_mask * (sum_plain + unit_conv * sum_scaled) / frames_total
    )
    grad_grid = grad_filtered.reshape(slot_count, frames_dev, width)
    grad_padded = with_halo(grad_grid.astype(jnp.bfloat16), (("tm", 1),), half_width).astype(
        grad_grid.dtype
    )
    grad_gated = jnp.zeros((slot_count, frames_dev, width), jnp.float32)
    taps_grad = []
    for kernel_tap in range(taps_count):
        lead = 2 * half_width - kernel_tap
        grad_gated = (
            grad_gated + depth_taps[:, kernel_tap] * grad_padded[:, lead : lead + frames_dev, :]
        )
        taps_grad.append(
            jnp.sum(grad_grid * padded[:, kernel_tap : kernel_tap + frames_dev, :], axis=(0, 1))
        )
    grad_depth = jnp.stack(taps_grad, axis=1)
    grad_gated_low = lax.optimization_barrier(
        grad_gated.reshape(row_count, width).astype(jnp.bfloat16)
    ).astype(jnp.float32)
    grad_masked = grad_gated_low * frame_mask
    grad_linear = grad_masked * sigmoid_gate
    grad_gate = grad_masked * linear_half * sigmoid_gate * (1.0 - sigmoid_gate)
    grad_expand = jnp.concatenate([grad_linear, grad_gate], 1).astype(jnp.bfloat16)
    grad_expand_weight = matmul_tn(conv_normed, grad_expand)
    grad_conv_normed = matmul_nt(grad_expand, full_expand)
    delta_rows, grad_conv_gain = norm_back(after_mixer, conv_norm_gain, grad_conv_normed)
    grad_rows = grad_rows + delta_rows
    grad_mix_top = grad_rows.astype(jnp.bfloat16)
    grad_output_weight = matmul_tn(mixture, grad_mix_top)
    grad_mixture = matmul_nt(grad_mix_top, full_output).astype(jnp.bfloat16)
    grad_heads = jnp.transpose(
        grad_mixture.reshape(slot_count, frames_dev, HEADS, head_dim), (2, 0, 1, 3)
    )
    delta_heads = jnp.sum(grad_heads.astype(jnp.float32) * attended, -1)
    start_grads = (
        jnp.zeros((HEADS, slot_count, frames_dev, head_dim), jnp.float32),
        jnp.zeros((HEADS, slot_count, full_length, head_dim), jnp.float32),
        jnp.zeros((HEADS, slot_count, full_length, head_dim), jnp.float32),
    )
    collect_key_part = lax.all_gather(key_rows, "tm", axis=1, tiled=True)
    collect_value_part = lax.all_gather(value_rows, "tm", axis=1, tiled=True)
    span_keys = collect_key_part.shape[1]

    def collect_per_head(inputs):
        head_index, grad_query, key_sums, value_sums, total_log, delta_head, grad_head = inputs
        scores, usable, query_head, key_head = head_scores(head_index, collect_key_part)
        value_head = lax.dynamic_slice_in_dim(
            collect_value_part, head_index * head_dim, head_dim, 2
        )
        probs = jnp.where(usable, jnp.exp(scores - total_log[..., None]), 0.0)
        grad_probs = jnp.einsum(
            "ucd,und->ucn", grad_head, value_head, preferred_element_type=jnp.float32
        )
        grad_raw = (probs * (grad_probs - delta_head[..., None]) * score_scale).astype(jnp.bfloat16)
        grad_query = grad_query + jnp.einsum(
            "ucn,und->ucd", grad_raw, key_head, preferred_element_type=jnp.float32
        )
        key_term = jnp.einsum(
            "ucn,ucd->und", grad_raw, query_head, preferred_element_type=jnp.float32
        )
        value_term = jnp.einsum(
            "ucn,ucd->und",
            probs.astype(jnp.bfloat16),
            grad_head,
            preferred_element_type=jnp.float32,
        )
        key_sums = key_sums + key_term
        value_sums = value_sums + value_term
        return (grad_query, key_sums, value_sums)

    folded = lax.map(
        collect_per_head,
        (head_numbers,) + tuple(start_grads) + (log_total, delta_heads, grad_heads),
    )
    grad_query_heads, key_sums, value_sums = folded
    grad_key_heads, grad_value_heads = (
        lax.psum_scatter(
            key_sums.astype(jnp.bfloat16), "tm", scatter_dimension=2, tiled=True
        ).astype(jnp.float32),
        lax.psum_scatter(
            value_sums.astype(jnp.bfloat16), "tm", scatter_dimension=2, tiled=True
        ).astype(jnp.float32),
    )

    def to_rows(heads_array):
        return (
            jnp.transpose(heads_array, (1, 2, 0, 3)).reshape(row_count, width).astype(jnp.bfloat16)
        )

    grad_query_rows = to_rows(grad_query_heads)
    grad_key_rows = to_rows(grad_key_heads)
    grad_value_rows = to_rows(grad_value_heads)
    grad_query_weight = matmul_tn(mixer_normed, grad_query_rows)
    grad_key_weight = matmul_tn(mixer_normed, grad_key_rows)
    grad_value_weight = matmul_tn(mixer_normed, grad_value_rows)
    grad_mixer_normed = (
        matmul_nt(grad_query_rows, full_query)
        + matmul_nt(grad_key_rows, full_key)
        + matmul_nt(grad_value_rows, full_value)
    )
    delta_rows, grad_mixer_gain = norm_back(after_front, mixer_norm_gain, grad_mixer_normed)
    grad_rows = grad_rows + delta_rows
    grad_rows, grad_front_gain, grad_front_in, grad_front_out = feed_back(
        residual_rows, front_norm_gain, full_front_in, full_front_out, front_kept, grad_rows
    )
    grad_features = grad_rows.astype(jnp.bfloat16).reshape(slot_count, frames_dev, width)
    partial_rows = (
        lax.psum_scatter(
            grad_front_gain.astype(jnp.bfloat16), "slots", scatter_dimension=0, tiled=True
        ).astype(jnp.float32),
        lax.psum_scatter(
            grad_front_in.astype(jnp.bfloat16), "slots", scatter_dimension=0, tiled=True
        ).astype(jnp.float32),
        lax.psum_scatter(
            grad_front_out.astype(jnp.bfloat16), "slots", scatter_dimension=0, tiled=True
        ).astype(jnp.float32),
        lax.psum_scatter(
            grad_mixer_gain.astype(jnp.bfloat16), "slots", scatter_dimension=0, tiled=True
        ).astype(jnp.float32),
        lax.psum_scatter(
            grad_query_weight.astype(jnp.bfloat16), "slots", scatter_dimension=0, tiled=True
        ).astype(jnp.float32),
        lax.psum_scatter(
            grad_key_weight.astype(jnp.bfloat16), "slots", scatter_dimension=0, tiled=True
        ).astype(jnp.float32),
        lax.psum_scatter(
            grad_value_weight.astype(jnp.bfloat16), "slots", scatter_dimension=0, tiled=True
        ).astype(jnp.float32),
        lax.psum_scatter(
            grad_output_weight.astype(jnp.bfloat16), "slots", scatter_dimension=0, tiled=True
        ).astype(jnp.float32),
        lax.psum_scatter(
            grad_conv_gain.astype(jnp.bfloat16), "slots", scatter_dimension=0, tiled=True
        ).astype(jnp.float32),
        lax.psum_scatter(
            grad_expand_weight.astype(jnp.bfloat16), "slots", scatter_dimension=0, tiled=True
        ).astype(jnp.float32),
        lax.psum_scatter(
            grad_depth.astype(jnp.bfloat16), "slots", scatter_dimension=0, tiled=True
        ).astype(jnp.float32),
        lax.psum_scatter(
            grad_batch_scale.astype(jnp.bfloat16), "slots", scatter_dimension=0, tiled=True
        ).astype(jnp.float32),
        lax.psum_scatter(
            grad_batch_shift.astype(jnp.bfloat16), "slots", scatter_dimension=0, tiled=True
        ).astype(jnp.float32),
        lax.psum_scatter(
            grad_project.astype(jnp.bfloat16), "slots", scatter_dimension=0, tiled=True
        ).astype(jnp.float32),
        lax.psum_scatter(
            grad_back_gain.astype(jnp.bfloat16), "slots", scatter_dimension=0, tiled=True
        ).astype(jnp.float32),
        lax.psum_scatter(
            grad_back_in.astype(jnp.bfloat16), "slots", scatter_dimension=0, tiled=True
        ).astype(jnp.float32),
        lax.psum_scatter(
            grad_back_out.astype(jnp.bfloat16), "slots", scatter_dimension=0, tiled=True
        ).astype(jnp.float32),
        lax.psum_scatter(
            grad_final.astype(jnp.bfloat16), "slots", scatter_dimension=0, tiled=True
        ).astype(jnp.float32),
    )
    (
        part_front_gain,
        part_front_in,
        part_front_out,
        part_mixer_gain,
        part_query,
        part_key,
        part_value,
        part_output,
        part_conv_gain,
        part_expand,
        part_depth,
        part_batch_gain,
        part_batch_bias,
        part_project,
        part_back_gain,
        part_back_in,
        part_back_out,
        part_final_gain,
    ) = partial_rows
    shards = (
        lax.psum(part_front_gain.astype(jnp.bfloat16), "tm").astype(jnp.float32),
        lax.psum(part_front_in.astype(jnp.bfloat16), "tm").astype(jnp.float32),
        lax.psum(part_front_out.astype(jnp.bfloat16), "tm").astype(jnp.float32),
        lax.psum(part_mixer_gain.astype(jnp.bfloat16), "tm").astype(jnp.float32),
        lax.psum(part_query.astype(jnp.bfloat16), "tm").astype(jnp.float32),
        lax.psum(part_key.astype(jnp.bfloat16), "tm").astype(jnp.float32),
        lax.psum(part_value.astype(jnp.bfloat16), "tm").astype(jnp.float32),
        lax.psum(part_output.astype(jnp.bfloat16), "tm").astype(jnp.float32),
        lax.psum(part_conv_gain.astype(jnp.bfloat16), "tm").astype(jnp.float32),
        lax.psum(part_expand.astype(jnp.bfloat16), "tm").astype(jnp.float32),
        lax.psum(part_depth.astype(jnp.bfloat16), "tm").astype(jnp.float32),
        lax.psum(part_batch_gain.astype(jnp.bfloat16), "tm").astype(jnp.float32),
        lax.psum(part_batch_bias.astype(jnp.bfloat16), "tm").astype(jnp.float32),
        lax.psum(part_project.astype(jnp.bfloat16), "tm").astype(jnp.float32),
        lax.psum(part_back_gain.astype(jnp.bfloat16), "tm").astype(jnp.float32),
        lax.psum(part_back_in.astype(jnp.bfloat16), "tm").astype(jnp.float32),
        lax.psum(part_back_out.astype(jnp.bfloat16), "tm").astype(jnp.float32),
        lax.psum(part_final_gain.astype(jnp.bfloat16), "tm").astype(jnp.float32),
    )
    return (output, grad_features) + tuple(shards)


def solution(mesh):
    in_specs = (
        P("slots", "tm", None),
        P("slots"),
        P("slots", "tm", None),
        P("slots"),
        P("slots", None),
        P("slots", None),
        P("slots"),
        P("slots", None),
        P("slots", None),
        P("slots", None),
        P("slots", None),
        P("slots"),
        P("slots", None),
        P("slots", None),
        P("slots"),
        P("slots"),
        P("slots", None),
        P("slots"),
        P("slots", None),
        P("slots", None),
        P("slots"),
    )
    out_specs = (
        P("slots", "tm", None),
        P("slots", "tm", None),
        P("slots"),
        P("slots", None),
        P("slots", None),
        P("slots"),
        P("slots", None),
        P("slots", None),
        P("slots", None),
        P("slots", None),
        P("slots"),
        P("slots", None),
        P("slots", None),
        P("slots"),
        P("slots"),
        P("slots", None),
        P("slots"),
        P("slots", None),
        P("slots", None),
        P("slots"),
    )
    return jax.shard_map(
        on_device, mesh=mesh, in_specs=in_specs, out_specs=out_specs, check_vma=False
    )
```

```python
import functools
import math

import jax
import jax.numpy as jnp
from jax import lax
from jax.experimental import pallas as pl
from jax.experimental.pallas import tpu as pltpu
from jax.sharding import PartitionSpec as P

HEADS = 8


EPSILON = 1e-05
MESH = pl.DeviceIdType.MESH
KEY_BLOCK = 256
QUERY_BLOCK = 256
MASKED = -1e30
HALO = 16
CORE_PAIRS = [(0, 1), (1, 0), (2, 3), (3, 2)]


def remote(src, dst, send_sem, recv_sem, where):
    return pltpu.make_async_remote_copy(
        src_ref=src,
        dst_ref=dst,
        send_sem=send_sem,
        recv_sem=recv_sem,
        device_id=where,
        device_id_type=MESH,
    )


def stats_kernel(combine, x_ref, o_ref, near, far, mid, send, recv):
    t, s = lax.axis_index("tm"), lax.axis_index("slots")
    n, m = lax.axis_size("tm"), lax.axis_size("slots")
    barrier = pltpu.get_barrier_semaphore()
    slot_places = [{"slots": lax.rem(s + k, m)} for k in range(1, m)]
    tm_places = [{"tm": lax.rem(t + k, n)} for k in range(1, n)]
    for place in slot_places + tm_places:
        pl.semaphore_signal(barrier, inc=1, device_id=place, device_id_type=MESH)
    pl.semaphore_wait(barrier, n + m - 2)

    def share(source, landing, places, first):
        copies = []
        for i, place in enumerate(places):
            copies.append(
                remote(source, landing.at[i], send.at[first + i], recv.at[first + i], place)
            )
            copies[-1].start()
        for copy in copies:
            copy.wait()
        return combine([source[...]] + [landing[i] for i in range(len(places))])

    mid[...] = share(x_ref, near, slot_places, 0)
    o_ref[...] = share(mid, far, tm_places, m - 1)


def add_blocks(blocks):
    total = blocks[0]
    for block in blocks[1:]:
        total = total + block
    return total


def merge_spreads(blocks):
    sums = add_blocks([b[0:1] for b in blocks])
    counts = add_blocks([b[2:3] for b in blocks])
    mean = sums / counts
    squares = add_blocks(
        [b[1:2] + b[2:3] * (b[0:1] / b[2:3] - mean) * (b[0:1] / b[2:3] - mean) for b in blocks]
    )
    return jnp.concatenate((sums, squares, counts, jnp.zeros((5,) + sums.shape[1:], sums.dtype)), 0)


def share_stats(block, combine, collective_id):
    n, m = lax.axis_size("tm"), lax.axis_size("slots")
    return pl.pallas_call(
        functools.partial(stats_kernel, combine),
        out_shape=jax.ShapeDtypeStruct(block.shape, block.dtype),
        in_specs=[pl.BlockSpec(memory_space=pltpu.VMEM)],
        out_specs=pl.BlockSpec(memory_space=pltpu.VMEM),
        scratch_shapes=[
            pltpu.VMEM((m - 1,) + block.shape, block.dtype),
            pltpu.VMEM((n - 1,) + block.shape, block.dtype),
            pltpu.VMEM(block.shape, block.dtype),
            pltpu.SemaphoreType.DMA((n + m - 2,)),
            pltpu.SemaphoreType.DMA((n + m - 2,)),
        ],
        compiler_params=pltpu.CompilerParams(collective_id=collective_id, has_side_effects=True),
        name="share_stats",
    )(block)


FRONT, MIXER, CONV, BATCH, BIAS, BACK, FINAL, TAPS = range(8)


def param(packs, i):
    rows = packs.shape[0] // 4
    return jnp.concatenate([packs[o * rows + i : o * rows + i + 1, :] for o in range(4)], 1)


def frame_count(packs):
    rows = packs.shape[0] // 4
    total = add_blocks([packs[o * rows + rows - 1 : (o + 1) * rows, :] for o in range(4)])
    return jnp.concatenate([total] * 4, 1)


def arrange_kernel(lengths, feat, cot, *refs):
    gains, (taps, feat_out, cot_out, pack, rank, own), scratch = refs[:7], refs[7:13], refs[13:]
    held, load, store = scratch
    n = feat.shape[0]
    core = lax.rem(lax.axis_index("slots"), 2)
    me = lax.axis_index("tm")
    all_lengths = [lengths[u] for u in range(n)]
    length, total = jnp.int32(0), jnp.int32(0)
    loads, stores = [], []
    for u in range(n):
        ahead = jnp.int32(0)
        for v in range(n):
            if v != u:
                before = all_lengths[v] >= all_lengths[u] if v < u else all_lengths[v] > all_lengths[u]
                ahead = ahead + before.astype(jnp.int32)
        place = jnp.where(core == 0, ahead, n - 1 - ahead)
        rank[u] = place
        length = length + jnp.where(place == me, all_lengths[u], 0)
        total = total + all_lengths[u]
        for j, (source, target) in enumerate(((feat, feat_out), (cot, cot_out))):
            loads.append(pltpu.make_async_copy(source.at[u], held.at[j, u], load.at[j, u]))
            stores.append(pltpu.make_async_copy(held.at[j, u], target.at[place], store.at[j, u]))
    own[0] = length
    for copy in loads:
        copy.start()
    width = pack.shape[1]
    count = taps.shape[0]
    pack[...] = jnp.zeros_like(pack)
    for i, gain in enumerate(gains):
        pack[i : i + 1, :] = gain[...].astype(jnp.float32).reshape(1, width)
    pack[TAPS : TAPS + count, :] = taps[...]
    rows = pack.shape[0]
    pack[rows - 2 : rows - 1, :] = jnp.full((1, width), length.astype(jnp.float32))
    pack[rows - 1 : rows, :] = jnp.full((1, width), total.astype(jnp.float32))
    for before, after in zip(loads, stores):
        before.wait()
        after.start()
    for copy in stores:
        copy.wait()


def arrange(lengths, features, cotangent, gains, taps):
    n = features.shape[0]
    rows = -(-(TAPS + taps.shape[0] + 2) // 8) * 8
    smem, vmem, anywhere = pltpu.SMEM, pltpu.VMEM, pl.ANY
    dma = pltpu.SemaphoreType.DMA
    return pl.pallas_call(
        arrange_kernel,
        out_shape=[
            jax.ShapeDtypeStruct(features.shape, features.dtype),
            jax.ShapeDtypeStruct(features.shape, features.dtype),
            jax.ShapeDtypeStruct((rows, taps.shape[1]), jnp.float32),
            jax.ShapeDtypeStruct((n,), jnp.int32),
            jax.ShapeDtypeStruct((1,), jnp.int32),
        ],
        in_specs=[pl.BlockSpec(memory_space=smem)]
        + [pl.BlockSpec(memory_space=anywhere)] * 2
        + [pl.BlockSpec(memory_space=vmem)] * 8,
        out_specs=[pl.BlockSpec(memory_space=x) for x in (anywhere, anywhere, vmem, smem, smem)],
        scratch_shapes=[vmem((2,) + features.shape, features.dtype), dma((2, n)), dma((2, n))],
        name="arrange",
    )(lengths, features, cotangent, *gains, taps)


def permute_kernel(places, x_ref, o_ref, held, load, store):
    n = x_ref.shape[0]
    loads = [pltpu.make_async_copy(x_ref.at[places[i]], held.at[i], load.at[i]) for i in range(n)]
    stores = [pltpu.make_async_copy(held.at[i], o_ref.at[i], store.at[i]) for i in range(n)]
    for copy in loads:
        copy.start()
    for i in range(n):
        loads[i].wait()
        stores[i].start()
    for copy in stores:
        copy.wait()


def take_slots(x, places):
    n = x.shape[0]
    return pl.pallas_call(
        permute_kernel,
        out_shape=jax.ShapeDtypeStruct(x.shape, x.dtype),
        grid_spec=pltpu.PrefetchScalarGridSpec(
            num_scalar_prefetch=1,
            grid=(1,),
            in_specs=[pl.BlockSpec(memory_space=pl.ANY)],
            out_specs=pl.BlockSpec(memory_space=pl.ANY),
            scratch_shapes=[
                pltpu.VMEM(x.shape, x.dtype),
                pltpu.SemaphoreType.DMA((n,)),
                pltpu.SemaphoreType.DMA((n,)),
            ],
        ),
        cost_estimate=pl.CostEstimate(flops=0, bytes_accessed=2 * x.size * 2, transcendentals=0),
        name="take_slots",
    )(places, x)


def split_parts(x):
    high = x.astype(jnp.bfloat16).astype(jnp.float32)
    rest = x - high
    middle = rest.astype(jnp.bfloat16).astype(jnp.float32)
    return high, middle, rest - middle


def dot_nn(a, b):
    return jnp.dot(a, b, preferred_element_type=jnp.float32)


def dot_nt(a, b):
    return lax.dot_general(a, b, (((1,), (1,)), ((), ())), preferred_element_type=jnp.float32)


def fill_bias(table, slope, blocks, span):
    rows = lax.broadcasted_iota(jnp.int32, (KEY_BLOCK, KEY_BLOCK), 0)
    lanes = lax.broadcasted_iota(jnp.int32, (KEY_BLOCK, KEY_BLOCK), 1)
    relative = (rows - lanes + (span - KEY_BLOCK)).astype(jnp.float32)

    def fill(c, carry):
        at = pl.multiple_of(c * KEY_BLOCK, KEY_BLOCK)
        table[:, pl.ds(at, KEY_BLOCK)] = slope * jnp.abs(relative - at.astype(jnp.float32))
        return carry

    lax.fori_loop(span // KEY_BLOCK - blocks, 2 * span // KEY_BLOCK - 1, fill, 0)


def lane_rows(span):
    lane = lax.broadcasted_iota(jnp.int32, (1, 128), 1)
    first = (lane < 64).astype(jnp.float32)
    return (first, 1.0 - first), lax.rem(lane, 64)


def one_hot(place, low, high):
    return ((place >= low) & (place < high)).astype(jnp.float32)


def key_tile(k, sel, place, length):
    row = lax.broadcasted_iota(jnp.int32, (k.shape[0], 1), 0)
    masked = jnp.where(row < length, 0.0, MASKED)
    extra = (1.0 - sel) * (one_hot(place, 1, 4) + masked * one_hot(place, 0, 1))
    return k * sel.astype(jnp.bfloat16) + extra.astype(jnp.bfloat16)


def block_count(length):
    return (length + KEY_BLOCK - 1) // KEY_BLOCK


def head_slope(i, span):
    core = lax.rem(lax.axis_index("slots"), 2)
    slope = jnp.float32(64.0 / span)
    for head in range(1, HEADS):
        slope = jnp.where(core * (HEADS // 2) + i == head, 64.0 * 2.0**-head / span, slope)
    return slope


def attend_kernel(lengths, *refs):
    qkv, (own_att, near_att, own_qa, near_qa) = (refs[0:3], refs[3:6]), refs[6:10]
    table, qa, ka, vt, acc, top = refs[10:]
    span = own_att.shape[0]
    pair = pl.program_id(0)
    sels, place = lane_rows(span)
    counts = [block_count(lengths[u]) for u in range(2)]
    most = jnp.maximum(counts[0], counts[1])
    for h in range(2):
        fill_bias(table.at[h], head_slope(2 * pair + h, span), most, span)
    ones = jnp.ones((16, span), jnp.bfloat16)
    for u in range(2):
        q, k, v = (r[...] for r in qkv[u])
        v_turned = jnp.transpose(v)
        for h in range(2):
            query_extra = (1.0 - sels[h]) * one_hot(place, 0, 1)
            qa[u, h] = q * (sels[h] * 0.125).astype(jnp.bfloat16) + query_extra.astype(jnp.bfloat16)
            ka[u, h] = key_tile(k, sels[h], place, lengths[u])
            vt[u, h, 0:64] = v_turned[64 * h : 64 * h + 64]
            vt[u, h, 64:80] = ones
    acc[...] = jnp.zeros_like(acc)
    top[...] = jnp.full_like(top, -3e38)

    def step(i, carry):
        u = (i >= counts[0]).astype(jnp.int32)
        at = pl.multiple_of((i - u * counts[0]) * KEY_BLOCK, KEY_BLOCK)
        x0 = pl.multiple_of((span - KEY_BLOCK) - at, KEY_BLOCK)
        for h in range(2):
            s = dot_nt(ka[u, h, pl.ds(at, KEY_BLOCK), :], qa[u, h]) - table[h, :, pl.ds(x0, span)]
            old = top[u, h, 0:1]
            new = jnp.maximum(old, jnp.max(s, axis=0, keepdims=True))
            p = jnp.exp(s - new).astype(jnp.bfloat16)
            top[u, h, 0:1] = new
            acc[u, h] = acc[u, h] * jnp.exp(old - new) + dot_nn(
                vt[u, h, :, pl.ds(at, KEY_BLOCK)], p
            )
        return carry

    lax.fori_loop(0, counts[0] + counts[1], step, 0)
    for u, att, qa_out in ((0, own_att, own_qa), (1, near_att, near_qa)):
        attended, extras = [], []
        for h in range(2):
            total = acc[u, h, 64:65, :]
            attended.append((acc[u, h, 0:64, :] / total).astype(jnp.bfloat16))
            parts = split_parts(-(top[u, h, 0:1, :] + jnp.log(total)))
            extras.append(
                jnp.concatenate(
                    (jnp.zeros_like(total),) + parts + (jnp.zeros((60, span), jnp.float32),), 0
                ).astype(jnp.bfloat16)
            )
        att[...] = jnp.transpose(jnp.concatenate(attended, 0))
        query_extra = jnp.transpose(jnp.concatenate((extras[1], extras[0]), 0))
        for h in range(2):
            qa_out[h] = qa[u, h] + query_extra * (1.0 - sels[h]).astype(jnp.bfloat16)


def pair_columns(span, pairs, which):
    return pl.BlockSpec((span, 128), lambda p, *_: (0, which * pairs + p))


def attend(own_qkv, near_qkv, lengths):
    span, columns = own_qkv.shape
    pairs = columns // 384
    cells = span * span * pairs * 2
    table_width = 2 * span - KEY_BLOCK
    columns3 = [pair_columns(span, pairs, i) for i in range(3)]
    tall = pl.BlockSpec((span, 128), lambda p, *_: (0, p))
    heads = pl.BlockSpec((2, span, 128), lambda p, *_: (p, 0, 0))
    return pl.pallas_call(
        attend_kernel,
        out_shape=[jax.ShapeDtypeStruct((span, pairs * 128), jnp.bfloat16)] * 2
        + [jax.ShapeDtypeStruct((2 * pairs, span, 128), jnp.bfloat16)] * 2,
        grid_spec=pltpu.PrefetchScalarGridSpec(
            num_scalar_prefetch=1,
            grid=(pairs,),
            in_specs=columns3 * 2,
            out_specs=[tall, tall, heads, heads],
            scratch_shapes=[
                pltpu.VMEM((2, KEY_BLOCK, table_width), jnp.float32),
                pltpu.VMEM((2, 2, span, 128), jnp.bfloat16),
                pltpu.VMEM((2, 2, span, 128), jnp.bfloat16),
                pltpu.VMEM((2, 2, 80, span), jnp.bfloat16),
                pltpu.VMEM((2, 2, 80, span), jnp.float32),
                pltpu.VMEM((2, 2, 8, span), jnp.float32),
            ],
        ),
        compiler_params=pltpu.CompilerParams(vmem_limit_bytes=56 << 20),
        cost_estimate=pl.CostEstimate(
            flops=cells * 4 * 256, bytes_accessed=span * columns * 8, transcendentals=cells
        ),
        name="attend",
    )(lengths, *([own_qkv] * 3), *([near_qkv] * 3))


def attend_back_kernel(lengths, *refs):
    inputs, outputs = (refs[0:5], refs[5:10]), (refs[10:13], refs[13:16])
    table, qa, ka, va, ga, kt, dqt, dk_out, dv_out = refs[16:]
    span = refs[1].shape[0]
    pair = pl.program_id(0)
    sels, place = lane_rows(span)
    counts = [block_count(lengths[u]) for u in range(2)]
    most = jnp.maximum(counts[0], counts[1])
    for h in range(2):
        fill_bias(table.at[h], head_slope(2 * pair + h, span), most, span)
    side = lax.broadcasted_iota(jnp.int32, (128, 128), 0) < 64
    other = lax.broadcasted_iota(jnp.int32, (128, 128), 1) >= 64
    gather = jnp.where(side == other, 1.0, 0.0).astype(jnp.bfloat16)
    for u in range(2):
        qa_in, k_in, v_in, g_in, att_in = inputs[u]
        k, v, g = k_in[...], v_in[...], g_in[...]
        product = g.astype(jnp.float32) * att_in[...].astype(jnp.float32)
        high = product.astype(jnp.bfloat16)
        low = (product - high.astype(jnp.float32)).astype(jnp.bfloat16)
        delta = split_parts(dot_nn(high, gather) + dot_nn(low, gather))
        grad_extra = sum(
            delta[i].astype(jnp.bfloat16) * one_hot(place, i, i + 1).astype(jnp.bfloat16)
            for i in range(3)
        )
        kt[u] = jnp.transpose(k)
        for h in range(2):
            sel = sels[h].astype(jnp.bfloat16)
            rest = (1.0 - sels[h]).astype(jnp.bfloat16)
            qa[u, h] = qa_in[h]
            ka[u, h] = key_tile(k, sels[h], place, lengths[u])
            va[u, h] = v * sel - ((1.0 - sels[h]) * one_hot(place, 0, 3)).astype(jnp.bfloat16)
            ga[u, h] = g * sel + grad_extra * rest
    dqt[...] = jnp.zeros_like(dqt)
    block_lane = lax.broadcasted_iota(jnp.int32, (KEY_BLOCK, 128), 1)

    def step(i, carry):
        u = (i >= counts[0]).astype(jnp.int32)
        at = pl.multiple_of((i - u * counts[0]) * KEY_BLOCK, KEY_BLOCK)
        keys = pl.ds(at, KEY_BLOCK)
        x0 = pl.multiple_of((span - KEY_BLOCK) - at, KEY_BLOCK)
        dk, dv = [], []
        for h in range(2):
            query_rows, grad_rows = qa[u, h], ga[u, h]
            s = dot_nt(ka[u, h, keys, :], query_rows)
            p = jnp.exp(s - table[h, :, pl.ds(x0, span)])
            d = (p * dot_nt(va[u, h, keys, :], grad_rows)).astype(jnp.bfloat16)
            dv.append(dot_nn(p.astype(jnp.bfloat16), grad_rows))
            dk.append(dot_nn(d, query_rows))
            rows = slice(64 * h, 64 * h + 64)
            dqt[u, rows] += dot_nn(kt[u, rows, keys], d)
        dk_out[u, keys, :] = jnp.where(block_lane < 64, dk[0], dk[1]).astype(jnp.bfloat16)
        dv_out[u, keys, :] = jnp.where(block_lane < 64, dv[0], dv[1]).astype(jnp.bfloat16)
        return carry

    lax.fori_loop(0, counts[0] + counts[1], step, 0)
    for u in range(2):

        def blank(b, carry, u=u):
            keys = pl.ds(pl.multiple_of(b * KEY_BLOCK, KEY_BLOCK), KEY_BLOCK)
            dk_out[u, keys, :] = jnp.zeros((KEY_BLOCK, 128), jnp.bfloat16)
            dv_out[u, keys, :] = jnp.zeros((KEY_BLOCK, 128), jnp.bfloat16)
            return carry

        lax.fori_loop(counts[u], span // KEY_BLOCK, blank, 0)
        dq_ref, dk_ref, dv_ref = outputs[u]
        dk_ref[...] = dk_out[u]
        dv_ref[...] = dv_out[u]
        dq_ref[...] = jnp.transpose((dqt[u] * 0.125).astype(jnp.bfloat16))


def attend_back(own, near, lengths):
    span, columns = own[1].shape
    pairs = columns // 384
    cells = span * span * pairs * 2
    table_width = 2 * span - KEY_BLOCK
    tall = pl.BlockSpec((span, 128), lambda p, *_: (0, p))
    heads = pl.BlockSpec((2, span, 128), lambda p, *_: (p, 0, 0))
    specs = [heads, pair_columns(span, pairs, 1), pair_columns(span, pairs, 2), tall, tall]
    tile = pltpu.VMEM((2, 2, span, 128), jnp.bfloat16)
    grads = pl.pallas_call(
        attend_back_kernel,
        out_shape=[jax.ShapeDtypeStruct((span, pairs * 128), jnp.bfloat16)] * 6,
        grid_spec=pltpu.PrefetchScalarGridSpec(
            num_scalar_prefetch=1,
            grid=(pairs,),
            in_specs=specs * 2,
            out_specs=[tall] * 6,
            scratch_shapes=[
                pltpu.VMEM((2, KEY_BLOCK, table_width), jnp.float32),
                tile,
                tile,
                tile,
                tile,
                pltpu.VMEM((2, 128, span), jnp.bfloat16),
                pltpu.VMEM((2, 128, span), jnp.float32),
                pltpu.VMEM((2, span, 128), jnp.bfloat16),
                pltpu.VMEM((2, span, 128), jnp.bfloat16),
            ],
        ),
        compiler_params=pltpu.CompilerParams(vmem_limit_bytes=56 << 20),
        cost_estimate=pl.CostEstimate(
            flops=cells * 10 * 256, bytes_accessed=span * columns * 16, transcendentals=cells
        ),
        name="attend_back",
    )(
        lengths,
        own[0], own[1], own[1], own[2], own[3],
        near[0], near[1], near[1], near[2], near[3],
    )
    return grads[:3], grads[3:]


CHUNK = 128


def tap_windows(padded, at, taps_count):
    first = HALO - taps_count // 2
    for o in range(8):
        window = padded[pl.ds(at + o, CHUNK + 24), :]
        for start in range(o, first + taps_count, 8):
            if start >= first:
                yield start - first, window[start - o : start - o + CHUNK]


def filter_kernel(taps_count, scalars, gated_ref, packs_ref, out_ref, stats_ref, padded):
    span = gated_ref.shape[0]
    length = scalars[0]
    padded[0:HALO] = jnp.zeros((HALO, 128), jnp.float32)
    padded[HALO + span : HALO + span + HALO] = jnp.zeros((HALO, 128), jnp.float32)
    padded[HALO : HALO + span] = gated_ref[...].astype(jnp.float32)

    def chunk(c, total):
        at = pl.multiple_of(c * CHUNK, CHUNK)
        value = jnp.zeros((CHUNK, 128), jnp.float32)
        for k, window in tap_windows(padded, at, taps_count):
            value = value + window * packs_ref[TAPS + k : TAPS + k + 1, :]
        out_ref[pl.ds(at, CHUNK), :] = value
        row = lax.broadcasted_iota(jnp.int32, (CHUNK, 128), 0) + at
        return total + jnp.sum(jnp.where(row < length, value, 0.0), axis=0, keepdims=True)

    total = lax.fori_loop(0, span // CHUNK, chunk, jnp.zeros((1, 128), jnp.float32))
    mean = total / length.astype(jnp.float32)

    def deviate(c, squares):
        at = pl.multiple_of(c * CHUNK, CHUNK)
        row = lax.broadcasted_iota(jnp.int32, (CHUNK, 128), 0) + at
        off = jnp.where(row < length, out_ref[pl.ds(at, CHUNK), :] - mean, 0.0)
        return squares + jnp.sum(off * off, axis=0, keepdims=True)

    squares = lax.fori_loop(0, span // CHUNK, deviate, jnp.zeros((1, 128), jnp.float32))
    count = jnp.full((1, 128), length.astype(jnp.float32))
    stats_ref[...] = jnp.concatenate((total, squares, count, jnp.zeros((5, 128), jnp.float32)), 0)


def filter_frames(gated, packs, taps_count, lengths):
    span, width = gated.shape
    return pl.pallas_call(
        functools.partial(filter_kernel, taps_count),
        out_shape=[
            jax.ShapeDtypeStruct((span, width), jnp.float32),
            jax.ShapeDtypeStruct((8, width), jnp.float32),
        ],
        grid_spec=pltpu.PrefetchScalarGridSpec(
            num_scalar_prefetch=1,
            grid=(width // 128,),
            in_specs=[
                pl.BlockSpec((span, 128), lambda c, *_: (0, c)),
                pl.BlockSpec((packs.shape[0] // 4, 128), lambda c, *_: (c, 0)),
            ],
            out_specs=[
                pl.BlockSpec((span, 128), lambda c, *_: (0, c)),
                pl.BlockSpec((8, 128), lambda c, *_: (0, c)),
            ],
            scratch_shapes=[pltpu.VMEM((span + 2 * HALO, 128), jnp.float32)],
        ),
        cost_estimate=pl.CostEstimate(
            flops=64 * span * width, bytes_accessed=6 * span * width, transcendentals=0
        ),
        name="filter_frames",
    )(lengths, gated, packs)


def filter_turned(taps_count, padded, packs, first, out_ref, cut):
    span = out_ref.shape[0]

    def chunk(c, carry):
        at = pl.multiple_of(c * CHUNK, CHUNK)
        value = jnp.zeros((CHUNK, 128), jnp.float32)
        for k, window in tap_windows(padded, at, taps_count):
            turned = first + taps_count - 1 - k
            value = value + window * packs[turned : turned + 1, :]
        out_ref[pl.ds(at, CHUNK), cut] = value.astype(jnp.bfloat16)
        return carry

    lax.fori_loop(0, span // CHUNK, chunk, 0)


def filter_taps(taps_count, span, padded, gpadded, held):
    def tally(c, sums):
        at = pl.multiple_of(c * CHUNK, CHUNK)
        grad = padded[pl.ds(at + HALO, CHUNK), :]
        added = list(sums)
        for k, window in tap_windows(gpadded, at, taps_count):
            term = grad * window
            folded = term[0:8]
            for r in range(8, CHUNK, 8):
                folded = folded + term[r : r + 8]
            added[k] = added[k] + folded
        return tuple(added)

    blank = tuple(jnp.zeros((8, 128), jnp.float32) for _ in range(taps_count))
    sums = lax.fori_loop(0, span // CHUNK, tally, blank)
    rest = jnp.zeros((held - taps_count, 128), jnp.float32)
    return jnp.concatenate([column_sum(x) for x in sums] + [rest], 0)


def dot_tn(a, b):
    return lax.dot_general(a, b, (((0,), (0,)), ((), ())), preferred_element_type=jnp.float32)


def sigmoid(x):
    return 0.5 * jnp.tanh(0.5 * x) + 0.5


def silu_parts(x):
    s = sigmoid(x)
    value = x * s
    return value, s + value * (1.0 - s)


def normed_parts(x):
    centred = x - jnp.mean(x, -1, keepdims=True)
    scale = lax.rsqrt(jnp.mean(centred * centred, -1, keepdims=True) + EPSILON)
    return centred * scale, scale


def normed_back(n, scale, e):
    return scale * (e - jnp.mean(e, -1, keepdims=True) - n * jnp.mean(e * n, -1, keepdims=True))


def column_sum(x):
    return jnp.sum(x, axis=0, keepdims=True)


def add_rows(ref, rows):
    @pl.when(pl.program_id(0) == 0)
    def _():
        ref[...] = jnp.zeros_like(ref)

    width = ref.shape[1]
    ref[...] += jnp.concatenate(list(rows) + [jnp.zeros((8 - len(rows), width), jnp.float32)], 0)


def row_call(kernel, name, scalars, tall, whole, outs, sums, block, flops):
    span = tall[0].shape[0]

    def rows(columns):
        return pl.BlockSpec((block, columns), lambda i, *_: (i, 0))

    def kept(x, at):
        return pl.BlockSpec(x.shape, lambda i, *_: (0, at), pipeline_mode=pl.Buffered(1))

    cuts = [x if isinstance(x, tuple) else (x, x.shape[1], 0) for x in whole]
    specs = [kept(jax.ShapeDtypeStruct((x.shape[0], w), x.dtype), at) for x, w, at in cuts]
    whole = [x for x, _, _ in cuts]
    width = tall[0].shape[1]
    moved = sum(x.size * x.dtype.itemsize for x in tall + whole)
    moved += sum(span * c * jnp.dtype(d).itemsize for c, d in outs)
    return pl.pallas_call(
        kernel,
        out_shape=[jax.ShapeDtypeStruct((span, c), d) for c, d in outs]
        + [jax.ShapeDtypeStruct((8, width), jnp.float32)] * sums,
        grid_spec=pltpu.PrefetchScalarGridSpec(
            num_scalar_prefetch=1,
            grid=(span // block,),
            in_specs=[rows(x.shape[1]) for x in tall] + specs,
            out_specs=[rows(c) for c, _ in outs]
            + [pl.BlockSpec((8, width), lambda i, *_: (0, 0))] * sums,
        ),
        compiler_params=pltpu.CompilerParams(vmem_limit_bytes=60 << 20),
        cost_estimate=pl.CostEstimate(
            flops=flops * span, bytes_accessed=moved, transcendentals=span * 2048
        ),
        name=name,
    )(scalars, *tall, *whole)


def head_columns(ref, which, width):
    return ref[:, pl.ds(pl.multiple_of(which * width, width), width)]


def head_rows(ref, which, width):
    return ref[pl.ds(pl.multiple_of(which * width, width), width), :]


def expand_kernel(
    scalars, own_ref, far_ref, after_ref, packs, w_output, w_expand,
    after_out, normed_out, gated_out, slope_out,
):
    core, length = lax.rem(lax.axis_index("slots"), 2), scalars[0]
    block, half = own_ref.shape
    after = (
        after_ref[...]
        + dot_nn(own_ref[...], head_rows(w_output, core, half))
        + dot_nn(far_ref[...], head_rows(w_output, 1 - core, half))
    )
    after_out[...] = after
    n, _ = normed_parts(after)
    normed = (n * param(packs, CONV)).astype(jnp.bfloat16)
    normed_out[...] = normed
    expand = dot_nn(normed, w_expand[...])
    width = expand.shape[1] // 2
    row = lax.broadcasted_iota(jnp.int32, (block, width), 0) + pl.program_id(0) * block
    gate = sigmoid(expand[:, width:])
    live = jnp.where(row < length, gate, 0.0)
    gated = expand[:, :width] * live
    gated_out[...] = gated.astype(jnp.bfloat16)
    slope_out[:, :width] = live.astype(jnp.bfloat16)
    slope_out[:, width:] = (gated * (1.0 - gate)).astype(jnp.bfloat16)


def spread_parts(shared, packs):
    frames = frame_count(packs)
    return shared[0:1, :] / frames, lax.rsqrt(shared[1:2, :] / frames + EPSILON)


def back_kernel(
    scalars, filtered_ref, after_ref, cot_ref, shared, packs, w_project, w_in, w_out,
    output_out, grad_out, dbn_out, swish_out, top_out, hidden_out, dpre_out, normed_out, half_out,
    sums,
):
    middle, inverse = spread_parts(shared, packs)
    back_gain, final_gain = param(packs, BACK), param(packs, FINAL)
    unit = (filtered_ref[...] - middle) * inverse
    value, slope_bn = silu_parts(unit * param(packs, BATCH) + param(packs, BIAS))
    swish = value.astype(jnp.bfloat16)
    swish_out[...] = swish
    after_conv = after_ref[...] + dot_nn(swish, w_project[...])
    n1, r1 = normed_parts(after_conv)
    normed = (n1 * back_gain).astype(jnp.bfloat16)
    normed_out[...] = normed
    value, slope = silu_parts(dot_nn(normed, w_in[...]))
    hidden = value.astype(jnp.bfloat16)
    hidden_out[...] = hidden
    n2, r2 = normed_parts(after_conv + 0.5 * dot_nn(hidden, w_out[...]))
    output_out[...] = (n2 * final_gain).astype(jnp.bfloat16)

    cot = cot_ref[...].astype(jnp.float32)
    grad = normed_back(n2, r2, cot * final_gain)
    half_grad = (0.5 * grad).astype(jnp.bfloat16)
    half_out[...] = half_grad
    dpre = (dot_nt(half_grad, w_out[...]) * slope).astype(jnp.bfloat16)
    dpre_out[...] = dpre
    dnormed = dot_nt(dpre, w_in[...])
    grad = grad + normed_back(n1, r1, dnormed * back_gain)
    grad_out[...] = grad
    top = grad.astype(jnp.bfloat16)
    top_out[...] = top
    dbn = dot_nt(top, w_project[...]) * slope_bn
    dbn_out[...] = dbn
    add_rows(
        sums,
        [column_sum(dbn), column_sum(dbn * unit), column_sum(cot * n2), column_sum(dnormed * n1)],
    )


CORE_PACE, PAIR_PACE = 1.5, 25.0
HOP = 3.0
CHUNK_BUFFERS = 8
DIRECT_FROM = 4
STAGES = 8


def chunk_scratch(chunks):
    dma = pltpu.SemaphoreType.DMA
    scratch = []
    for r, w, kind, direct in chunks:
        shapes = [(2, r, w), (2, r, w), (2, r, w), (r, w), (r // 2, w), (r // 4, w), (r // 8, w), (r, w)]
        if direct:
            shapes[4:7] = [(7, r // 8, w), (8, w), (8, w)]
        scratch += [pltpu.VMEM(shape, kind) for shape in shapes]
    n = len(chunks)
    return scratch + [dma((n, STAGES + 14)), dma((n, STAGES + 14))]


class Flow:
    def __init__(self, chunks, refs, finish, stages=None):
        count = len(chunks)
        self.stages = stages or [4 if chunk[3] else STAGES for chunk in chunks]
        self.others = [{"tm": lax.rem(lax.axis_index("tm") + k, 8)} for k in range(1, 8)]
        self.chunks, self.finish = chunks, finish
        self.buffers = [refs[CHUNK_BUFFERS * c : CHUNK_BUFFERS * (c + 1)] for c in range(count)]
        self.send_sems, self.recv_sems = refs[CHUNK_BUFFERS * count :]
        me, n = lax.axis_index("tm"), lax.axis_size("tm")
        s = lax.axis_index("slots")
        self.core, self.y = lax.rem(s, 2), lax.div(s, 2)
        self.x, self.z = lax.rem(me, 2), lax.div(me, 2)
        self.sibling, self.across = {"slots": s + 1 - 2 * self.core}, {"slots": lax.rem(s + 2, 4)}
        self.beside = {"tm": me + 1 - 2 * self.x}
        self.low, self.high = lax.rem(self.z, 2), lax.div(self.z, 2)
        self.next, self.beyond = {"tm": me + 2 - 4 * self.low}, {"tm": me + 4 - 8 * self.high}
        self.sent = []
        self.going = {}
        self.clock, self.waiting, self.busy = 0.0, [], {}

    def put(self, c, y, even, odd):
        send, total = self.buffers[c][0], self.buffers[c][1]
        total[y] = jnp.where(self.core == 0, even, odd)
        send[y] = jnp.where(self.core == 0, odd, even)

    def put_all(self, c, terms):
        for y in range(2):
            self.put(c, y, terms[2 * y], terms[2 * y + 1])

    def stage(self, c, k):
        send, total, core_in, y_in, x_in, low_in, high_in, final = self.buffers[c]
        r, _, kind, direct = self.chunks[c]
        x, y, low, high = self.x, self.y, self.low, self.high
        me = lax.axis_index("tm")

        def add(ref, place, arrived):
            value = ref[place].astype(jnp.float32) + arrived.astype(jnp.float32)
            return value.astype(kind)

        def part(start, rows):
            return pl.ds(pl.multiple_of(start, rows), rows)

        half, quarter, piece = r // 2, r // 4, r // 8
        at_half = x * half
        at_quarter = at_half + low * quarter
        at_piece = at_quarter + high * piece
        if k:
            for copy in self.going[c]:
                copy.wait_recv()
        if k == 0:
            copy = (send, core_in, self.sibling)
        elif k == 1:
            for i in range(2):
                total[i] = add(total, i, core_in[i])
            copy = (total.at[1 - y], y_in, self.across)
        elif k == 2:
            total[y] = add(total, y, y_in[...])
            copy = (total.at[y, part((1 - x) * half, half)], x_in, self.beside)
        elif direct and k == 3:
            mine = part(me * piece, piece)
            value = total[y, mine].astype(jnp.float32)
            for i in range(7):
                value = value + x_in[i].astype(jnp.float32)
            final[mine] = value.astype(kind)
        elif direct:
            pass
        elif k == 3:
            mine = (y, part(at_half, half))
            total[mine] = add(total, mine, x_in[...])
            copy = (total.at[y, part(at_half + (1 - low) * quarter, quarter)], low_in, self.next)
        elif k == 4:
            mine = (y, part(at_quarter, quarter))
            total[mine] = add(total, mine, low_in[...])
            copy = (total.at[y, part(at_quarter + (1 - high) * piece, piece)], high_in, self.beyond)
        elif k == 5:
            mine = part(at_piece, piece)
            final[mine] = add(total, (y, mine), high_in[...])
            copy = (final.at[mine], final.at[mine], self.beyond)
        elif k == 6:
            mine = part(at_quarter, quarter)
            copy = (final.at[mine], final.at[mine], self.next)
        elif k == 7:
            mine = part(at_half, half)
            copy = (final.at[mine], final.at[mine], self.beside)
        if k == self.stages[c]:
            return
        if direct and k >= 2:
            copies, first = [], STAGES + 7 * (k - 2)
            for i, where in enumerate(self.others):
                if k == 2:
                    source, target = total.at[y, part(lax.rem(me + i + 1, 8) * piece, piece)], x_in.at[i]
                else:
                    source = target = final.at[part(me * piece, piece)]
                sems = self.send_sems.at[c, first + i], self.recv_sems.at[c, first + i]
                copies.append(remote(source, target, *sems, where))
        else:
            source, target, where = copy
            copies = [remote(source, target, self.send_sems.at[c, k], self.recv_sems.at[c, k], where)]
        for copy in copies:
            copy.start()
        self.sent += copies
        self.going[c] = copies

    def occupy(self, link, time):
        self.busy[link] = max(self.busy.get(link, 0.0), self.clock) + time
        return self.busy[link] + HOP

    def step(self, c, k):
        self.stage(c, k)
        r, w, kind, direct = self.chunks[c]
        size = r * w * jnp.dtype(kind).itemsize / 1e6
        half, quarter, piece = (size / cut * PAIR_PACE for cut in (2, 4, 8))
        pace = (
            ("core", 2 * size * CORE_PACE), ("y", size * PAIR_PACE), ("x", half), ("z", quarter),
            ("z", 2 * piece), ("z", 2 * piece), ("z", quarter), ("x", half),
        )
        if direct:
            pace = pace[:2] + (("z", size * PAIR_PACE),) * 2
        if k < self.stages[c]:
            self.waiting.append((self.occupy(*pace[k]), c, k + 1))
        else:
            self.finish(c, self.buffers[c])
        self.clock += size

    def begin(self, c):
        self.step(c, 0)

    def spend(self, time):
        self.clock += time
        while self.waiting and min(self.waiting)[0] <= self.clock:
            first = min(self.waiting)
            self.waiting.remove(first)
            self.step(*first[1:])

    def drain(self):
        while self.waiting:
            self.spend(max(min(self.waiting)[0] - self.clock, 0.0))
        for copy in self.sent:
            copy.wait_send()


def greet(places):
    barrier = pltpu.get_barrier_semaphore()
    for place in places:
        pl.semaphore_signal(barrier, inc=1, device_id=place, device_id_type=MESH)
    pl.semaphore_wait(barrier, len(places))


class Named:
    def __init__(self, names, refs):
        self.__dict__.update(zip(names, refs))


def named_call(kernel, name, inputs, outputs, scratch, extra, collective_id, flops):
    names = [*inputs, *outputs, *scratch]

    def body(*refs):
        kernel(Named(names, refs), refs[len(names) :])

    results = pl.pallas_call(
        body,
        out_shape=[jax.ShapeDtypeStruct(shape, kind) for shape, kind, _ in outputs.values()],
        in_specs=[pl.BlockSpec(memory_space=space) for _, space in inputs.values()],
        out_specs=[pl.BlockSpec(memory_space=space) for _, _, space in outputs.values()],
        scratch_shapes=[*scratch.values(), *extra],
        compiler_params=pltpu.CompilerParams(
            collective_id=collective_id,
            has_side_effects=collective_id is not None,
            vmem_limit_bytes=62 << 20,
        ),
        cost_estimate=pl.CostEstimate(
            flops=flops, bytes_accessed=sum(2 * x.size for x, _ in inputs.values()), transcendentals=0
        ),
        name=name,
    )(*(x for x, _ in inputs.values()))
    return Named(outputs, results)


class Stream:
    def __init__(self, sources, slots, semaphores, blocks):
        self.copies = [
            [
                pltpu.make_async_copy(ref.at[block], held.at[i % 2], semaphores.at[i % 2, j])
                for j, (ref, held) in enumerate(zip(sources, slots))
            ]
            for i, block in enumerate(blocks)
        ]

    def begin(self, i):
        if i < len(self.copies):
            for copy in self.copies[i]:
                copy.start()

    def take(self, i):
        self.begin(i + 1)
        for copy in self.copies[i]:
            copy.wait()


WEIGHTS = ("pack", "w_in", "w_out", "w_query", "w_key", "w_value")
PAIR_ORDER = (0, 1, 3, 2)


def opening_kernel(r, _):
    me, n = lax.axis_index("tm"), lax.axis_size("tm")
    s = lax.axis_index("slots")
    core, x, z = lax.rem(s, 2), lax.rem(me, 2), lax.div(me, 2)
    sibling, across = {"slots": s + 1 - 2 * core}, {"slots": lax.rem(s + 2, 4)}
    theirs, beside = lax.rem(s + 2, 4), {"tm": me + 1 - 2 * x}
    frames = r.feats.shape[1]
    span, width = r.x.shape
    half = width // 2
    shards = [getattr(r, name) for name in WEIGHTS]
    fulls = [getattr(r, "full_" + name) for name in WEIGHTS]
    greet([{"tm": lax.rem(me + k, n)} for k in range(1, n)] + [sibling, across])

    def part(i, owner, piece=None):
        rows = shards[i].shape[0]
        if piece is None:
            return fulls[i].at[pl.ds(pl.multiple_of(owner * rows, rows), rows)]
        size = rows // 2
        return fulls[i].at[pl.ds(pl.multiple_of(owner * rows + piece * size, size), size)]

    def link(kind, i, source, target, where):
        copy = remote(source, target, r.w_send.at[i, kind], r.w_recv.at[i, kind], where)
        copy.start()
        return copy

    count = len(WEIGHTS)
    y_copies, c_copies, b_copies, f_copies, g_copies, locals_ = [], [], {}, [], {}, []
    for i in range(count):
        if i == 0:
            y_copies.append(link(0, i, shards[i], part(i, s), across))
        else:
            size = shards[i].shape[0] // 2
            source = shards[i].at[pl.ds(pl.multiple_of(x * size, size), size)]
            y_copies.append(link(0, i, source, part(i, s, x), across))
    rows_copies = {}
    for k in PAIR_ORDER:
        for j in range(2):
            to = 2 * lax.rem(z + 4 - k, 4) + lax.rem(x + j, 2)
            target = r.x.at[pl.ds(pl.multiple_of(me * frames, frames), frames)]
            sems = r.x_send.at[2 * k + j], r.x_recv.at[2 * k + j]
            if k == 0 and j == 0:
                copy = pltpu.make_async_copy(r.feats.at[me], target, sems[0])
            else:
                copy = remote(r.feats.at[to], target, *sems, {"tm": to})
            copy.start()
            rows_copies[k, j] = copy
    for i in range(count):
        c_copies.append(link(1, i, shards[i], part(i, s), sibling))
        locals_.append(pltpu.make_async_copy(shards[i], part(i, s), r.w_local.at[i]))
        locals_[-1].start()
    for i in range(count):
        y_copies[i].wait_recv()
        piece = None if i == 0 else x
        block = part(i, theirs, piece)
        if i:
            b_copies[i] = link(2, i, block, block, beside)
        f_copies.append(link(3, i, block, block, sibling))

    def complete(i):
        if i:
            b_copies[i].wait_recv()
            block = part(i, theirs, 1 - x)
            g_copies[i] = link(4, i, block, block, sibling)
        c_copies[i].wait_recv()
        f_copies[i].wait_recv()
        locals_[i].wait()

    def received(i):
        if i:
            g_copies[i].wait_recv()
        store = pltpu.make_async_copy(fulls[i], getattr(r, "out_" + WEIGHTS[i]), r.w_local.at[i])
        store.start()
        stores.append(store)

    stores, outgoing, block_stores = [], [], []
    for i in range(3):
        complete(i)
    for i in range(3):
        received(i)
    packs, w_in, w_out, wq, wk, wv = fulls
    for step, k in enumerate(PAIR_ORDER):
        for j in range(2):
            copy = rows_copies[k, j]
            if k == 0 and j == 0:
                copy.wait()
            else:
                copy.wait_recv()
        slot = step % 2
        place = pl.ds(pl.multiple_of(lax.rem(z + k, 4) * 2 * frames, 2 * frames), 2 * frames)
        if step >= 2:
            for copy in block_stores[step - 2]:
                copy.wait()
        rows = r.x[place].astype(jnp.float32)
        normed, _ = normed_parts(rows)
        normed = (normed * param(packs, FRONT)).astype(jnp.bfloat16)
        r.slot_normed[slot] = normed
        value, slope = silu_parts(dot_nn(normed, w_in[...]))
        hidden = value.astype(jnp.bfloat16)
        r.slot_hidden[slot] = hidden
        r.slot_slope[slot] = slope.astype(jnp.bfloat16)
        after = rows + 0.5 * dot_nn(hidden, w_out[...])
        r.slot_after[slot] = after
        mixer, _ = normed_parts(after)
        mixer = (mixer * param(packs, MIXER)).astype(jnp.bfloat16)
        r.slot_mixer[slot] = mixer
        if step == 0:
            for i in range(3, count):
                complete(i)
            for i in range(3, count):
                received(i)
        for j, w in enumerate((wq, wk, wv)):
            lanes = slice(j * half, (j + 1) * half)
            r.far[place, lanes] = dot_nn(mixer, head_columns(w, 1 - core, half)).astype(jnp.bfloat16)
        outgoing.append(
            remote(
                r.far.at[place], r.near_qkv.at[place], r.far_send.at[step], r.far_recv.at[step],
                sibling,
            )
        )
        outgoing[-1].start()
        for j, w in enumerate((wq, wk, wv)):
            lanes = slice(j * half, (j + 1) * half)
            r.slot_own[slot, :, lanes] = dot_nn(mixer, head_columns(w, core, half)).astype(jnp.bfloat16)
        block_stores.append([
            pltpu.make_async_copy(source, target.at[place], r.store.at[slot, j])
            for j, (source, target) in enumerate((
                (r.x.at[place], r.rows),
                (r.slot_normed.at[slot], r.normed),
                (r.slot_hidden.at[slot], r.hidden),
                (r.slot_slope.at[slot], r.slope),
                (r.slot_after.at[slot], r.after),
                (r.slot_mixer.at[slot], r.mixer),
                (r.slot_own.at[slot], r.own_qkv),
            ))
        ])
        for copy in block_stores[-1]:
            copy.start()
    for copy in outgoing + stores + block_stores[-2] + block_stores[-1]:
        copy.wait()
    for copy in [*y_copies, *c_copies, *f_copies, *b_copies.values(), *g_copies.values()]:
        copy.wait_send()
    for place, copy in rows_copies.items():
        if place != (0, 0):
            copy.wait_send()


def opening(feats, shards, collective_id):
    bf16, f32 = jnp.bfloat16, jnp.float32
    anywhere, vmem = pl.ANY, pltpu.VMEM
    dma = pltpu.SemaphoreType.DMA
    n, frames, width = feats.shape
    span, pair = n * frames, 2 * frames
    ff = shards["w_in"].shape[1]
    half = width // 2
    inputs = {"feats": (feats, anywhere)}
    inputs |= {name: (shards[name], vmem) for name in WEIGHTS}
    whole = {name: (4 * shards[name].shape[0], shards[name].shape[1]) for name in WEIGHTS}
    tall = dict(normed=(width, bf16), hidden=(ff, bf16), slope=(ff, bf16), after=(width, f32))
    tall |= dict(mixer=(width, bf16), own_qkv=(3 * half, bf16))
    outputs = {"rows": ((span, width), bf16, anywhere), "near_qkv": ((span, 3 * half), bf16, anywhere)}
    outputs |= {name: ((span, columns), kind, anywhere) for name, (columns, kind) in tall.items()}
    outputs |= {"out_" + name: (whole[name], shards[name].dtype, anywhere) for name in WEIGHTS}
    scratch = {"full_" + name: vmem(whole[name], shards[name].dtype) for name in WEIGHTS}
    scratch |= {
        "slot_" + name.split("_")[0]: vmem((2, pair, columns), kind)
        for name, (columns, kind) in tall.items()
    }
    count = len(WEIGHTS)
    scratch |= {
        "x": vmem((span, width), bf16),
        "far": vmem((span, 3 * half), bf16),
        "w_send": dma((count, 5)),
        "w_recv": dma((count, 5)),
        "w_local": dma((count,)),
        "x_send": dma((n,)),
        "x_recv": dma((n,)),
        "far_send": dma((4,)),
        "far_recv": dma((4,)),
        "store": dma((2, 7)),
    }
    return named_call(
        opening_kernel, "opening", inputs, outputs, scratch, [], collective_id,
        span * (4 * width * ff + 6 * width * width),
    )


ROWS = 256


def middle_kernel(chunks, taps_count, r, flow_refs):
    t, s = lax.axis_index("tm"), lax.axis_index("slots")
    n, m = lax.axis_size("tm"), lax.axis_size("slots")
    span, width = r.half.shape
    shard = width // 4
    quarter, half = r.hidden.shape[1] // 4, width // 2
    back_chunks = len(chunks) - 3
    length = r.length[0]
    core = lax.rem(s, 2)
    others = pltpu.make_async_copy(r.others, r.held_others, r.load.at[6])
    others.start()
    wanted = ("half", "hidden", "normed", "dpre", "swish", "top")
    loads = {
        name: pltpu.make_async_copy(getattr(r, name), getattr(r, "held_" + name), r.load.at[i])
        for i, name in enumerate(wanted)
    }
    for load in loads.values():
        load.start()
    everything = slice(None)
    columns = Stream(
        [r.filtered, r.dbn, r.gated],
        [r.filtered_slots, r.dbn_slots, r.gated_slots],
        r.column_load,
        [(everything, slice(128 * c, 128 * c + 128)) for c in range(width // 128)],
    )
    rows = Stream(
        [r.glu_slope, r.grad, r.after],
        [r.slope_slots, r.grad_slots, r.after_slots],
        r.row_load,
        [(slice(i * ROWS, (i + 1) * ROWS), everything) for i in range(span // ROWS)],
    )
    columns.begin(0)
    rows.begin(0)

    slot_places = [{"slots": lax.rem(s + k, m)} for k in range(1, m)]
    tm_places = [{"tm": lax.rem(t + k, n)} for k in range(1, n)]
    greet(slot_places + tm_places)

    def share(source, landing, places, first):
        copies = [
            remote(source, landing.at[i], r.stat_send.at[first + i], r.stat_recv.at[first + i], place)
            for i, place in enumerate(places)
        ]
        for copy in copies:
            copy.start()
        return copies

    def gathered(copies, source, landing):
        for copy in copies:
            copy.wait()
        return add_blocks([source[...]] + [landing[i] for i in range(len(copies))])

    held = {}

    def need(name):
        if name not in held:
            loads[name].wait()
            held[name] = getattr(r, "held_" + name)
        return held[name]

    def finish(c, buffers):
        if c >= back_chunks:
            cut = slice((c - back_chunks) * shard, (c - back_chunks + 1) * shard)
            r.part_middle[cut] = buffers[1][flow.y]
            return
        value = buffers[-1][...].astype(jnp.float32)
        if c < 2:
            rows_here = chunks[0][0]
            r.part_out[c * rows_here : (c + 1) * rows_here] = value
        elif c < back_chunks - 1:
            r.part_in[:, (c - 2) * width : (c - 1) * width] = value
        else:
            r.part_project[...] = value

    flow = Flow(chunks, flow_refs, finish, [STAGES] * back_chunks + [2] * (len(chunks) - back_chunks))

    def make(c):
        if c < 2:
            a, b = need("hidden"), need("half")
            rows_here = chunks[0][0]
            terms = []
            for o in range(4):
                at = o * quarter + c * rows_here
                terms.append(dot_tn(a[:, at : at + rows_here], b[...]).astype(jnp.bfloat16))
        elif c < back_chunks - 1:
            b = need("dpre")[:, (c - 2) * width : (c - 1) * width]
            terms = dot_tn(need("normed")[...], b).astype(jnp.bfloat16).reshape(4, shard, width)
        else:
            terms = dot_tn(need("swish")[...], need("top")[...]).astype(jnp.bfloat16)
            terms = terms.reshape(4, shard, width)
        flow.put_all(c, terms)
        flow.begin(c)
        flow.spend(2.6 if c < 2 else 1.4)

    first = share(r.sums_in, r.stat_near, slot_places, 0)
    make(0)
    r.stat_mid[...] = gathered(first, r.sums_in, r.stat_near)
    second = share(r.stat_mid, r.stat_far, tm_places, m - 1)
    make(1)
    make(2)
    r.sums_out[...] = gathered(second, r.stat_mid, r.stat_far)
    for c in range(3, back_chunks):
        make(c)
    later = [
        pltpu.make_async_copy(source, target, r.load.at[i])
        for i, (source, target) in enumerate((
            (r.conv_normed, r.held_normed),
            (r.own_att, r.held_half.at[:, 0:half]),
            (r.far_att, r.held_half.at[:, half:width]),
        ))
    ]
    for copy in later:
        copy.start()

    means, inverses = spread_parts(r.shared, r.packs)
    batch_gain, conv_gain, frames = param(r.packs, BATCH), param(r.packs, CONV), frame_count(r.packs)
    pack_rows = r.packs.shape[0] // 4
    halo = jnp.zeros((HALO, 128), jnp.float32)
    for ref in (r.padded, r.gpadded):
        ref[0:HALO] = halo
        ref[HALO + span : HALO + span + HALO] = halo
    for c in range(width // 128):
        columns.take(c)
        cut = slice(128 * c, 128 * c + 128)
        middle, inverse, gain = means[:, cut], inverses[:, cut], batch_gain[:, cut]
        shift_sum, scale_sum = r.sums_out[0:1, cut], r.sums_out[1:2, cut]
        r.gpadded[HALO : HALO + span] = r.gated_slots[c % 2].astype(jnp.float32)
        row = lax.broadcasted_iota(jnp.int32, (span, 128), 0)
        unit = (r.filtered_slots[c % 2] - middle) * inverse
        shift = (gain * shift_sum + unit * (gain * scale_sum)) / frames[:, cut]
        r.padded[HALO : HALO + span] = inverse * (
            r.dbn_slots[c % 2] * gain - jnp.where(row < length, shift, 0.0)
        )
        filter_turned(taps_count, r.padded, r.packs, c * pack_rows + TAPS, r.held_swish, cut)
        flow.spend(2.3)
        r.grad_taps[:, cut] = filter_taps(taps_count, span, r.padded, r.gpadded, r.grad_taps.shape[0])
        flow.spend(2.7)

    others.wait()
    w_expand = r.held_others.at[:, 0 : 2 * width]
    w_output = r.held_others.at[:, 2 * width : 3 * width]
    conv_sum = jnp.zeros((1, width), jnp.float32)
    outgoing, stores = [], []
    for i in range(span // ROWS):
        rows.take(i)
        cut = slice(i * ROWS, (i + 1) * ROWS)
        if i >= 2:
            for copy in stores[i - 2]:
                copy.wait()
        dgated = r.held_swish[cut].astype(jnp.float32)
        slopes = r.slope_slots[i % 2].astype(jnp.float32)
        dexpand = jnp.concatenate((dgated * slopes[:, :width], dgated * slopes[:, width:]), 1)
        dexpand = dexpand.astype(jnp.bfloat16)
        r.held_dpre[cut, 0 : 2 * width] = dexpand
        dnormed = dot_nt(dexpand, w_expand[...])
        normed, scale = normed_parts(r.after_slots[i % 2])
        grad = r.grad_slots[i % 2] + normed_back(normed, scale, dnormed * conv_gain)
        r.grad_store[i % 2] = grad
        top = grad.astype(jnp.bfloat16)
        r.held_top[cut] = top
        r.far_rows[cut] = dot_nt(top, head_rows(w_output, 1 - core, half)).astype(jnp.bfloat16)
        outgoing.append(
            remote(
                r.far_rows.at[cut], r.near_grad.at[cut], r.far_send.at[i], r.far_recv.at[i],
                flow.sibling,
            )
        )
        outgoing[-1].start()
        r.own_slots[i % 2] = dot_nt(top, head_rows(w_output, core, half)).astype(jnp.bfloat16)
        conv_sum = conv_sum + column_sum(dnormed * normed)
        stores.append([
            pltpu.make_async_copy(source.at[i % 2], target.at[cut], r.store.at[i % 2, j])
            for j, (source, target) in enumerate((
                (r.grad_store, r.grad_out),
                (r.own_slots, r.own_grad),
            ))
        ])
        for copy in stores[-1]:
            copy.start()
        flow.spend(2.0)
    r.conv_sums[...] = jnp.concatenate((conv_sum, jnp.zeros((7, width), jnp.float32)), 0)
    for copy in later:
        copy.wait()
    for j in range(2):
        b = r.held_dpre[:, j * width : (j + 1) * width]
        terms = dot_tn(r.held_normed[...], b).astype(jnp.bfloat16).reshape(4, shard, width)
        flow.put_all(back_chunks + j, terms)
        flow.begin(back_chunks + j)
        flow.spend(1.6)
    for which, lanes in ((core, slice(0, half)), (1 - core, slice(half, width))):
        terms = dot_tn(r.held_half[:, lanes], r.held_top[...]).astype(jnp.bfloat16)
        flow.put(back_chunks + 2, which, terms[:shard], terms[shard:])
    flow.begin(back_chunks + 2)
    flow.drain()
    for copy in outgoing + [copy for group in stores[-2:] for copy in group]:
        copy.wait()


def middle(lengths, sums, shared, packs, taps_count, big, collective_id):
    bf16, f32 = jnp.bfloat16, jnp.float32
    anywhere, vmem = pl.ANY, pltpu.VMEM
    span, width = big["half"].shape
    ff = big["hidden"].shape[1]
    shard, quarter, half = width // 4, ff // 4, width // 2
    n, m = lax.axis_size("tm"), lax.axis_size("slots")
    dma = pltpu.SemaphoreType.DMA
    chunks = [(quarter // 2, width, bf16, False)] * 2
    chunks += [(shard, width, bf16, False)] * (ff // width + 4)
    held_taps = -(-taps_count // 8) * 8
    inputs = {"length": (lengths, pltpu.SMEM), "sums_in": (sums, vmem)}
    inputs |= {"shared": (shared, vmem), "packs": (packs, vmem)}
    inputs |= {name: (x, anywhere) for name, x in big.items()}
    outputs = {
        "part_in": ((shard, ff), f32, vmem),
        "part_out": ((quarter, width), f32, vmem),
        "part_project": ((shard, width), f32, vmem),
        "sums_out": ((8, width), f32, vmem),
        "conv_sums": ((8, width), f32, vmem),
        "grad_taps": ((held_taps, width), f32, vmem),
        "part_middle": ((3 * shard, width), bf16, vmem),
        "grad_out": ((span, width), f32, anywhere),
        "own_grad": ((span, half), bf16, anywhere),
        "near_grad": ((span, half), bf16, anywhere),
    }
    scratch = {
        "held_" + name: vmem(big[name].shape, bf16)
        for name in ("half", "hidden", "normed", "dpre", "swish", "top")
    }
    scratch |= {
        "held_others": vmem(big["others"].shape, bf16),
        "load": dma((7,)),
        "filtered_slots": vmem((2, span, 128), f32),
        "dbn_slots": vmem((2, span, 128), f32),
        "gated_slots": vmem((2, span, 128), bf16),
        "column_load": dma((2, 3)),
        "slope_slots": vmem((2, ROWS, 2 * width), bf16),
        "grad_slots": vmem((2, ROWS, width), f32),
        "after_slots": vmem((2, ROWS, width), f32),
        "row_load": dma((2, 3)),
        "stat_near": vmem((m - 1, 8, width), f32),
        "stat_mid": vmem((8, width), f32),
        "stat_far": vmem((n - 1, 8, width), f32),
        "stat_send": dma((n + m - 2,)),
        "stat_recv": dma((n + m - 2,)),
        "padded": vmem((span + 2 * HALO, 128), f32),
        "gpadded": vmem((span + 2 * HALO, 128), f32),
        "grad_store": vmem((2, ROWS, width), f32),
        "own_slots": vmem((2, ROWS, half), bf16),
        "far_rows": vmem((span, half), bf16),
        "far_send": dma((span // ROWS,)),
        "far_recv": dma((span // ROWS,)),
        "store": dma((2, 2)),
    }
    return named_call(
        functools.partial(middle_kernel, chunks, taps_count), "middle", inputs, outputs, scratch,
        chunk_scratch(chunks), collective_id, span * (4 * ff * width + 8 * width * width),
    )


def closing_kernel(chunks, r, flow_refs):
    me, n = lax.axis_index("tm"), lax.axis_size("tm")
    core = lax.rem(lax.axis_index("slots"), 2)
    span, width = r.x.shape
    frames = span // n
    ff = r.hidden.shape[1]
    shard, quarter, half = width // 4, ff // 4, width // 2
    names = ("dq", "dk", "dv", "mixer", "hidden", "normed")
    loads = {
        name: pltpu.make_async_copy(getattr(r, name), getattr(r, "held_" + name), r.load.at[i])
        for i, name in enumerate(names)
    }
    for load in loads.values():
        load.start()
    x, z = lax.rem(me, 2), lax.div(me, 2)
    order = (2, 1, 3, 0)
    block = 2 * frames
    places = [pl.ds(pl.multiple_of(lax.rem(z + k, 4) * block, block), block) for k in order]
    rows = Stream(
        [r.grad, r.after, r.x, r.slope],
        [r.grad_slots, r.after_slots, r.x_slots, r.slope_slots],
        r.row_load,
        [(place, slice(None)) for place in places],
    )
    rows.begin(0)
    held = {}

    def need(name):
        if name not in held:
            loads[name].wait()
            held[name] = getattr(r, "held_" + name)
        return held[name]

    in_chunk = 3
    out_chunk = in_chunk + ff // width
    gain_chunk = len(chunks) - 1

    def finish(c, buffers):
        value = buffers[-1][...].astype(jnp.float32)
        if c < in_chunk:
            (r.part_query, r.part_key, r.part_value)[c][...] = value
        elif c < out_chunk:
            r.part_in[:, (c - in_chunk) * width : (c - in_chunk + 1) * width] = value
        elif c < gain_chunk:
            size = chunks[c][0]
            r.part_out[(c - out_chunk) * size : (c - out_chunk + 1) * size] = value
        else:
            r.part_gains[...] = value

    flow = Flow(chunks, flow_refs, finish)
    greet([{"tm": lax.rem(me + k, n)} for k in range(1, n)] + [flow.sibling, flow.across])
    heads = [
        remote(getattr(r, name), r.far.at[i], r.far_send.at[i], r.far_recv.at[i], flow.sibling)
        for i, name in enumerate(("near_dq", "near_dk", "near_dv"))
    ]
    for copy in heads:
        copy.start()

    sums = [jnp.zeros((1, width), jnp.float32)] * 2
    w_heads = (r.w_query, r.w_key, r.w_value)
    own_heads = [
        dot_tn(need("mixer")[...], need(name)[...]).astype(jnp.bfloat16)
        for name in ("dq", "dk", "dv")
    ]
    flow.spend(2.0)
    for i, own in enumerate(own_heads):
        heads[i].wait_recv()
        far = dot_tn(need("mixer")[...], r.far[i]).astype(jnp.bfloat16)
        total = jnp.concatenate(
            (jnp.where(core == 0, own, far), jnp.where(core == 0, far, own)), 1
        )
        flow.put_all(i, total.reshape(4, shard, width))
        flow.begin(i)
        flow.spend(1.2)

    sends = []
    for i, place in enumerate(places):
        rows.take(i)
        dnormed = None
        for j, name in enumerate(("dq", "dk", "dv")):
            for which, d in ((core, need(name)[place]), (1 - core, r.far[j, place])):
                term = dot_nt(d, head_columns(w_heads[j], which, half))
                dnormed = term if dnormed is None else dnormed + term
        normed, scale = normed_parts(r.after_slots[i % 2])
        sums[1] = sums[1] + column_sum(dnormed * normed)
        grad = r.grad_slots[i % 2] + normed_back(normed, scale, dnormed * param(r.packs, MIXER))
        half_grad = (0.5 * grad).astype(jnp.bfloat16)
        r.half_grad[place] = half_grad
        slope = r.slope_slots[i % 2].astype(jnp.float32)
        dpre = (dot_nt(half_grad, r.w_out[...]) * slope).astype(jnp.bfloat16)
        r.dpre[place] = dpre
        dnormed = dot_nt(dpre, r.w_in[...])
        normed, scale = normed_parts(r.x_slots[i % 2].astype(jnp.float32))
        sums[0] = sums[0] + column_sum(dnormed * normed)
        r.home_rows[place] = (
            grad + normed_back(normed, scale, dnormed * param(r.packs, FRONT))
        ).astype(jnp.bfloat16)
        for j in range(2):
            to = 2 * lax.rem(z + order[i], 4) + lax.rem(x + j, 2)
            source = r.home_rows.at[pl.ds(pl.multiple_of(to * frames, frames), frames)]
            sems = r.home_send.at[2 * i + j], r.home_recv.at[2 * i + j]
            if order[i] or j:
                sends.append(remote(source, r.home.at[me], *sems, {"tm": to}))
                flow.occupy("z", 4.5)
                flow.occupy("x", 2.2)
            else:
                sends.append(pltpu.make_async_copy(source, r.home.at[me], sems[0]))
            sends[-1].start()
        flow.spend(5.0)

    size = chunks[gain_chunk][0]
    rows_of = [sums[0], sums[1], r.conv_sums[0:1, :], r.back_sums[3:4, :], r.back_sums[2:3, :]]
    rows_of.append(r.grad_taps[...])
    rows_of.append(jnp.zeros((size - 5 - r.grad_taps.shape[0], width), jnp.float32))
    total = jnp.concatenate(rows_of, 0)
    terms = [total[:, o * shard : (o + 1) * shard] for o in range(4)]
    flow.put_all(gain_chunk, terms)
    flow.begin(gain_chunk)
    for j in range(gain_chunk - out_chunk):
        size = chunks[out_chunk + j][0]
        terms = []
        for o in range(4):
            at = o * quarter + j * size
            terms.append(
                dot_tn(need("hidden")[:, at : at + size], r.half_grad[...]).astype(jnp.bfloat16)
            )
        flow.put_all(out_chunk + j, terms)
        flow.begin(out_chunk + j)
        flow.spend(2.7)
    for j in range(ff // width):
        total = dot_tn(need("normed")[...], r.dpre[:, j * width : (j + 1) * width])
        flow.put_all(in_chunk + j, total.astype(jnp.bfloat16).reshape(4, shard, width))
        flow.begin(in_chunk + j)
        flow.spend(1.6)
    flow.drain()
    for copy in heads:
        copy.wait_send()
    for copy in sends:
        copy.wait()


def closing(packs, conv_sums, back_sums, grad_taps, weights, big, collective_id):
    bf16, f32 = jnp.bfloat16, jnp.float32
    anywhere, vmem = pl.ANY, pltpu.VMEM
    dma = pltpu.SemaphoreType.DMA
    span, width = big["x"].shape
    ff = big["hidden"].shape[1]
    n = lax.axis_size("tm")
    shard, quarter, half, frames = width // 4, ff // 4, width // 2, span // n
    chunks = [(shard, width, bf16, i >= 3 + DIRECT_FROM) for i in range(3 + ff // width)]
    chunks += [(quarter // 2, width, bf16, False)] * 2 + [(64, shard, f32, True)]
    inputs = {"packs": (packs, vmem), "conv_sums": (conv_sums, vmem)}
    inputs |= {"back_sums": (back_sums, vmem), "grad_taps": (grad_taps, vmem)}
    inputs |= {name: (x, vmem) for name, x in weights.items()}
    inputs |= {name: (x, anywhere) for name, x in big.items()}
    outputs = {
        "part_in": ((shard, ff), f32, vmem),
        "part_out": ((quarter, width), f32, vmem),
        "part_query": ((shard, width), f32, vmem),
        "part_key": ((shard, width), f32, vmem),
        "part_value": ((shard, width), f32, vmem),
        "part_gains": (chunks[-1][:2], f32, vmem),
        "home": ((n, frames, width), bf16, anywhere),
    }
    scratch = {
        "held_" + name: vmem(big[name].shape, bf16)
        for name in ("dq", "dk", "dv", "mixer", "hidden", "normed")
    }
    scratch |= {
        "load": dma((6,)),
        "grad_slots": vmem((2, 2 * frames, width), f32),
        "after_slots": vmem((2, 2 * frames, width), f32),
        "x_slots": vmem((2, 2 * frames, width), bf16),
        "slope_slots": vmem((2, 2 * frames, ff), bf16),
        "row_load": dma((2, 4)),
        "far": vmem((3, span, half), bf16),
        "far_send": dma((3,)),
        "far_recv": dma((3,)),
        "half_grad": vmem((span, width), bf16),
        "dpre": vmem((span, ff), bf16),
        "home_rows": vmem((span, width), bf16),
        "home_send": dma((n,)),
        "home_recv": dma((n,)),
    }
    return named_call(
        functools.partial(closing_kernel, chunks), "closing", inputs, outputs, scratch,
        chunk_scratch(chunks), collective_id, span * (8 * ff * width + 12 * width * width),
    )


def finish_kernel(taps_count, r, _):
    n = r.home.shape[0]
    slots = lax.axis_index("slots")
    shard = r.gains.shape[1]
    moved = [name for name in r.__dict__ if name.startswith("from_")]
    pairs = [(r.home.at[r.rank[u]], r.held_home.at[u], r.features.at[u]) for u in range(n)]
    for name in moved:
        bare = name[len("from_") :]
        pairs.append((getattr(r, name), getattr(r, "held_" + bare), getattr(r, "to_" + bare)))
    loads = [pltpu.make_async_copy(a, b, r.load.at[i]) for i, (a, b, _) in enumerate(pairs)]
    stores = [pltpu.make_async_copy(b, c, r.store.at[i]) for i, (_, b, c) in enumerate(pairs)]
    for copy in loads:
        copy.start()
    for i, ref in enumerate((r.front_gain, r.mixer_gain, r.conv_gain, r.back_gain, r.final_gain)):
        ref[...] = r.gains[i : i + 1, :].reshape(shard)
    taps = jnp.transpose(r.gains[5:37, :])
    r.depth[...] = taps[:, :taps_count]
    lanes = pl.ds(pl.multiple_of(slots * shard, shard), shard)
    r.batch_bias[...] = r.sums[0:1, lanes].reshape(shard)
    r.batch_gain[...] = r.sums[1:2, lanes].reshape(shard)
    width = r.output_weight.shape[1]
    for j in range(2):
        r.expand[:, j * width : (j + 1) * width] = r.middle[j * shard : (j + 1) * shard].astype(jnp.float32)
    r.output_weight[...] = r.middle[2 * shard :].astype(jnp.float32)
    for before, after in zip(loads, stores):
        before.wait()
        after.start()
    for copy in stores:
        copy.wait()


def finish(rank, home, gains, sums, middle, taps_count, parts):
    f32, vmem, anywhere = jnp.float32, pltpu.VMEM, pl.ANY
    dma = pltpu.SemaphoreType.DMA
    shard, width = gains.shape[1], middle.shape[1]
    inputs = {"rank": (rank, pltpu.SMEM), "home": (home, anywhere), "gains": (gains, vmem)}
    inputs |= {"sums": (sums, vmem), "middle": (middle, vmem)}
    inputs |= {"from_" + name: (x, anywhere) for name, x in parts.items()}
    outputs = {"features": (home.shape, home.dtype, anywhere)}
    outputs |= {
        name: ((shard,), f32, vmem)
        for name in ("front_gain", "mixer_gain", "conv_gain", "back_gain", "final_gain", "batch_bias", "batch_gain")
    }
    outputs |= {"depth": ((shard, taps_count), f32, vmem)}
    outputs |= {"expand": ((shard, 2 * width), f32, vmem), "output_weight": ((shard, width), f32, vmem)}
    outputs |= {"to_" + name: (x.shape, x.dtype, anywhere) for name, x in parts.items()}
    scratch = {"held_home": vmem(home.shape, home.dtype)}
    scratch |= {"held_" + name: vmem(x.shape, x.dtype) for name, x in parts.items()}
    count = home.shape[0] + len(parts)
    scratch |= {"load": dma((count,)), "store": dma((count,))}
    return named_call(
        functools.partial(finish_kernel, taps_count), "finish", inputs, outputs, scratch, [], None, 0
    )


def with_halo(block, sides, width):
    for axis, dim in sides:
        count = lax.axis_size(axis)
        forward = [(i, i + 1) for i in range(count - 1)]
        backward = [(target, source) for source, target in forward]
        low = lax.ppermute(
            lax.slice_in_dim(block, block.shape[dim] - width, None, axis=dim), axis, forward
        )
        high = lax.ppermute(lax.slice_in_dim(block, 0, width, axis=dim), axis, backward)
        block = jnp.concatenate([low, block, high], axis=dim)
    return block


def layer_norm(inputs, norm_gain):
    centred = inputs - jnp.mean(inputs, -1, keepdims=True)
    spread = jnp.mean(centred * centred, -1, keepdims=True)
    return centred * lax.rsqrt(spread + EPSILON) * norm_gain


def norm_back(inputs, norm_gain, incoming):
    result, pullback = jax.vjp(layer_norm, inputs, norm_gain)
    return pullback(incoming)


def matmul(left_side, right_side):
    return jnp.dot(left_side, right_side, preferred_element_type=jnp.float32)


def matmul_tn(left_side, right_side):
    return lax.dot_general(
        left_side, right_side, (((0,), (0,)), ((), ())), preferred_element_type=jnp.float32
    )


def matmul_nt(left_side, right_side):
    return lax.dot_general(
        left_side, right_side, (((1,), (1,)), ((), ())), preferred_element_type=jnp.float32
    )


def silu_slope(inputs):
    sigmoid_gate = jax.nn.sigmoid(inputs)
    return sigmoid_gate * (1.0 + inputs * (1.0 - sigmoid_gate))


def feed_forward(residual_rows, norm_gain, w_in, w_out):
    normed = layer_norm(residual_rows, norm_gain).astype(jnp.bfloat16)
    before_act = matmul(normed, w_in)
    hidden = jax.nn.silu(before_act).astype(jnp.bfloat16)
    return (residual_rows + 0.5 * matmul(hidden, w_out), (normed, before_act, hidden))


def feed_back(residual_rows, norm_gain, w_in, w_out, kept, incoming):
    normed, before_act, hidden = kept
    grad_top = (0.5 * incoming).astype(jnp.bfloat16)
    grad_w_out = matmul_tn(hidden, grad_top)
    grad_before = (matmul_nt(grad_top, w_out) * silu_slope(before_act)).astype(jnp.bfloat16)
    grad_w_in = matmul_tn(normed, grad_before)
    grad_normed = matmul_nt(grad_before, w_in)
    grad_rows, grad_gain = norm_back(residual_rows, norm_gain, grad_normed)
    return (incoming + grad_rows, grad_gain, grad_w_in, grad_w_out)


def exchange(x, pairs=CORE_PAIRS):
    return lax.ppermute(x, "slots", pairs)


def on_device_fast(
    features, lengths, cotangent, front_gain, front_in, front_out, mixer_gain, query_weight,
    key_weight, value_weight, output_weight, conv_gain, expand_weight, depth_weight, batch_gain,
    batch_bias, project_weight, back_gain, back_in, back_out, final_gain,
):
    slot_count, frames_dev, width = features.shape
    full_length = slot_count * frames_dev
    head_dim = width // HEADS
    half = width // 2
    tm, slots = lax.axis_index("tm"), lax.axis_index("slots")
    core = lax.rem(slots, 2)
    shard = front_gain.shape[0]
    taps_count = depth_weight.shape[1]

    feats, cots, pack, rank, length = arrange(
        lengths, features, cotangent,
        [front_gain, mixer_gain, conv_gain, batch_gain, batch_bias, back_gain, final_gain],
        depth_weight.astype(jnp.float32).T,
    )
    first = opening(
        feats,
        dict(pack=pack, w_in=front_in, w_out=front_out, w_query=query_weight, w_key=key_weight,
             w_value=value_weight),
        0,
    )
    packs = first.out_pack
    others = jnp.concatenate([expand_weight, output_weight, project_weight], 1)
    others, back_in, back_out, cots, _ = lax.optimization_barrier(
        (others, back_in, back_out, cots, packs)
    )
    gather = functools.partial(lax.all_gather, axis_name="slots", axis=0, tiled=True)
    full_others, full_back_in, full_back_out = gather(others), gather(back_in), gather(back_out)
    cot_rows = lax.all_to_all(cots, "tm", 0, 1, tiled=True)[0]

    pack_rows = packs.shape[0] // 4
    near_row = (slots + 1 - 2 * core) * pack_rows + pack_rows - 2
    near_length = lax.dynamic_slice(packs, (near_row, 0), (1, 1)).astype(jnp.int32)
    both_lengths = jnp.concatenate([length, near_length[0]])
    bf16, f32 = jnp.bfloat16, jnp.float32
    ff = front_in.shape[1]
    own_att, near_att, own_qa, near_qa = attend(first.own_qkv, first.near_qkv, both_lengths)
    far_att = exchange(near_att)
    after_mixer, conv_normed, gated, glu_slope = row_call(
        expand_kernel, "expand", length, [own_att, far_att, first.after],
        [packs, (full_others, width, 2), (full_others, 2 * width, 0)],
        [(width, f32), (width, bf16), (width, bf16), (2 * width, bf16)],
        0, 512, 6 * width * width,
    )
    filtered, stats = filter_frames(gated, packs, taps_count, length)
    shared = share_stats(stats, merge_spreads, 1)
    (output_rows, grad_rows, dbn, swish, conv_top, back_hidden, back_dpre, back_normed, back_half,
     back_sums) = row_call(
        back_kernel, "back", length, [filtered, after_mixer, cot_rows],
        [shared, packs, (full_others, width, 3), full_back_in, full_back_out],
        [(width, bf16), (width, f32), (width, f32), (width, bf16), (width, bf16), (ff, bf16),
         (ff, bf16), (width, bf16), (width, bf16)],
        1, 256, 8 * width * ff + 4 * width * width,
    )
    mid = middle(
        length, back_sums, shared, packs, taps_count,
        dict(hidden=back_hidden, dpre=back_dpre, half=back_half, normed=back_normed, swish=swish,
             top=conv_top, filtered=filtered, dbn=dbn, gated=gated, glu_slope=glu_slope,
             grad=grad_rows, after=after_mixer, conv_normed=conv_normed, own_att=own_att,
             far_att=far_att, others=full_others),
        2,
    )
    output_rows, _ = lax.optimization_barrier((output_rows, mid.sums_out))
    parts = lax.all_to_all(
        output_rows.reshape(slot_count, frames_dev, width), "tm", 0, 0, tiled=True
    )
    output = take_slots(parts, rank)
    part_middle = lax.psum(mid.part_middle, "tm")
    own_dqkv, near_dqkv = attend_back(
        (own_qa, first.own_qkv, mid.own_grad, own_att),
        (near_qa, first.near_qkv, mid.near_grad, near_att),
        both_lengths,
    )
    grad_taps, output = lax.optimization_barrier((mid.grad_taps, output))
    last = closing(
        packs, mid.conv_sums, back_sums, grad_taps,
        dict(w_in=first.out_w_in, w_out=first.out_w_out, w_query=first.out_w_query,
             w_key=first.out_w_key, w_value=first.out_w_value),
        dict(dq=own_dqkv[0], dk=own_dqkv[1], dv=own_dqkv[2],
             near_dq=near_dqkv[0], near_dk=near_dqkv[1], near_dv=near_dqkv[2], mixer=first.mixer,
             hidden=first.hidden, normed=first.normed, grad=mid.grad_out, after=first.after,
             x=first.rows, slope=first.slope),
        3,
    )
    done = finish(
        rank, last.home, last.part_gains, mid.sums_out, part_middle, taps_count,
        dict(front_in=last.part_in, front_out=last.part_out, query=last.part_query,
             key=last.part_key, value=last.part_value, project=mid.part_project,
             back_in=mid.part_in, back_out=mid.part_out),
    )
    return (
        output,
        done.features,
        done.front_gain,
        done.to_front_in,
        done.to_front_out,
        done.mixer_gain,
        done.to_query,
        done.to_key,
        done.to_value,
        done.output_weight,
        done.conv_gain,
        done.expand,
        done.depth,
        done.batch_gain,
        done.batch_bias,
        done.to_project,
        done.back_gain,
        done.to_back_in,
        done.to_back_out,
        done.final_gain,
    )


def on_device(features, *rest):
    whole = features.shape[0] == lax.axis_size("tm") and lax.axis_size("slots") == 4
    return (on_device_fast if whole else on_device_general)(features, *rest)


def on_device_general(
    features,
    lengths,
    cotangent,
    front_gain,
    front_in,
    front_out,
    mixer_gain,
    query_weight,
    key_weight,
    value_weight,
    output_weight,
    conv_gain,
    expand_weight,
    depth_weight,
    batch_gain,
    batch_bias,
    project_weight,
    back_gain,
    back_in,
    back_out,
    final_gain,
):
    gathered = (
        lax.all_gather(front_gain, "slots", axis=0, tiled=True),
        lax.all_gather(front_in, "slots", axis=0, tiled=True),
        lax.all_gather(front_out, "slots", axis=0, tiled=True),
        lax.all_gather(mixer_gain, "slots", axis=0, tiled=True),
        lax.all_gather(query_weight, "slots", axis=0, tiled=True),
        lax.all_gather(key_weight, "slots", axis=0, tiled=True),
        lax.all_gather(value_weight, "slots", axis=0, tiled=True),
        lax.all_gather(output_weight, "slots", axis=0, tiled=True),
        lax.all_gather(conv_gain, "slots", axis=0, tiled=True),
        lax.all_gather(expand_weight, "slots", axis=0, tiled=True),
        lax.all_gather(depth_weight, "slots", axis=0, tiled=True),
        lax.all_gather(batch_gain, "slots", axis=0, tiled=True),
        lax.all_gather(batch_bias, "slots", axis=0, tiled=True),
        lax.all_gather(project_weight, "slots", axis=0, tiled=True),
        lax.all_gather(back_gain, "slots", axis=0, tiled=True),
        lax.all_gather(back_in, "slots", axis=0, tiled=True),
        lax.all_gather(back_out, "slots", axis=0, tiled=True),
        lax.all_gather(final_gain, "slots", axis=0, tiled=True),
    )
    (
        full_front_gain,
        full_front_in,
        full_front_out,
        full_mixer_gain,
        full_query,
        full_key,
        full_value,
        full_output,
        full_conv_gain,
        full_expand,
        full_depth,
        full_batch_gain,
        full_batch_bias,
        full_project,
        full_back_gain,
        full_back_in,
        full_back_out,
        full_final_gain,
    ) = gathered
    front_norm_gain = full_front_gain.astype(jnp.float32)
    mixer_norm_gain = full_mixer_gain.astype(jnp.float32)
    conv_norm_gain = full_conv_gain.astype(jnp.float32)
    batch_scale = full_batch_gain.astype(jnp.float32)
    batch_shift = full_batch_bias.astype(jnp.float32)
    back_norm_gain = full_back_gain.astype(jnp.float32)
    final_norm_gain = full_final_gain.astype(jnp.float32)
    depth_taps = full_depth.astype(jnp.float32)
    slot_count, frames_dev, width = features.shape
    row_count = slot_count * frames_dev
    full_length = frames_dev * lax.axis_size("tm")
    head_dim = width // HEADS
    taps_count = full_depth.shape[1]
    half_width = taps_count // 2
    score_scale = 1.0 / math.sqrt(head_dim)
    head_numbers = jnp.arange(HEADS, dtype=jnp.int32)
    frame_index = lax.axis_index("tm") * frames_dev + jnp.arange(frames_dev, dtype=jnp.int32)
    frame_mask = (frame_index[None, :] < lengths[:, None]).astype(jnp.float32).reshape(row_count, 1)
    residual_rows = features.astype(jnp.float32).reshape(row_count, width)
    after_front, front_kept = feed_forward(
        residual_rows, front_norm_gain, full_front_in, full_front_out
    )
    mixer_normed = layer_norm(after_front, mixer_norm_gain).astype(jnp.bfloat16)
    query_rows = (
        matmul(mixer_normed, full_query).astype(jnp.bfloat16).reshape(slot_count, frames_dev, width)
    )
    key_rows = (
        matmul(mixer_normed, full_key).astype(jnp.bfloat16).reshape(slot_count, frames_dev, width)
    )
    value_rows = (
        matmul(mixer_normed, full_value).astype(jnp.bfloat16).reshape(slot_count, frames_dev, width)
    )

    def head_scores(head_index, key_part):
        span_keys = key_part.shape[1]
        query_head = lax.dynamic_slice_in_dim(query_rows, head_index * head_dim, head_dim, 2)
        key_head = lax.dynamic_slice_in_dim(key_part, head_index * head_dim, head_dim, 2)
        products = jnp.einsum(
            "ucd,und->ucn", query_head, key_head, preferred_element_type=jnp.float32
        )
        key_index = jnp.arange(span_keys, dtype=jnp.int32)
        slope_head = 64.0 * 2.0 ** (-head_index.astype(jnp.float32)) / full_length
        distance = jnp.abs(frame_index[:, None] - key_index[None, :]).astype(jnp.float32)
        scores = products * score_scale - slope_head * distance
        usable = key_index[None, None, :] < lengths[:, None, None]
        return (scores, usable, query_head, key_head)

    start_state = (
        jnp.full((HEADS, slot_count, frames_dev), -1e30, jnp.float32),
        jnp.zeros((HEADS, slot_count, frames_dev), jnp.float32),
        jnp.zeros((HEADS, slot_count, frames_dev, head_dim), jnp.float32),
    )
    key_part = lax.all_gather(key_rows, "tm", axis=1, tiled=True)
    value_part = lax.all_gather(value_rows, "tm", axis=1, tiled=True)

    def absorb_per_head(inputs):
        head_index, run_max, run_sum, accumulator = inputs
        scores, usable, query_head, key_head = head_scores(head_index, key_part)
        value_head = lax.dynamic_slice_in_dim(value_part, head_index * head_dim, head_dim, 2)
        new_max = jnp.maximum(run_max, jnp.max(jnp.where(usable, scores, -1e30), -1))
        weights_now = jnp.where(usable, jnp.exp(scores - new_max[..., None]), 0.0)
        factor = jnp.exp(run_max - new_max)
        new_sum = run_sum * factor + jnp.sum(weights_now, -1)
        new_accum = accumulator * factor[..., None] + jnp.einsum(
            "ucn,und->ucd",
            weights_now.astype(jnp.bfloat16),
            value_head,
            preferred_element_type=jnp.float32,
        )
        return (new_max, new_sum, new_accum)

    run_max, run_sum, accumulator = lax.map(absorb_per_head, (head_numbers,) + tuple(start_state))
    attended = accumulator / run_sum[..., None]
    log_total = run_max + jnp.log(run_sum)
    mixture = jnp.transpose(attended, (1, 2, 0, 3)).reshape(row_count, width).astype(jnp.bfloat16)
    after_mixer = after_front + matmul(mixture, full_output)
    conv_normed = layer_norm(after_mixer, conv_norm_gain).astype(jnp.bfloat16)
    expand = matmul(conv_normed, full_expand)
    linear_half = expand[:, :width]
    sigmoid_gate = jax.nn.sigmoid(expand[:, width:])
    gated = (
        (linear_half * sigmoid_gate * frame_mask)
        .astype(jnp.bfloat16)
        .reshape(slot_count, frames_dev, width)
    )
    padded = with_halo(gated, (("tm", 1),), half_width)
    filtered = padded[:, 0:frames_dev, :] * depth_taps[:, 0]
    for kernel_tap in range(1, taps_count):
        filtered = (
            filtered
            + padded[:, kernel_tap : kernel_tap + frames_dev, :] * depth_taps[:, kernel_tap]
        )
    filtered = filtered.reshape(row_count, width)
    mask_total, frames_total = lax.psum(
        (jnp.sum(filtered * frame_mask, 0), jnp.sum(frame_mask)), ("tm", "slots")
    )
    middle = mask_total / frames_total
    offset = filtered - middle
    spread = lax.psum(jnp.sum(frame_mask * offset * offset, 0), ("tm", "slots")) / frames_total
    inverse_spread = lax.rsqrt(spread + EPSILON)
    unit_conv = offset * inverse_spread
    batch_normed = unit_conv * batch_scale + batch_shift
    swish = jax.nn.silu(batch_normed).astype(jnp.bfloat16)
    after_conv = after_mixer + matmul(swish, full_project)
    after_back, back_kept = feed_forward(after_conv, back_norm_gain, full_back_in, full_back_out)
    output = (
        layer_norm(after_back, final_norm_gain)
        .astype(jnp.bfloat16)
        .reshape(slot_count, frames_dev, width)
    )
    incoming = cotangent.astype(jnp.float32).reshape(row_count, width)
    grad_rows, grad_final = norm_back(after_back, final_norm_gain, incoming)
    grad_rows, grad_back_gain, grad_back_in, grad_back_out = feed_back(
        after_conv, back_norm_gain, full_back_in, full_back_out, back_kept, grad_rows
    )
    grad_conv_top = grad_rows.astype(jnp.bfloat16)
    grad_project = matmul_tn(swish, grad_conv_top)
    grad_batch_normed = matmul_nt(grad_conv_top, full_project) * silu_slope(batch_normed)
    grad_batch_scale = jnp.sum(grad_batch_normed * unit_conv, 0)
    grad_batch_shift = jnp.sum(grad_batch_normed, 0)
    grad_unit = grad_batch_normed * batch_scale
    sum_plain, sum_scaled = lax.psum(
        (jnp.sum(grad_unit, 0), jnp.sum(grad_unit * unit_conv, 0)), ("tm", "slots")
    )
    grad_filtered = inverse_spread * (
        grad_unit - frame_mask * (sum_plain + unit_conv * sum_scaled) / frames_total
    )
    grad_grid = grad_filtered.reshape(slot_count, frames_dev, width)
    grad_padded = with_halo(grad_grid.astype(jnp.bfloat16), (("tm", 1),), half_width).astype(
        grad_grid.dtype
    )
    grad_gated = jnp.zeros((slot_count, frames_dev, width), jnp.float32)
    taps_grad = []
    for kernel_tap in range(taps_count):
        lead = 2 * half_width - kernel_tap
        grad_gated = (
            grad_gated + depth_taps[:, kernel_tap] * grad_padded[:, lead : lead + frames_dev, :]
        )
        taps_grad.append(
            jnp.sum(grad_grid * padded[:, kernel_tap : kernel_tap + frames_dev, :], axis=(0, 1))
        )
    grad_depth = jnp.stack(taps_grad, axis=1)
    grad_gated_low = lax.optimization_barrier(
        grad_gated.reshape(row_count, width).astype(jnp.bfloat16)
    ).astype(jnp.float32)
    grad_masked = grad_gated_low * frame_mask
    grad_linear = grad_masked * sigmoid_gate
    grad_gate = grad_masked * linear_half * sigmoid_gate * (1.0 - sigmoid_gate)
    grad_expand = jnp.concatenate([grad_linear, grad_gate], 1).astype(jnp.bfloat16)
    grad_expand_weight = matmul_tn(conv_normed, grad_expand)
    grad_conv_normed = matmul_nt(grad_expand, full_expand)
    delta_rows, grad_conv_gain = norm_back(after_mixer, conv_norm_gain, grad_conv_normed)
    grad_rows = grad_rows + delta_rows
    grad_mix_top = grad_rows.astype(jnp.bfloat16)
    grad_output_weight = matmul_tn(mixture, grad_mix_top)
    grad_mixture = matmul_nt(grad_mix_top, full_output).astype(jnp.bfloat16)
    grad_heads = jnp.transpose(
        grad_mixture.reshape(slot_count, frames_dev, HEADS, head_dim), (2, 0, 1, 3)
    )
    delta_heads = jnp.sum(grad_heads.astype(jnp.float32) * attended, -1)
    start_grads = (
        jnp.zeros((HEADS, slot_count, frames_dev, head_dim), jnp.float32),
        jnp.zeros((HEADS, slot_count, full_length, head_dim), jnp.float32),
        jnp.zeros((HEADS, slot_count, full_length, head_dim), jnp.float32),
    )
    collect_key_part = lax.all_gather(key_rows, "tm", axis=1, tiled=True)
    collect_value_part = lax.all_gather(value_rows, "tm", axis=1, tiled=True)
    span_keys = collect_key_part.shape[1]

    def collect_per_head(inputs):
        head_index, grad_query, key_sums, value_sums, total_log, delta_head, grad_head = inputs
        scores, usable, query_head, key_head = head_scores(head_index, collect_key_part)
        value_head = lax.dynamic_slice_in_dim(
            collect_value_part, head_index * head_dim, head_dim, 2
        )
        probs = jnp.where(usable, jnp.exp(scores - total_log[..., None]), 0.0)
        grad_probs = jnp.einsum(
            "ucd,und->ucn", grad_head, value_head, preferred_element_type=jnp.float32
        )
        grad_raw = (probs * (grad_probs - delta_head[..., None]) * score_scale).astype(jnp.bfloat16)
        grad_query = grad_query + jnp.einsum(
            "ucn,und->ucd", grad_raw, key_head, preferred_element_type=jnp.float32
        )
        key_term = jnp.einsum(
            "ucn,ucd->und", grad_raw, query_head, preferred_element_type=jnp.float32
        )
        value_term = jnp.einsum(
            "ucn,ucd->und",
            probs.astype(jnp.bfloat16),
            grad_head,
            preferred_element_type=jnp.float32,
        )
        key_sums = key_sums + key_term
        value_sums = value_sums + value_term
        return (grad_query, key_sums, value_sums)

    folded = lax.map(
        collect_per_head,
        (head_numbers,) + tuple(start_grads) + (log_total, delta_heads, grad_heads),
    )
    grad_query_heads, key_sums, value_sums = folded
    grad_key_heads, grad_value_heads = (
        lax.psum_scatter(
            key_sums.astype(jnp.bfloat16), "tm", scatter_dimension=2, tiled=True
        ).astype(jnp.float32),
        lax.psum_scatter(
            value_sums.astype(jnp.bfloat16), "tm", scatter_dimension=2, tiled=True
        ).astype(jnp.float32),
    )

    def to_rows(heads_array):
        return (
            jnp.transpose(heads_array, (1, 2, 0, 3)).reshape(row_count, width).astype(jnp.bfloat16)
        )

    grad_query_rows = to_rows(grad_query_heads)
    grad_key_rows = to_rows(grad_key_heads)
    grad_value_rows = to_rows(grad_value_heads)
    grad_query_weight = matmul_tn(mixer_normed, grad_query_rows)
    grad_key_weight = matmul_tn(mixer_normed, grad_key_rows)
    grad_value_weight = matmul_tn(mixer_normed, grad_value_rows)
    grad_mixer_normed = (
        matmul_nt(grad_query_rows, full_query)
        + matmul_nt(grad_key_rows, full_key)
        + matmul_nt(grad_value_rows, full_value)
    )
    delta_rows, grad_mixer_gain = norm_back(after_front, mixer_norm_gain, grad_mixer_normed)
    grad_rows = grad_rows + delta_rows
    grad_rows, grad_front_gain, grad_front_in, grad_front_out = feed_back(
        residual_rows, front_norm_gain, full_front_in, full_front_out, front_kept, grad_rows
    )
    grad_features = grad_rows.astype(jnp.bfloat16).reshape(slot_count, frames_dev, width)
    partial_rows = (
        lax.psum_scatter(
            grad_front_gain.astype(jnp.bfloat16), "slots", scatter_dimension=0, tiled=True
        ).astype(jnp.float32),
        lax.psum_scatter(
            grad_front_in.astype(jnp.bfloat16), "slots", scatter_dimension=0, tiled=True
        ).astype(jnp.float32),
        lax.psum_scatter(
            grad_front_out.astype(jnp.bfloat16), "slots", scatter_dimension=0, tiled=True
        ).astype(jnp.float32),
        lax.psum_scatter(
            grad_mixer_gain.astype(jnp.bfloat16), "slots", scatter_dimension=0, tiled=True
        ).astype(jnp.float32),
        lax.psum_scatter(
            grad_query_weight.astype(jnp.bfloat16), "slots", scatter_dimension=0, tiled=True
        ).astype(jnp.float32),
        lax.psum_scatter(
            grad_key_weight.astype(jnp.bfloat16), "slots", scatter_dimension=0, tiled=True
        ).astype(jnp.float32),
        lax.psum_scatter(
            grad_value_weight.astype(jnp.bfloat16), "slots", scatter_dimension=0, tiled=True
        ).astype(jnp.float32),
        lax.psum_scatter(
            grad_output_weight.astype(jnp.bfloat16), "slots", scatter_dimension=0, tiled=True
        ).astype(jnp.float32),
        lax.psum_scatter(
            grad_conv_gain.astype(jnp.bfloat16), "slots", scatter_dimension=0, tiled=True
        ).astype(jnp.float32),
        lax.psum_scatter(
            grad_expand_weight.astype(jnp.bfloat16), "slots", scatter_dimension=0, tiled=True
        ).astype(jnp.float32),
        lax.psum_scatter(
            grad_depth.astype(jnp.bfloat16), "slots", scatter_dimension=0, tiled=True
        ).astype(jnp.float32),
        lax.psum_scatter(
            grad_batch_scale.astype(jnp.bfloat16), "slots", scatter_dimension=0, tiled=True
        ).astype(jnp.float32),
        lax.psum_scatter(
            grad_batch_shift.astype(jnp.bfloat16), "slots", scatter_dimension=0, tiled=True
        ).astype(jnp.float32),
        lax.psum_scatter(
            grad_project.astype(jnp.bfloat16), "slots", scatter_dimension=0, tiled=True
        ).astype(jnp.float32),
        lax.psum_scatter(
            grad_back_gain.astype(jnp.bfloat16), "slots", scatter_dimension=0, tiled=True
        ).astype(jnp.float32),
        lax.psum_scatter(
            grad_back_in.astype(jnp.bfloat16), "slots", scatter_dimension=0, tiled=True
        ).astype(jnp.float32),
        lax.psum_scatter(
            grad_back_out.astype(jnp.bfloat16), "slots", scatter_dimension=0, tiled=True
        ).astype(jnp.float32),
        lax.psum_scatter(
            grad_final.astype(jnp.bfloat16), "slots", scatter_dimension=0, tiled=True
        ).astype(jnp.float32),
    )
    (
        part_front_gain,
        part_front_in,
        part_front_out,
        part_mixer_gain,
        part_query,
        part_key,
        part_value,
        part_output,
        part_conv_gain,
        part_expand,
        part_depth,
        part_batch_gain,
        part_batch_bias,
        part_project,
        part_back_gain,
        part_back_in,
        part_back_out,
        part_final_gain,
    ) = partial_rows
    shards = (
        lax.psum(part_front_gain.astype(jnp.bfloat16), "tm").astype(jnp.float32),
        lax.psum(part_front_in.astype(jnp.bfloat16), "tm").astype(jnp.float32),
        lax.psum(part_front_out.astype(jnp.bfloat16), "tm").astype(jnp.float32),
        lax.psum(part_mixer_gain.astype(jnp.bfloat16), "tm").astype(jnp.float32),
        lax.psum(part_query.astype(jnp.bfloat16), "tm").astype(jnp.float32),
        lax.psum(part_key.astype(jnp.bfloat16), "tm").astype(jnp.float32),
        lax.psum(part_value.astype(jnp.bfloat16), "tm").astype(jnp.float32),
        lax.psum(part_output.astype(jnp.bfloat16), "tm").astype(jnp.float32),
        lax.psum(part_conv_gain.astype(jnp.bfloat16), "tm").astype(jnp.float32),
        lax.psum(part_expand.astype(jnp.bfloat16), "tm").astype(jnp.float32),
        lax.psum(part_depth.astype(jnp.bfloat16), "tm").astype(jnp.float32),
        lax.psum(part_batch_gain.astype(jnp.bfloat16), "tm").astype(jnp.float32),
        lax.psum(part_batch_bias.astype(jnp.bfloat16), "tm").astype(jnp.float32),
        lax.psum(part_project.astype(jnp.bfloat16), "tm").astype(jnp.float32),
        lax.psum(part_back_gain.astype(jnp.bfloat16), "tm").astype(jnp.float32),
        lax.psum(part_back_in.astype(jnp.bfloat16), "tm").astype(jnp.float32),
        lax.psum(part_back_out.astype(jnp.bfloat16), "tm").astype(jnp.float32),
        lax.psum(part_final_gain.astype(jnp.bfloat16), "tm").astype(jnp.float32),
    )
    return (output, grad_features) + tuple(shards)


def solution(mesh):
    in_specs = (
        P("slots", "tm", None),
        P("slots"),
        P("slots", "tm", None),
        P("slots"),
        P("slots", None),
        P("slots", None),
        P("slots"),
        P("slots", None),
        P("slots", None),
        P("slots", None),
        P("slots", None),
        P("slots"),
        P("slots", None),
        P("slots", None),
        P("slots"),
        P("slots"),
        P("slots", None),
        P("slots"),
        P("slots", None),
        P("slots", None),
        P("slots"),
    )
    out_specs = (
        P("slots", "tm", None),
        P("slots", "tm", None),
        P("slots"),
        P("slots", None),
        P("slots", None),
        P("slots"),
        P("slots", None),
        P("slots", None),
        P("slots", None),
        P("slots", None),
        P("slots"),
        P("slots", None),
        P("slots", None),
        P("slots"),
        P("slots"),
        P("slots", None),
        P("slots"),
        P("slots", None),
        P("slots", None),
        P("slots"),
    )
    return jax.shard_map(
        on_device, mesh=mesh, in_specs=in_specs, out_specs=out_specs, check_vma=False
    )
```

```python
import functools
import math

import jax
import jax.numpy as jnp
from jax import lax
from jax.experimental import pallas as pl
from jax.experimental.pallas import tpu as pltpu
from jax.sharding import PartitionSpec as P

HEADS = 8


EPSILON = 1e-05
MESH = pl.DeviceIdType.MESH
KEY_BLOCK = 256
QUERY_BLOCK = 256
MASKED = -1e30
HALO = 16
CORE_PAIRS = [(0, 1), (1, 0), (2, 3), (3, 2)]


def remote(src, dst, send_sem, recv_sem, where):
    return pltpu.make_async_remote_copy(
        src_ref=src,
        dst_ref=dst,
        send_sem=send_sem,
        recv_sem=recv_sem,
        device_id=where,
        device_id_type=MESH,
    )


def stats_kernel(combine, x_ref, o_ref, near, far, mid, send, recv):
    t, s = lax.axis_index("tm"), lax.axis_index("slots")
    n, m = lax.axis_size("tm"), lax.axis_size("slots")
    barrier = pltpu.get_barrier_semaphore()
    slot_places = [{"slots": lax.rem(s + k, m)} for k in range(1, m)]
    tm_places = [{"tm": lax.rem(t + k, n)} for k in range(1, n)]
    for place in slot_places + tm_places:
        pl.semaphore_signal(barrier, inc=1, device_id=place, device_id_type=MESH)
    pl.semaphore_wait(barrier, n + m - 2)

    def share(source, landing, places, first):
        copies = []
        for i, place in enumerate(places):
            copies.append(
                remote(source, landing.at[i], send.at[first + i], recv.at[first + i], place)
            )
            copies[-1].start()
        for copy in copies:
            copy.wait()
        return combine([source[...]] + [landing[i] for i in range(len(places))])

    mid[...] = share(x_ref, near, slot_places, 0)
    o_ref[...] = share(mid, far, tm_places, m - 1)


def add_blocks(blocks):
    total = blocks[0]
    for block in blocks[1:]:
        total = total + block
    return total


def merge_spreads(blocks):
    sums = add_blocks([b[0:1] for b in blocks])
    counts = add_blocks([b[2:3] for b in blocks])
    mean = sums / counts
    squares = add_blocks(
        [b[1:2] + b[2:3] * (b[0:1] / b[2:3] - mean) * (b[0:1] / b[2:3] - mean) for b in blocks]
    )
    return jnp.concatenate((sums, squares, counts, jnp.zeros((5,) + sums.shape[1:], sums.dtype)), 0)


def share_stats(block, combine, collective_id):
    n, m = lax.axis_size("tm"), lax.axis_size("slots")
    return pl.pallas_call(
        functools.partial(stats_kernel, combine),
        out_shape=jax.ShapeDtypeStruct(block.shape, block.dtype),
        in_specs=[pl.BlockSpec(memory_space=pltpu.VMEM)],
        out_specs=pl.BlockSpec(memory_space=pltpu.VMEM),
        scratch_shapes=[
            pltpu.VMEM((m - 1,) + block.shape, block.dtype),
            pltpu.VMEM((n - 1,) + block.shape, block.dtype),
            pltpu.VMEM(block.shape, block.dtype),
            pltpu.SemaphoreType.DMA((n + m - 2,)),
            pltpu.SemaphoreType.DMA((n + m - 2,)),
        ],
        compiler_params=pltpu.CompilerParams(collective_id=collective_id, has_side_effects=True),
        name="share_stats",
    )(block)


FRONT, MIXER, CONV, BATCH, BIAS, BACK, FINAL, TAPS = range(8)


def param(packs, i):
    rows = packs.shape[0] // 4
    return jnp.concatenate([packs[o * rows + i : o * rows + i + 1, :] for o in range(4)], 1)


def frame_count(packs):
    rows = packs.shape[0] // 4
    total = add_blocks([packs[o * rows + rows - 1 : (o + 1) * rows, :] for o in range(4)])
    return jnp.concatenate([total] * 4, 1)


def arrange_kernel(lengths, feat, cot, w_expand, w_output, w_project, *refs):
    gains, (taps, feat_out, cot_out, pack, others, rank, own), scratch = refs[:7], refs[7:14], refs[14:]
    held, load, store = scratch
    n = feat.shape[0]
    core = lax.rem(lax.axis_index("slots"), 2)
    me = lax.axis_index("tm")
    all_lengths = [lengths[u] for u in range(n)]
    length, total = jnp.int32(0), jnp.int32(0)
    loads, stores = [], []
    for u in range(n):
        ahead = jnp.int32(0)
        for v in range(n):
            if v != u:
                before = all_lengths[v] >= all_lengths[u] if v < u else all_lengths[v] > all_lengths[u]
                ahead = ahead + before.astype(jnp.int32)
        place = jnp.where(core == 0, ahead, n - 1 - ahead)
        rank[u] = place
        length = length + jnp.where(place == me, all_lengths[u], 0)
        total = total + all_lengths[u]
        for j, (source, target) in enumerate(((feat, feat_out), (cot, cot_out))):
            loads.append(pltpu.make_async_copy(source.at[u], held.at[j, u], load.at[j, u]))
            stores.append(pltpu.make_async_copy(held.at[j, u], target.at[place], store.at[j, u]))
    own[0] = length
    for copy in loads:
        copy.start()
    at = 0
    for w in (w_expand, w_output, w_project):
        others[:, at : at + w.shape[1]] = w[...]
        at += w.shape[1]
    width = pack.shape[1]
    count = taps.shape[0]
    pack[...] = jnp.zeros_like(pack)
    for i, gain in enumerate(gains):
        pack[i : i + 1, :] = gain[...].astype(jnp.float32).reshape(1, width)
    pack[TAPS : TAPS + count, :] = taps[...]
    rows = pack.shape[0]
    pack[rows - 2 : rows - 1, :] = jnp.full((1, width), length.astype(jnp.float32))
    pack[rows - 1 : rows, :] = jnp.full((1, width), total.astype(jnp.float32))
    for before, after in zip(loads, stores):
        before.wait()
        after.start()
    for copy in stores:
        copy.wait()


def arrange(lengths, features, cotangent, weights, gains, taps):
    n = features.shape[0]
    rows = -(-(TAPS + taps.shape[0] + 2) // 8) * 8
    smem, vmem, anywhere = pltpu.SMEM, pltpu.VMEM, pl.ANY
    dma = pltpu.SemaphoreType.DMA
    return pl.pallas_call(
        arrange_kernel,
        out_shape=[
            jax.ShapeDtypeStruct(features.shape, features.dtype),
            jax.ShapeDtypeStruct(features.shape, features.dtype),
            jax.ShapeDtypeStruct((rows, taps.shape[1]), jnp.float32),
            jax.ShapeDtypeStruct(
                (weights[0].shape[0], sum(w.shape[1] for w in weights)), weights[0].dtype
            ),
            jax.ShapeDtypeStruct((n,), jnp.int32),
            jax.ShapeDtypeStruct((1,), jnp.int32),
        ],
        in_specs=[pl.BlockSpec(memory_space=smem)]
        + [pl.BlockSpec(memory_space=anywhere)] * 2
        + [pl.BlockSpec(memory_space=vmem)] * 11,
        out_specs=[pl.BlockSpec(memory_space=x) for x in (anywhere, anywhere, vmem, vmem, smem, smem)],
        scratch_shapes=[vmem((2,) + features.shape, features.dtype), dma((2, n)), dma((2, n))],
        name="arrange",
    )(lengths, features, cotangent, *weights, *gains, taps)


def split_parts(x):
    high = x.astype(jnp.bfloat16).astype(jnp.float32)
    rest = x - high
    middle = rest.astype(jnp.bfloat16).astype(jnp.float32)
    return high, middle, rest - middle


def dot_nn(a, b):
    return jnp.dot(a, b, preferred_element_type=jnp.float32)


def dot_nt(a, b):
    return lax.dot_general(a, b, (((1,), (1,)), ((), ())), preferred_element_type=jnp.float32)


def fill_bias(table, slope, blocks, span):
    rows = lax.broadcasted_iota(jnp.int32, (KEY_BLOCK, KEY_BLOCK), 0)
    lanes = lax.broadcasted_iota(jnp.int32, (KEY_BLOCK, KEY_BLOCK), 1)
    relative = (rows - lanes + (span - KEY_BLOCK)).astype(jnp.float32)

    def fill(c, carry):
        at = pl.multiple_of(c * KEY_BLOCK, KEY_BLOCK)
        table[:, pl.ds(at, KEY_BLOCK)] = slope * jnp.abs(relative - at.astype(jnp.float32))
        return carry

    lax.fori_loop(span // KEY_BLOCK - blocks, 2 * span // KEY_BLOCK - 1, fill, 0)


def lane_rows(span):
    lane = lax.broadcasted_iota(jnp.int32, (1, 128), 1)
    first = (lane < 64).astype(jnp.float32)
    return (first, 1.0 - first), lax.rem(lane, 64)


def one_hot(place, low, high):
    return ((place >= low) & (place < high)).astype(jnp.float32)


def key_tile(k, sel, place, length):
    row = lax.broadcasted_iota(jnp.int32, (k.shape[0], 1), 0)
    masked = jnp.where(row < length, 0.0, MASKED)
    extra = (1.0 - sel) * (one_hot(place, 1, 4) + masked * one_hot(place, 0, 1))
    return k * sel.astype(jnp.bfloat16) + extra.astype(jnp.bfloat16)


def block_count(length):
    return (length + KEY_BLOCK - 1) // KEY_BLOCK


def head_slope(i, span):
    core = lax.rem(lax.axis_index("slots"), 2)
    slope = jnp.float32(64.0 / span)
    for head in range(1, HEADS):
        slope = jnp.where(core * (HEADS // 2) + i == head, 64.0 * 2.0**-head / span, slope)
    return slope


def attend_kernel(lengths, *refs):
    qkv, (own_att, near_att, own_qa, near_qa) = (refs[0:3], refs[3:6]), refs[6:10]
    table, qa, ka, vt, acc, top = refs[10:]
    span = own_att.shape[0]
    pair = pl.program_id(0)
    sels, place = lane_rows(span)
    counts = [block_count(lengths[u]) for u in range(2)]
    most = jnp.maximum(counts[0], counts[1])
    for h in range(2):
        fill_bias(table.at[h], head_slope(2 * pair + h, span), most, span)
    ones = jnp.ones((16, span), jnp.bfloat16)
    for u in range(2):
        q, k, v = (r[...] for r in qkv[u])
        v_turned = jnp.transpose(v)
        for h in range(2):
            query_extra = (1.0 - sels[h]) * one_hot(place, 0, 1)
            qa[u, h] = q * (sels[h] * 0.125).astype(jnp.bfloat16) + query_extra.astype(jnp.bfloat16)
            ka[u, h] = key_tile(k, sels[h], place, lengths[u])
            vt[u, h, 0:64] = v_turned[64 * h : 64 * h + 64]
            vt[u, h, 64:80] = ones
    acc[...] = jnp.zeros_like(acc)
    top[...] = jnp.full_like(top, -3e38)

    def step(i, carry):
        u = (i >= counts[0]).astype(jnp.int32)
        at = pl.multiple_of((i - u * counts[0]) * KEY_BLOCK, KEY_BLOCK)
        x0 = pl.multiple_of((span - KEY_BLOCK) - at, KEY_BLOCK)
        for h in range(2):
            s = dot_nt(ka[u, h, pl.ds(at, KEY_BLOCK), :], qa[u, h]) - table[h, :, pl.ds(x0, span)]
            old = top[u, h, 0:1]
            new = jnp.maximum(old, jnp.max(s, axis=0, keepdims=True))
            p = jnp.exp(s - new).astype(jnp.bfloat16)
            top[u, h, 0:1] = new
            acc[u, h] = acc[u, h] * jnp.exp(old - new) + dot_nn(
                vt[u, h, :, pl.ds(at, KEY_BLOCK)], p
            )
        return carry

    lax.fori_loop(0, counts[0] + counts[1], step, 0)
    for u, att, qa_out in ((0, own_att, own_qa), (1, near_att, near_qa)):
        attended, extras = [], []
        for h in range(2):
            total = acc[u, h, 64:65, :]
            attended.append((acc[u, h, 0:64, :] / total).astype(jnp.bfloat16))
            parts = split_parts(-(top[u, h, 0:1, :] + jnp.log(total)))
            extras.append(
                jnp.concatenate(
                    (jnp.zeros_like(total),) + parts + (jnp.zeros((60, span), jnp.float32),), 0
                ).astype(jnp.bfloat16)
            )
        att[...] = jnp.transpose(jnp.concatenate(attended, 0))
        query_extra = jnp.transpose(jnp.concatenate((extras[1], extras[0]), 0))
        for h in range(2):
            qa_out[h] = qa[u, h] + query_extra * (1.0 - sels[h]).astype(jnp.bfloat16)


def pair_columns(span, pairs, which):
    return pl.BlockSpec((span, 128), lambda p, *_: (0, which * pairs + p))


def attend(own_qkv, near_qkv, lengths):
    span, columns = own_qkv.shape
    pairs = columns // 384
    cells = span * span * pairs * 2
    table_width = 2 * span - KEY_BLOCK
    columns3 = [pair_columns(span, pairs, i) for i in range(3)]
    tall = pl.BlockSpec((span, 128), lambda p, *_: (0, p))
    heads = pl.BlockSpec((2, span, 128), lambda p, *_: (p, 0, 0))
    return pl.pallas_call(
        attend_kernel,
        out_shape=[jax.ShapeDtypeStruct((span, pairs * 128), jnp.bfloat16)] * 2
        + [jax.ShapeDtypeStruct((2 * pairs, span, 128), jnp.bfloat16)] * 2,
        grid_spec=pltpu.PrefetchScalarGridSpec(
            num_scalar_prefetch=1,
            grid=(pairs,),
            in_specs=columns3 * 2,
            out_specs=[tall, tall, heads, heads],
            scratch_shapes=[
                pltpu.VMEM((2, KEY_BLOCK, table_width), jnp.float32),
                pltpu.VMEM((2, 2, span, 128), jnp.bfloat16),
                pltpu.VMEM((2, 2, span, 128), jnp.bfloat16),
                pltpu.VMEM((2, 2, 80, span), jnp.bfloat16),
                pltpu.VMEM((2, 2, 80, span), jnp.float32),
                pltpu.VMEM((2, 2, 8, span), jnp.float32),
            ],
        ),
        compiler_params=pltpu.CompilerParams(vmem_limit_bytes=56 << 20),
        cost_estimate=pl.CostEstimate(
            flops=cells * 4 * 256, bytes_accessed=span * columns * 8, transcendentals=cells
        ),
        name="attend",
    )(lengths, *([own_qkv] * 3), *([near_qkv] * 3))


def attend_back_kernel(lengths, *refs):
    inputs, outputs = (refs[0:5], refs[5:10]), (refs[10:13], refs[13:16])
    table, qa, ka, va, ga, kt, dqt, dk_out, dv_out = refs[16:]
    span = refs[1].shape[0]
    pair = pl.program_id(0)
    sels, place = lane_rows(span)
    counts = [block_count(lengths[u]) for u in range(2)]
    most = jnp.maximum(counts[0], counts[1])
    for h in range(2):
        fill_bias(table.at[h], head_slope(2 * pair + h, span), most, span)
    side = lax.broadcasted_iota(jnp.int32, (128, 128), 0) < 64
    other = lax.broadcasted_iota(jnp.int32, (128, 128), 1) >= 64
    gather = jnp.where(side == other, 1.0, 0.0).astype(jnp.bfloat16)
    for u in range(2):
        qa_in, k_in, v_in, g_in, att_in = inputs[u]
        k, v, g = k_in[...], v_in[...], g_in[...]
        product = g.astype(jnp.float32) * att_in[...].astype(jnp.float32)
        high = product.astype(jnp.bfloat16)
        low = (product - high.astype(jnp.float32)).astype(jnp.bfloat16)
        delta = split_parts(dot_nn(high, gather) + dot_nn(low, gather))
        grad_extra = sum(
            delta[i].astype(jnp.bfloat16) * one_hot(place, i, i + 1).astype(jnp.bfloat16)
            for i in range(3)
        )
        kt[u] = jnp.transpose(k)
        for h in range(2):
            sel = sels[h].astype(jnp.bfloat16)
            rest = (1.0 - sels[h]).astype(jnp.bfloat16)
            qa[u, h] = qa_in[h]
            ka[u, h] = key_tile(k, sels[h], place, lengths[u])
            va[u, h] = v * sel - ((1.0 - sels[h]) * one_hot(place, 0, 3)).astype(jnp.bfloat16)
            ga[u, h] = g * sel + grad_extra * rest
    dqt[...] = jnp.zeros_like(dqt)
    block_lane = lax.broadcasted_iota(jnp.int32, (KEY_BLOCK, 128), 1)

    def step(i, carry):
        u = (i >= counts[0]).astype(jnp.int32)
        at = pl.multiple_of((i - u * counts[0]) * KEY_BLOCK, KEY_BLOCK)
        keys = pl.ds(at, KEY_BLOCK)
        x0 = pl.multiple_of((span - KEY_BLOCK) - at, KEY_BLOCK)
        dk, dv = [], []
        for h in range(2):
            query_rows, grad_rows = qa[u, h], ga[u, h]
            s = dot_nt(ka[u, h, keys, :], query_rows)
            p = jnp.exp(s - table[h, :, pl.ds(x0, span)])
            d = (p * dot_nt(va[u, h, keys, :], grad_rows)).astype(jnp.bfloat16)
            dv.append(dot_nn(p.astype(jnp.bfloat16), grad_rows))
            dk.append(dot_nn(d, query_rows))
            rows = slice(64 * h, 64 * h + 64)
            dqt[u, rows] += dot_nn(kt[u, rows, keys], d)
        dk_out[u, keys, :] = jnp.where(block_lane < 64, dk[0], dk[1]).astype(jnp.bfloat16)
        dv_out[u, keys, :] = jnp.where(block_lane < 64, dv[0], dv[1]).astype(jnp.bfloat16)
        return carry

    lax.fori_loop(0, counts[0] + counts[1], step, 0)
    for u in range(2):

        def blank(b, carry, u=u):
            keys = pl.ds(pl.multiple_of(b * KEY_BLOCK, KEY_BLOCK), KEY_BLOCK)
            dk_out[u, keys, :] = jnp.zeros((KEY_BLOCK, 128), jnp.bfloat16)
            dv_out[u, keys, :] = jnp.zeros((KEY_BLOCK, 128), jnp.bfloat16)
            return carry

        lax.fori_loop(counts[u], span // KEY_BLOCK, blank, 0)
        dq_ref, dk_ref, dv_ref = outputs[u]
        dk_ref[...] = dk_out[u]
        dv_ref[...] = dv_out[u]
        dq_ref[...] = jnp.transpose((dqt[u] * 0.125).astype(jnp.bfloat16))


def attend_back(own, near, lengths):
    span, columns = own[1].shape
    pairs = columns // 384
    cells = span * span * pairs * 2
    table_width = 2 * span - KEY_BLOCK
    tall = pl.BlockSpec((span, 128), lambda p, *_: (0, p))
    heads = pl.BlockSpec((2, span, 128), lambda p, *_: (p, 0, 0))
    specs = [heads, pair_columns(span, pairs, 1), pair_columns(span, pairs, 2), tall, tall]
    tile = pltpu.VMEM((2, 2, span, 128), jnp.bfloat16)
    grads = pl.pallas_call(
        attend_back_kernel,
        out_shape=[jax.ShapeDtypeStruct((span, pairs * 128), jnp.bfloat16)] * 6,
        grid_spec=pltpu.PrefetchScalarGridSpec(
            num_scalar_prefetch=1,
            grid=(pairs,),
            in_specs=specs * 2,
            out_specs=[tall] * 6,
            scratch_shapes=[
                pltpu.VMEM((2, KEY_BLOCK, table_width), jnp.float32),
                tile,
                tile,
                tile,
                tile,
                pltpu.VMEM((2, 128, span), jnp.bfloat16),
                pltpu.VMEM((2, 128, span), jnp.float32),
                pltpu.VMEM((2, span, 128), jnp.bfloat16),
                pltpu.VMEM((2, span, 128), jnp.bfloat16),
            ],
        ),
        compiler_params=pltpu.CompilerParams(vmem_limit_bytes=56 << 20),
        cost_estimate=pl.CostEstimate(
            flops=cells * 10 * 256, bytes_accessed=span * columns * 16, transcendentals=cells
        ),
        name="attend_back",
    )(
        lengths,
        own[0], own[1], own[1], own[2], own[3],
        near[0], near[1], near[1], near[2], near[3],
    )
    return grads[:3], grads[3:]


CHUNK = 128


def tap_windows(padded, at, taps_count):
    first = HALO - taps_count // 2
    for o in range(8):
        window = padded[pl.ds(at + o, CHUNK + 24), :]
        for start in range(o, first + taps_count, 8):
            if start >= first:
                yield start - first, window[start - o : start - o + CHUNK]


def filter_kernel(taps_count, scalars, gated_ref, packs_ref, out_ref, stats_ref, padded):
    span = gated_ref.shape[0]
    length = scalars[0]
    padded[0:HALO] = jnp.zeros((HALO, 128), jnp.float32)
    padded[HALO + span : HALO + span + HALO] = jnp.zeros((HALO, 128), jnp.float32)
    padded[HALO : HALO + span] = gated_ref[...].astype(jnp.float32)

    def chunk(c, total):
        at = pl.multiple_of(c * CHUNK, CHUNK)
        value = jnp.zeros((CHUNK, 128), jnp.float32)
        for k, window in tap_windows(padded, at, taps_count):
            value = value + window * packs_ref[TAPS + k : TAPS + k + 1, :]
        out_ref[pl.ds(at, CHUNK), :] = value
        row = lax.broadcasted_iota(jnp.int32, (CHUNK, 128), 0) + at
        return total + jnp.sum(jnp.where(row < length, value, 0.0), axis=0, keepdims=True)

    total = lax.fori_loop(0, span // CHUNK, chunk, jnp.zeros((1, 128), jnp.float32))
    mean = total / length.astype(jnp.float32)

    def deviate(c, squares):
        at = pl.multiple_of(c * CHUNK, CHUNK)
        row = lax.broadcasted_iota(jnp.int32, (CHUNK, 128), 0) + at
        off = jnp.where(row < length, out_ref[pl.ds(at, CHUNK), :] - mean, 0.0)
        return squares + jnp.sum(off * off, axis=0, keepdims=True)

    squares = lax.fori_loop(0, span // CHUNK, deviate, jnp.zeros((1, 128), jnp.float32))
    count = jnp.full((1, 128), length.astype(jnp.float32))
    stats_ref[...] = jnp.concatenate((total, squares, count, jnp.zeros((5, 128), jnp.float32)), 0)


def filter_frames(gated, packs, taps_count, lengths):
    span, width = gated.shape
    return pl.pallas_call(
        functools.partial(filter_kernel, taps_count),
        out_shape=[
            jax.ShapeDtypeStruct((span, width), jnp.float32),
            jax.ShapeDtypeStruct((8, width), jnp.float32),
        ],
        grid_spec=pltpu.PrefetchScalarGridSpec(
            num_scalar_prefetch=1,
            grid=(width // 128,),
            in_specs=[
                pl.BlockSpec((span, 128), lambda c, *_: (0, c)),
                pl.BlockSpec((packs.shape[0] // 4, 128), lambda c, *_: (c, 0)),
            ],
            out_specs=[
                pl.BlockSpec((span, 128), lambda c, *_: (0, c)),
                pl.BlockSpec((8, 128), lambda c, *_: (0, c)),
            ],
            scratch_shapes=[pltpu.VMEM((span + 2 * HALO, 128), jnp.float32)],
        ),
        cost_estimate=pl.CostEstimate(
            flops=64 * span * width, bytes_accessed=6 * span * width, transcendentals=0
        ),
        name="filter_frames",
    )(lengths, gated, packs)


def filter_turned(taps_count, padded, packs, first, out_ref, cut):
    span = out_ref.shape[0]

    def chunk(c, carry):
        at = pl.multiple_of(c * CHUNK, CHUNK)
        value = jnp.zeros((CHUNK, 128), jnp.float32)
        for k, window in tap_windows(padded, at, taps_count):
            turned = first + taps_count - 1 - k
            value = value + window * packs[turned : turned + 1, :]
        out_ref[pl.ds(at, CHUNK), cut] = value.astype(jnp.bfloat16)
        return carry

    lax.fori_loop(0, span // CHUNK, chunk, 0)


def filter_taps(taps_count, span, padded, gpadded, held):
    def tally(c, sums):
        at = pl.multiple_of(c * CHUNK, CHUNK)
        grad = padded[pl.ds(at + HALO, CHUNK), :]
        added = list(sums)
        for k, window in tap_windows(gpadded, at, taps_count):
            term = grad * window
            folded = term[0:8]
            for r in range(8, CHUNK, 8):
                folded = folded + term[r : r + 8]
            added[k] = added[k] + folded
        return tuple(added)

    blank = tuple(jnp.zeros((8, 128), jnp.float32) for _ in range(taps_count))
    sums = lax.fori_loop(0, span // CHUNK, tally, blank)
    rest = jnp.zeros((held - taps_count, 128), jnp.float32)
    return jnp.concatenate([column_sum(x) for x in sums] + [rest], 0)


def dot_tn(a, b):
    return lax.dot_general(a, b, (((0,), (0,)), ((), ())), preferred_element_type=jnp.float32)


def sigmoid(x):
    return 0.5 * jnp.tanh(0.5 * x) + 0.5


def silu_parts(x):
    s = sigmoid(x)
    value = x * s
    return value, s + value * (1.0 - s)


def normed_parts(x):
    centred = x - jnp.mean(x, -1, keepdims=True)
    scale = lax.rsqrt(jnp.mean(centred * centred, -1, keepdims=True) + EPSILON)
    return centred * scale, scale


def normed_back(n, scale, e):
    return scale * (e - jnp.mean(e, -1, keepdims=True) - n * jnp.mean(e * n, -1, keepdims=True))


def column_sum(x):
    return jnp.sum(x, axis=0, keepdims=True)


def add_rows(ref, rows):
    @pl.when(pl.program_id(0) == 0)
    def _():
        ref[...] = jnp.zeros_like(ref)

    width = ref.shape[1]
    ref[...] += jnp.concatenate(list(rows) + [jnp.zeros((8 - len(rows), width), jnp.float32)], 0)


def row_call(kernel, name, scalars, tall, whole, outs, sums, block, flops):
    span = tall[0].shape[0]

    def rows(columns):
        return pl.BlockSpec((block, columns), lambda i, *_: (i, 0))

    def kept(x, at):
        return pl.BlockSpec(x.shape, lambda i, *_: (0, at), pipeline_mode=pl.Buffered(1))

    cuts = [x if isinstance(x, tuple) else (x, x.shape[1], 0) for x in whole]
    specs = [kept(jax.ShapeDtypeStruct((x.shape[0], w), x.dtype), at) for x, w, at in cuts]
    whole = [x for x, _, _ in cuts]
    width = tall[0].shape[1]
    moved = sum(x.size * x.dtype.itemsize for x in tall + whole)
    moved += sum(span * c * jnp.dtype(d).itemsize for c, d in outs)
    return pl.pallas_call(
        kernel,
        out_shape=[jax.ShapeDtypeStruct((span, c), d) for c, d in outs]
        + [jax.ShapeDtypeStruct((8, width), jnp.float32)] * sums,
        grid_spec=pltpu.PrefetchScalarGridSpec(
            num_scalar_prefetch=1,
            grid=(span // block,),
            in_specs=[rows(x.shape[1]) for x in tall] + specs,
            out_specs=[rows(c) for c, _ in outs]
            + [pl.BlockSpec((8, width), lambda i, *_: (0, 0))] * sums,
        ),
        compiler_params=pltpu.CompilerParams(vmem_limit_bytes=60 << 20),
        cost_estimate=pl.CostEstimate(
            flops=flops * span, bytes_accessed=moved, transcendentals=span * 2048
        ),
        name=name,
    )(scalars, *tall, *whole)


def head_columns(ref, which, width):
    return ref[:, pl.ds(pl.multiple_of(which * width, width), width)]


def head_rows(ref, which, width):
    return ref[pl.ds(pl.multiple_of(which * width, width), width), :]


def expand_kernel(
    scalars, own_ref, far_ref, after_ref, packs, w_output, w_expand,
    after_out, normed_out, gated_out, slope_out,
):
    core, length = lax.rem(lax.axis_index("slots"), 2), scalars[0]
    block, half = own_ref.shape
    after = (
        after_ref[...]
        + dot_nn(own_ref[...], head_rows(w_output, core, half))
        + dot_nn(far_ref[...], head_rows(w_output, 1 - core, half))
    )
    after_out[...] = after
    n, _ = normed_parts(after)
    normed = (n * param(packs, CONV)).astype(jnp.bfloat16)
    normed_out[...] = normed
    expand = dot_nn(normed, w_expand[...])
    width = expand.shape[1] // 2
    row = lax.broadcasted_iota(jnp.int32, (block, width), 0) + pl.program_id(0) * block
    gate = sigmoid(expand[:, width:])
    live = jnp.where(row < length, gate, 0.0)
    gated = expand[:, :width] * live
    gated_out[...] = gated.astype(jnp.bfloat16)
    slope_out[:, :width] = live.astype(jnp.bfloat16)
    slope_out[:, width:] = (gated * (1.0 - gate)).astype(jnp.bfloat16)


def spread_parts(shared, packs):
    frames = frame_count(packs)
    return shared[0:1, :] / frames, lax.rsqrt(shared[1:2, :] / frames + EPSILON)


def back_kernel(
    scalars, filtered_ref, after_ref, cot_ref, shared, packs, w_project, w_in, w_out,
    output_out, grad_out, dbn_out, swish_out, top_out, hidden_out, dpre_out, normed_out, half_out,
    sums,
):
    middle, inverse = spread_parts(shared, packs)
    back_gain, final_gain = param(packs, BACK), param(packs, FINAL)
    unit = (filtered_ref[...] - middle) * inverse
    value, slope_bn = silu_parts(unit * param(packs, BATCH) + param(packs, BIAS))
    swish = value.astype(jnp.bfloat16)
    swish_out[...] = swish
    after_conv = after_ref[...] + dot_nn(swish, w_project[...])
    n1, r1 = normed_parts(after_conv)
    normed = (n1 * back_gain).astype(jnp.bfloat16)
    normed_out[...] = normed
    value, slope = silu_parts(dot_nn(normed, w_in[...]))
    hidden = value.astype(jnp.bfloat16)
    hidden_out[...] = hidden
    n2, r2 = normed_parts(after_conv + 0.5 * dot_nn(hidden, w_out[...]))
    output_out[...] = (n2 * final_gain).astype(jnp.bfloat16)

    cot = cot_ref[...].astype(jnp.float32)
    grad = normed_back(n2, r2, cot * final_gain)
    half_grad = (0.5 * grad).astype(jnp.bfloat16)
    half_out[...] = half_grad
    dpre = (dot_nt(half_grad, w_out[...]) * slope).astype(jnp.bfloat16)
    dpre_out[...] = dpre
    dnormed = dot_nt(dpre, w_in[...])
    grad = grad + normed_back(n1, r1, dnormed * back_gain)
    grad_out[...] = grad
    top = grad.astype(jnp.bfloat16)
    top_out[...] = top
    dbn = dot_nt(top, w_project[...]) * slope_bn
    dbn_out[...] = dbn
    add_rows(
        sums,
        [column_sum(dbn), column_sum(dbn * unit), column_sum(cot * n2), column_sum(dnormed * n1)],
    )


CORE_PACE, PAIR_PACE = 1.5, 25.0
HOP = 4.0
CHUNK_BUFFERS = 8
DIRECT_FROM = 4
STAGES = 8


def chunk_scratch(chunks):
    dma = pltpu.SemaphoreType.DMA
    scratch = []
    for r, w, kind, direct in chunks:
        shapes = [(2, r, w), (2, r, w), (2, r, w), (r, w), (r // 2, w), (r // 4, w), (r // 8, w), (r, w)]
        if direct:
            shapes[4:7] = [(7, r // 8, w), (8, w), (8, w)]
        scratch += [pltpu.VMEM(shape, kind) for shape in shapes]
    n = len(chunks)
    return scratch + [dma((n, STAGES + 14)), dma((n, STAGES + 14))]


class Flow:
    def __init__(self, chunks, refs, finish, stages=None):
        count = len(chunks)
        self.stages = stages or [4 if chunk[3] else STAGES for chunk in chunks]
        self.others = [{"tm": lax.rem(lax.axis_index("tm") + k, 8)} for k in range(1, 8)]
        self.chunks, self.finish = chunks, finish
        self.buffers = [refs[CHUNK_BUFFERS * c : CHUNK_BUFFERS * (c + 1)] for c in range(count)]
        self.send_sems, self.recv_sems = refs[CHUNK_BUFFERS * count :]
        me, n = lax.axis_index("tm"), lax.axis_size("tm")
        s = lax.axis_index("slots")
        self.core, self.y = lax.rem(s, 2), lax.div(s, 2)
        self.x, self.z = lax.rem(me, 2), lax.div(me, 2)
        self.sibling, self.across = {"slots": s + 1 - 2 * self.core}, {"slots": lax.rem(s + 2, 4)}
        self.beside = {"tm": me + 1 - 2 * self.x}
        self.low, self.high = lax.rem(self.z, 2), lax.div(self.z, 2)
        self.next, self.beyond = {"tm": me + 2 - 4 * self.low}, {"tm": me + 4 - 8 * self.high}
        self.sent = []
        self.going = {}
        self.clock, self.waiting, self.busy = 0.0, [], {}

    def put(self, c, y, even, odd):
        send, total = self.buffers[c][0], self.buffers[c][1]
        total[y] = jnp.where(self.core == 0, even, odd)
        send[y] = jnp.where(self.core == 0, odd, even)

    def put_all(self, c, terms):
        for y in range(2):
            self.put(c, y, terms[2 * y], terms[2 * y + 1])

    def stage(self, c, k):
        send, total, core_in, y_in, x_in, low_in, high_in, final = self.buffers[c]
        r, _, kind, direct = self.chunks[c]
        x, y, low, high = self.x, self.y, self.low, self.high
        me = lax.axis_index("tm")

        def add(ref, place, arrived):
            value = ref[place].astype(jnp.float32) + arrived.astype(jnp.float32)
            return value.astype(kind)

        def part(start, rows):
            return pl.ds(pl.multiple_of(start, rows), rows)

        half, quarter, piece = r // 2, r // 4, r // 8
        at_half = x * half
        at_quarter = at_half + low * quarter
        at_piece = at_quarter + high * piece
        if k:
            for copy in self.going[c]:
                copy.wait_recv()
        if k == 0:
            copy = (send, core_in, self.sibling)
        elif k == 1:
            for i in range(2):
                total[i] = add(total, i, core_in[i])
            copy = (total.at[1 - y], y_in, self.across)
        elif k == 2:
            total[y] = add(total, y, y_in[...])
            copy = (total.at[y, part((1 - x) * half, half)], x_in, self.beside)
        elif direct and k == 3:
            mine = part(me * piece, piece)
            value = total[y, mine].astype(jnp.float32)
            for i in range(7):
                value = value + x_in[i].astype(jnp.float32)
            final[mine] = value.astype(kind)
        elif direct:
            pass
        elif k == 3:
            mine = (y, part(at_half, half))
            total[mine] = add(total, mine, x_in[...])
            copy = (total.at[y, part(at_half + (1 - low) * quarter, quarter)], low_in, self.next)
        elif k == 4:
            mine = (y, part(at_quarter, quarter))
            total[mine] = add(total, mine, low_in[...])
            copy = (total.at[y, part(at_quarter + (1 - high) * piece, piece)], high_in, self.beyond)
        elif k == 5:
            mine = part(at_piece, piece)
            final[mine] = add(total, (y, mine), high_in[...])
            copy = (final.at[mine], final.at[mine], self.beyond)
        elif k == 6:
            mine = part(at_quarter, quarter)
            copy = (final.at[mine], final.at[mine], self.next)
        elif k == 7:
            mine = part(at_half, half)
            copy = (final.at[mine], final.at[mine], self.beside)
        if k == self.stages[c]:
            return
        if direct and k >= 2:
            copies, first = [], STAGES + 7 * (k - 2)
            for i, where in enumerate(self.others):
                if k == 2:
                    source, target = total.at[y, part(lax.rem(me + i + 1, 8) * piece, piece)], x_in.at[i]
                else:
                    source = target = final.at[part(me * piece, piece)]
                sems = self.send_sems.at[c, first + i], self.recv_sems.at[c, first + i]
                copies.append(remote(source, target, *sems, where))
        else:
            source, target, where = copy
            copies = [remote(source, target, self.send_sems.at[c, k], self.recv_sems.at[c, k], where)]
        for copy in copies:
            copy.start()
        self.sent += copies
        self.going[c] = copies

    def occupy(self, link, time):
        self.busy[link] = max(self.busy.get(link, 0.0), self.clock) + time
        return self.busy[link] + HOP

    def step(self, c, k):
        self.stage(c, k)
        r, w, kind, direct = self.chunks[c]
        size = r * w * jnp.dtype(kind).itemsize / 1e6
        half, quarter, piece = (size / cut * PAIR_PACE for cut in (2, 4, 8))
        pace = (
            ("core", 2 * size * CORE_PACE), ("y", size * PAIR_PACE), ("x", half), ("z", quarter),
            ("z", 2 * piece), ("z", 2 * piece), ("z", quarter), ("x", half),
        )
        if direct:
            pace = pace[:2] + (("z", size * PAIR_PACE),) * 2
        if k < self.stages[c]:
            self.waiting.append((self.occupy(*pace[k]), c, k + 1))
        else:
            self.finish(c, self.buffers[c])
        self.clock += size

    def begin(self, c):
        self.step(c, 0)

    def spend(self, time):
        self.clock += time
        while self.waiting and min(self.waiting)[0] <= self.clock:
            first = min(self.waiting)
            self.waiting.remove(first)
            self.step(*first[1:])

    def drain(self):
        while self.waiting:
            self.spend(max(min(self.waiting)[0] - self.clock, 0.0))
        for copy in self.sent:
            copy.wait_send()


def greet(places):
    barrier = pltpu.get_barrier_semaphore()
    for place in places:
        pl.semaphore_signal(barrier, inc=1, device_id=place, device_id_type=MESH)
    pl.semaphore_wait(barrier, len(places))


class Named:
    def __init__(self, names, refs):
        self.__dict__.update(zip(names, refs))


def named_call(kernel, name, inputs, outputs, scratch, extra, collective_id, flops):
    names = [*inputs, *outputs, *scratch]

    def body(*refs):
        kernel(Named(names, refs), refs[len(names) :])

    results = pl.pallas_call(
        body,
        out_shape=[jax.ShapeDtypeStruct(shape, kind) for shape, kind, _ in outputs.values()],
        in_specs=[pl.BlockSpec(memory_space=space) for _, space in inputs.values()],
        out_specs=[pl.BlockSpec(memory_space=space) for _, _, space in outputs.values()],
        scratch_shapes=[*scratch.values(), *extra],
        compiler_params=pltpu.CompilerParams(
            collective_id=collective_id,
            has_side_effects=collective_id is not None,
            vmem_limit_bytes=62 << 20,
        ),
        cost_estimate=pl.CostEstimate(
            flops=flops, bytes_accessed=sum(2 * x.size for x, _ in inputs.values()), transcendentals=0
        ),
        name=name,
    )(*(x for x, _ in inputs.values()))
    return Named(outputs, results)


class Stream:
    def __init__(self, sources, slots, semaphores, blocks):
        self.copies = [
            [
                pltpu.make_async_copy(ref.at[block], held.at[i % 2], semaphores.at[i % 2, j])
                for j, (ref, held) in enumerate(zip(sources, slots))
            ]
            for i, block in enumerate(blocks)
        ]

    def begin(self, i):
        if i < len(self.copies):
            for copy in self.copies[i]:
                copy.start()

    def take(self, i):
        self.begin(i + 1)
        for copy in self.copies[i]:
            copy.wait()


WEIGHTS = ("pack", "w_in", "w_out", "w_query", "w_key", "w_value")
PAIR_ORDER = (0, 1, 3, 2)


def opening_kernel(r, _):
    me, n = lax.axis_index("tm"), lax.axis_size("tm")
    s = lax.axis_index("slots")
    core, x, z = lax.rem(s, 2), lax.rem(me, 2), lax.div(me, 2)
    sibling, across = {"slots": s + 1 - 2 * core}, {"slots": lax.rem(s + 2, 4)}
    theirs, beside = lax.rem(s + 2, 4), {"tm": me + 1 - 2 * x}
    frames = r.feats.shape[1]
    span, width = r.x.shape
    half = width // 2
    shards = [getattr(r, name) for name in WEIGHTS]
    fulls = [getattr(r, "full_" + name) for name in WEIGHTS]
    greet([{"tm": lax.rem(me + k, n)} for k in range(1, n)] + [sibling, across])

    def part(i, owner, piece=None):
        rows = shards[i].shape[0]
        if piece is None:
            return fulls[i].at[pl.ds(pl.multiple_of(owner * rows, rows), rows)]
        size = rows // 2
        return fulls[i].at[pl.ds(pl.multiple_of(owner * rows + piece * size, size), size)]

    def link(kind, i, source, target, where):
        copy = remote(source, target, r.w_send.at[i, kind], r.w_recv.at[i, kind], where)
        copy.start()
        return copy

    count = len(WEIGHTS)
    y_copies, c_copies, b_copies, f_copies, g_copies, locals_ = [], [], {}, [], {}, []
    for i in range(count):
        if i == 0:
            y_copies.append(link(0, i, shards[i], part(i, s), across))
        else:
            size = shards[i].shape[0] // 2
            source = shards[i].at[pl.ds(pl.multiple_of(x * size, size), size)]
            y_copies.append(link(0, i, source, part(i, s, x), across))
    rows_copies = {}
    for k in PAIR_ORDER:
        for j in range(2):
            to = 2 * lax.rem(z + 4 - k, 4) + lax.rem(x + j, 2)
            target = r.x.at[pl.ds(pl.multiple_of(me * frames, frames), frames)]
            sems = r.x_send.at[2 * k + j], r.x_recv.at[2 * k + j]
            if k == 0 and j == 0:
                copy = pltpu.make_async_copy(r.feats.at[me], target, sems[0])
            else:
                copy = remote(r.feats.at[to], target, *sems, {"tm": to})
            copy.start()
            rows_copies[k, j] = copy
    for i in range(count):
        c_copies.append(link(1, i, shards[i], part(i, s), sibling))
        locals_.append(pltpu.make_async_copy(shards[i], part(i, s), r.w_local.at[i]))
        locals_[-1].start()
    for i in range(count):
        y_copies[i].wait_recv()
        piece = None if i == 0 else x
        block = part(i, theirs, piece)
        if i:
            b_copies[i] = link(2, i, block, block, beside)
        f_copies.append(link(3, i, block, block, sibling))

    def complete(i):
        if i:
            b_copies[i].wait_recv()
            block = part(i, theirs, 1 - x)
            g_copies[i] = link(4, i, block, block, sibling)
        c_copies[i].wait_recv()
        f_copies[i].wait_recv()
        locals_[i].wait()

    def received(i):
        if i:
            g_copies[i].wait_recv()
        store = pltpu.make_async_copy(fulls[i], getattr(r, "out_" + WEIGHTS[i]), r.w_local.at[i])
        store.start()
        stores.append(store)

    stores, outgoing, block_stores = [], [], []
    for i in range(3):
        complete(i)
    for i in range(3):
        received(i)
    packs, w_in, w_out, wq, wk, wv = fulls
    rows = packs.shape[0] // 4
    near = packs[pl.ds(pl.multiple_of((s + 1 - 2 * core) * rows + rows - 8, 8), 8), :]
    r.lengths[0] = r.length[0]
    r.lengths[1] = jnp.max(near[6:7, :]).astype(jnp.int32)
    for step, k in enumerate(PAIR_ORDER):
        for j in range(2):
            copy = rows_copies[k, j]
            if k == 0 and j == 0:
                copy.wait()
            else:
                copy.wait_recv()
        slot = step % 2
        place = pl.ds(pl.multiple_of(lax.rem(z + k, 4) * 2 * frames, 2 * frames), 2 * frames)
        if step >= 2:
            for copy in block_stores[step - 2]:
                copy.wait()
        rows = r.x[place].astype(jnp.float32)
        normed, _ = normed_parts(rows)
        normed = (normed * param(packs, FRONT)).astype(jnp.bfloat16)
        r.slot_normed[slot] = normed
        value, slope = silu_parts(dot_nn(normed, w_in[...]))
        hidden = value.astype(jnp.bfloat16)
        r.slot_hidden[slot] = hidden
        r.slot_slope[slot] = slope.astype(jnp.bfloat16)
        after = rows + 0.5 * dot_nn(hidden, w_out[...])
        r.slot_after[slot] = after
        mixer, _ = normed_parts(after)
        mixer = (mixer * param(packs, MIXER)).astype(jnp.bfloat16)
        r.slot_mixer[slot] = mixer
        if step == 0:
            for i in range(3, count):
                complete(i)
            for i in range(3, count):
                received(i)
        for j, w in enumerate((wq, wk, wv)):
            lanes = slice(j * half, (j + 1) * half)
            r.far[place, lanes] = dot_nn(mixer, head_columns(w, 1 - core, half)).astype(jnp.bfloat16)
        outgoing.append(
            remote(
                r.far.at[place], r.near_qkv.at[place], r.far_send.at[step], r.far_recv.at[step],
                sibling,
            )
        )
        outgoing[-1].start()
        for j, w in enumerate((wq, wk, wv)):
            lanes = slice(j * half, (j + 1) * half)
            r.slot_own[slot, :, lanes] = dot_nn(mixer, head_columns(w, core, half)).astype(jnp.bfloat16)
        block_stores.append([
            pltpu.make_async_copy(source, target.at[place], r.store.at[slot, j])
            for j, (source, target) in enumerate((
                (r.x.at[place], r.rows),
                (r.slot_normed.at[slot], r.normed),
                (r.slot_hidden.at[slot], r.hidden),
                (r.slot_slope.at[slot], r.slope),
                (r.slot_after.at[slot], r.after),
                (r.slot_mixer.at[slot], r.mixer),
                (r.slot_own.at[slot], r.own_qkv),
            ))
        ])
        for copy in block_stores[-1]:
            copy.start()
    for copy in outgoing + stores + block_stores[-2] + block_stores[-1]:
        copy.wait()
    for copy in [*y_copies, *c_copies, *f_copies, *b_copies.values(), *g_copies.values()]:
        copy.wait_send()
    for place, copy in rows_copies.items():
        if place != (0, 0):
            copy.wait_send()


def opening(feats, length, shards, collective_id):
    bf16, f32 = jnp.bfloat16, jnp.float32
    anywhere, vmem = pl.ANY, pltpu.VMEM
    dma = pltpu.SemaphoreType.DMA
    n, frames, width = feats.shape
    span, pair = n * frames, 2 * frames
    ff = shards["w_in"].shape[1]
    half = width // 2
    inputs = {"feats": (feats, anywhere), "length": (length, pltpu.SMEM)}
    inputs |= {name: (shards[name], vmem) for name in WEIGHTS}
    whole = {name: (4 * shards[name].shape[0], shards[name].shape[1]) for name in WEIGHTS}
    tall = dict(normed=(width, bf16), hidden=(ff, bf16), slope=(ff, bf16), after=(width, f32))
    tall |= dict(mixer=(width, bf16), own_qkv=(3 * half, bf16))
    outputs = {"rows": ((span, width), bf16, anywhere), "near_qkv": ((span, 3 * half), bf16, anywhere)}
    outputs |= {name: ((span, columns), kind, anywhere) for name, (columns, kind) in tall.items()}
    outputs |= {"out_" + name: (whole[name], shards[name].dtype, anywhere) for name in WEIGHTS}
    outputs |= {"lengths": ((2,), jnp.int32, pltpu.SMEM)}
    scratch = {"full_" + name: vmem(whole[name], shards[name].dtype) for name in WEIGHTS}
    scratch |= {
        "slot_" + name.split("_")[0]: vmem((2, pair, columns), kind)
        for name, (columns, kind) in tall.items()
    }
    count = len(WEIGHTS)
    scratch |= {
        "x": vmem((span, width), bf16),
        "far": vmem((span, 3 * half), bf16),
        "w_send": dma((count, 5)),
        "w_recv": dma((count, 5)),
        "w_local": dma((count,)),
        "x_send": dma((n,)),
        "x_recv": dma((n,)),
        "far_send": dma((4,)),
        "far_recv": dma((4,)),
        "store": dma((2, 7)),
    }
    return named_call(
        opening_kernel, "opening", inputs, outputs, scratch, [], collective_id,
        span * (4 * width * ff + 6 * width * width),
    )


ROWS = 256


def middle_kernel(chunks, taps_count, r, flow_refs):
    t, s = lax.axis_index("tm"), lax.axis_index("slots")
    n, m = lax.axis_size("tm"), lax.axis_size("slots")
    span, width = r.half.shape
    shard = width // 4
    quarter, half = r.hidden.shape[1] // 4, width // 2
    back_chunks = len(chunks) - 3
    length = r.length[0]
    core = lax.rem(s, 2)
    others = pltpu.make_async_copy(r.others, r.held_others, r.load.at[6])
    others.start()
    wanted = ("half", "hidden", "normed", "dpre", "swish", "top")
    loads = {
        name: pltpu.make_async_copy(getattr(r, name), getattr(r, "held_" + name), r.load.at[i])
        for i, name in enumerate(wanted)
    }
    for load in loads.values():
        load.start()
    everything = slice(None)
    columns = Stream(
        [r.filtered, r.dbn, r.gated],
        [r.filtered_slots, r.dbn_slots, r.gated_slots],
        r.column_load,
        [(everything, slice(128 * c, 128 * c + 128)) for c in range(width // 128)],
    )
    rows = Stream(
        [r.glu_slope, r.grad, r.after],
        [r.slope_slots, r.grad_slots, r.after_slots],
        r.row_load,
        [(slice(i * ROWS, (i + 1) * ROWS), everything) for i in range(span // ROWS)],
    )
    columns.begin(0)
    rows.begin(0)

    slot_places = [{"slots": lax.rem(s + k, m)} for k in range(1, m)]
    tm_places = [{"tm": lax.rem(t + k, n)} for k in range(1, n)]
    greet(slot_places + tm_places)

    def share(source, landing, places, first):
        copies = [
            remote(source, landing.at[i], r.stat_send.at[first + i], r.stat_recv.at[first + i], place)
            for i, place in enumerate(places)
        ]
        for copy in copies:
            copy.start()
        return copies

    def gathered(copies, source, landing):
        for copy in copies:
            copy.wait()
        return add_blocks([source[...]] + [landing[i] for i in range(len(copies))])

    held = {}

    def need(name):
        if name not in held:
            loads[name].wait()
            held[name] = getattr(r, "held_" + name)
        return held[name]

    def finish(c, buffers):
        if c >= back_chunks:
            cut = slice((c - back_chunks) * shard, (c - back_chunks + 1) * shard)
            r.part_middle[cut] = buffers[1][flow.y]
            return
        value = buffers[-1][...].astype(jnp.float32)
        if c < 2:
            rows_here = chunks[0][0]
            r.part_out[c * rows_here : (c + 1) * rows_here] = value
        elif c < back_chunks - 1:
            r.part_in[:, (c - 2) * width : (c - 1) * width] = value
        else:
            r.part_project[...] = value

    flow = Flow(chunks, flow_refs, finish, [STAGES] * back_chunks + [2] * (len(chunks) - back_chunks))

    def make(c):
        if c < 2:
            a, b = need("hidden"), need("half")
            rows_here = chunks[0][0]
            terms = []
            for o in range(4):
                at = o * quarter + c * rows_here
                terms.append(dot_tn(a[:, at : at + rows_here], b[...]).astype(jnp.bfloat16))
        elif c < back_chunks - 1:
            b = need("dpre")[:, (c - 2) * width : (c - 1) * width]
            terms = dot_tn(need("normed")[...], b).astype(jnp.bfloat16).reshape(4, shard, width)
        else:
            terms = dot_tn(need("swish")[...], need("top")[...]).astype(jnp.bfloat16)
            terms = terms.reshape(4, shard, width)
        flow.put_all(c, terms)
        flow.begin(c)
        flow.spend(2.6 if c < 2 else 1.4)

    first = share(r.sums_in, r.stat_near, slot_places, 0)
    make(0)
    r.stat_mid[...] = gathered(first, r.sums_in, r.stat_near)
    second = share(r.stat_mid, r.stat_far, tm_places, m - 1)
    make(1)
    make(2)
    r.sums_out[...] = gathered(second, r.stat_mid, r.stat_far)
    for c in range(3, back_chunks):
        make(c)
    later = [
        pltpu.make_async_copy(source, target, r.load.at[i])
        for i, (source, target) in enumerate((
            (r.conv_normed, r.held_normed),
            (r.own_att, r.held_half.at[:, 0:half]),
            (r.far_att, r.held_half.at[:, half:width]),
        ))
    ]
    for copy in later:
        copy.start()

    means, inverses = spread_parts(r.shared, r.packs)
    batch_gain, conv_gain, frames = param(r.packs, BATCH), param(r.packs, CONV), frame_count(r.packs)
    pack_rows = r.packs.shape[0] // 4
    halo = jnp.zeros((HALO, 128), jnp.float32)
    for ref in (r.padded, r.gpadded):
        ref[0:HALO] = halo
        ref[HALO + span : HALO + span + HALO] = halo
    for c in range(width // 128):
        columns.take(c)
        cut = slice(128 * c, 128 * c + 128)
        middle, inverse, gain = means[:, cut], inverses[:, cut], batch_gain[:, cut]
        shift_sum, scale_sum = r.sums_out[0:1, cut], r.sums_out[1:2, cut]
        r.gpadded[HALO : HALO + span] = r.gated_slots[c % 2].astype(jnp.float32)
        row = lax.broadcasted_iota(jnp.int32, (span, 128), 0)
        unit = (r.filtered_slots[c % 2] - middle) * inverse
        shift = (gain * shift_sum + unit * (gain * scale_sum)) / frames[:, cut]
        r.padded[HALO : HALO + span] = inverse * (
            r.dbn_slots[c % 2] * gain - jnp.where(row < length, shift, 0.0)
        )
        filter_turned(taps_count, r.padded, r.packs, c * pack_rows + TAPS, r.held_swish, cut)
        flow.spend(2.3)
        r.grad_taps[:, cut] = filter_taps(taps_count, span, r.padded, r.gpadded, r.grad_taps.shape[0])
        flow.spend(2.7)

    others.wait()
    w_expand = r.held_others.at[:, 0 : 2 * width]
    w_output = r.held_others.at[:, 2 * width : 3 * width]
    conv_sum = jnp.zeros((1, width), jnp.float32)
    outgoing, stores = [], []
    for i in range(span // ROWS):
        rows.take(i)
        cut = slice(i * ROWS, (i + 1) * ROWS)
        if i >= 2:
            for copy in stores[i - 2]:
                copy.wait()
        dgated = r.held_swish[cut].astype(jnp.float32)
        slopes = r.slope_slots[i % 2].astype(jnp.float32)
        dexpand = jnp.concatenate((dgated * slopes[:, :width], dgated * slopes[:, width:]), 1)
        dexpand = dexpand.astype(jnp.bfloat16)
        r.held_dpre[cut, 0 : 2 * width] = dexpand
        dnormed = dot_nt(dexpand, w_expand[...])
        normed, scale = normed_parts(r.after_slots[i % 2])
        grad = r.grad_slots[i % 2] + normed_back(normed, scale, dnormed * conv_gain)
        r.grad_store[i % 2] = grad
        top = grad.astype(jnp.bfloat16)
        r.held_top[cut] = top
        r.far_rows[cut] = dot_nt(top, head_rows(w_output, 1 - core, half)).astype(jnp.bfloat16)
        outgoing.append(
            remote(
                r.far_rows.at[cut], r.near_grad.at[cut], r.far_send.at[i], r.far_recv.at[i],
                flow.sibling,
            )
        )
        outgoing[-1].start()
        r.own_slots[i % 2] = dot_nt(top, head_rows(w_output, core, half)).astype(jnp.bfloat16)
        conv_sum = conv_sum + column_sum(dnormed * normed)
        stores.append([
            pltpu.make_async_copy(source.at[i % 2], target.at[cut], r.store.at[i % 2, j])
            for j, (source, target) in enumerate((
                (r.grad_store, r.grad_out),
                (r.own_slots, r.own_grad),
            ))
        ])
        for copy in stores[-1]:
            copy.start()
        flow.spend(2.0)
    r.conv_sums[...] = jnp.concatenate((conv_sum, jnp.zeros((7, width), jnp.float32)), 0)
    for copy in later:
        copy.wait()
    for j in range(2):
        b = r.held_dpre[:, j * width : (j + 1) * width]
        terms = dot_tn(r.held_normed[...], b).astype(jnp.bfloat16).reshape(4, shard, width)
        flow.put_all(back_chunks + j, terms)
        flow.begin(back_chunks + j)
        flow.spend(1.6)
    for which, lanes in ((core, slice(0, half)), (1 - core, slice(half, width))):
        terms = dot_tn(r.held_half[:, lanes], r.held_top[...]).astype(jnp.bfloat16)
        flow.put(back_chunks + 2, which, terms[:shard], terms[shard:])
    flow.begin(back_chunks + 2)
    flow.drain()
    for copy in outgoing + [copy for group in stores[-2:] for copy in group]:
        copy.wait()


def middle(lengths, sums, shared, packs, taps_count, big, collective_id):
    bf16, f32 = jnp.bfloat16, jnp.float32
    anywhere, vmem = pl.ANY, pltpu.VMEM
    span, width = big["half"].shape
    ff = big["hidden"].shape[1]
    shard, quarter, half = width // 4, ff // 4, width // 2
    n, m = lax.axis_size("tm"), lax.axis_size("slots")
    dma = pltpu.SemaphoreType.DMA
    chunks = [(quarter // 2, width, bf16, False)] * 2
    chunks += [(shard, width, bf16, False)] * (ff // width + 4)
    held_taps = -(-taps_count // 8) * 8
    inputs = {"length": (lengths, pltpu.SMEM), "sums_in": (sums, vmem)}
    inputs |= {"shared": (shared, vmem), "packs": (packs, vmem)}
    inputs |= {name: (x, anywhere) for name, x in big.items()}
    outputs = {
        "part_in": ((shard, ff), f32, vmem),
        "part_out": ((quarter, width), f32, vmem),
        "part_project": ((shard, width), f32, vmem),
        "sums_out": ((8, width), f32, vmem),
        "conv_sums": ((8, width), f32, vmem),
        "grad_taps": ((held_taps, width), f32, vmem),
        "part_middle": ((3 * shard, width), bf16, vmem),
        "grad_out": ((span, width), f32, anywhere),
        "own_grad": ((span, half), bf16, anywhere),
        "near_grad": ((span, half), bf16, anywhere),
    }
    scratch = {
        "held_" + name: vmem(big[name].shape, bf16)
        for name in ("half", "hidden", "normed", "dpre", "swish", "top")
    }
    scratch |= {
        "held_others": vmem(big["others"].shape, bf16),
        "load": dma((7,)),
        "filtered_slots": vmem((2, span, 128), f32),
        "dbn_slots": vmem((2, span, 128), f32),
        "gated_slots": vmem((2, span, 128), bf16),
        "column_load": dma((2, 3)),
        "slope_slots": vmem((2, ROWS, 2 * width), bf16),
        "grad_slots": vmem((2, ROWS, width), f32),
        "after_slots": vmem((2, ROWS, width), f32),
        "row_load": dma((2, 3)),
        "stat_near": vmem((m - 1, 8, width), f32),
        "stat_mid": vmem((8, width), f32),
        "stat_far": vmem((n - 1, 8, width), f32),
        "stat_send": dma((n + m - 2,)),
        "stat_recv": dma((n + m - 2,)),
        "padded": vmem((span + 2 * HALO, 128), f32),
        "gpadded": vmem((span + 2 * HALO, 128), f32),
        "grad_store": vmem((2, ROWS, width), f32),
        "own_slots": vmem((2, ROWS, half), bf16),
        "far_rows": vmem((span, half), bf16),
        "far_send": dma((span // ROWS,)),
        "far_recv": dma((span // ROWS,)),
        "store": dma((2, 2)),
    }
    return named_call(
        functools.partial(middle_kernel, chunks, taps_count), "middle", inputs, outputs, scratch,
        chunk_scratch(chunks), collective_id, span * (4 * ff * width + 8 * width * width),
    )


def closing_kernel(chunks, r, flow_refs):
    me, n = lax.axis_index("tm"), lax.axis_size("tm")
    core = lax.rem(lax.axis_index("slots"), 2)
    span, width = r.x.shape
    frames = span // n
    ff = r.hidden.shape[1]
    shard, quarter, half = width // 4, ff // 4, width // 2
    names = ("dq", "dk", "dv", "mixer", "hidden", "normed")
    loads = {
        name: pltpu.make_async_copy(getattr(r, name), getattr(r, "held_" + name), r.load.at[i])
        for i, name in enumerate(names)
    }
    for load in loads.values():
        load.start()
    x, z = lax.rem(me, 2), lax.div(me, 2)
    order = (2, 1, 3, 0)
    block = 2 * frames
    places = [pl.ds(pl.multiple_of(lax.rem(z + k, 4) * block, block), block) for k in order]
    rows = Stream(
        [r.grad, r.after, r.x, r.slope],
        [r.grad_slots, r.after_slots, r.x_slots, r.slope_slots],
        r.row_load,
        [(place, slice(None)) for place in places],
    )
    rows.begin(0)
    held = {}

    def need(name):
        if name not in held:
            loads[name].wait()
            held[name] = getattr(r, "held_" + name)
        return held[name]

    in_chunk = 3
    out_chunk = in_chunk + ff // width
    gain_chunk = len(chunks) - 1

    def finish(c, buffers):
        value = buffers[-1][...].astype(jnp.float32)
        if c < in_chunk:
            (r.part_query, r.part_key, r.part_value)[c][...] = value
        elif c < out_chunk:
            r.part_in[:, (c - in_chunk) * width : (c - in_chunk + 1) * width] = value
        elif c < gain_chunk:
            size = chunks[c][0]
            r.part_out[(c - out_chunk) * size : (c - out_chunk + 1) * size] = value
        else:
            r.part_gains[...] = value

    flow = Flow(chunks, flow_refs, finish)
    greet([{"tm": lax.rem(me + k, n)} for k in range(1, n)] + [flow.sibling, flow.across])
    heads = [
        remote(getattr(r, name), r.far.at[i], r.far_send.at[i], r.far_recv.at[i], flow.sibling)
        for i, name in enumerate(("near_dq", "near_dk", "near_dv"))
    ]
    for copy in heads:
        copy.start()

    sums = [jnp.zeros((1, width), jnp.float32)] * 2
    w_heads = (r.w_query, r.w_key, r.w_value)
    own_heads = [
        dot_tn(need("mixer")[...], need(name)[...]).astype(jnp.bfloat16)
        for name in ("dq", "dk", "dv")
    ]
    flow.spend(2.0)
    for i, own in enumerate(own_heads):
        heads[i].wait_recv()
        far = dot_tn(need("mixer")[...], r.far[i]).astype(jnp.bfloat16)
        total = jnp.concatenate(
            (jnp.where(core == 0, own, far), jnp.where(core == 0, far, own)), 1
        )
        flow.put_all(i, total.reshape(4, shard, width))
        flow.begin(i)
        flow.spend(1.2)

    sends = []
    for i, place in enumerate(places):
        rows.take(i)
        dnormed = None
        for j, name in enumerate(("dq", "dk", "dv")):
            for which, d in ((core, need(name)[place]), (1 - core, r.far[j, place])):
                term = dot_nt(d, head_columns(w_heads[j], which, half))
                dnormed = term if dnormed is None else dnormed + term
        normed, scale = normed_parts(r.after_slots[i % 2])
        sums[1] = sums[1] + column_sum(dnormed * normed)
        grad = r.grad_slots[i % 2] + normed_back(normed, scale, dnormed * param(r.packs, MIXER))
        half_grad = (0.5 * grad).astype(jnp.bfloat16)
        r.half_grad[place] = half_grad
        slope = r.slope_slots[i % 2].astype(jnp.float32)
        dpre = (dot_nt(half_grad, r.w_out[...]) * slope).astype(jnp.bfloat16)
        r.dpre[place] = dpre
        dnormed = dot_nt(dpre, r.w_in[...])
        normed, scale = normed_parts(r.x_slots[i % 2].astype(jnp.float32))
        sums[0] = sums[0] + column_sum(dnormed * normed)
        r.home_rows[place] = (
            grad + normed_back(normed, scale, dnormed * param(r.packs, FRONT))
        ).astype(jnp.bfloat16)
        for j in range(2):
            to = 2 * lax.rem(z + order[i], 4) + lax.rem(x + j, 2)
            source = r.home_rows.at[pl.ds(pl.multiple_of(to * frames, frames), frames)]
            sems = r.home_send.at[2 * i + j], r.home_recv.at[2 * i + j]
            if order[i] or j:
                sends.append(remote(source, r.home.at[me], *sems, {"tm": to}))
                flow.occupy("z", 4.5)
                flow.occupy("x", 2.2)
            else:
                sends.append(pltpu.make_async_copy(source, r.home.at[me], sems[0]))
            sends[-1].start()
        flow.spend(5.0)

    size = chunks[gain_chunk][0]
    rows_of = [sums[0], sums[1], r.conv_sums[0:1, :], r.back_sums[3:4, :], r.back_sums[2:3, :]]
    rows_of.append(r.grad_taps[...])
    rows_of.append(jnp.zeros((size - 5 - r.grad_taps.shape[0], width), jnp.float32))
    total = jnp.concatenate(rows_of, 0)
    terms = [total[:, o * shard : (o + 1) * shard] for o in range(4)]
    flow.put_all(gain_chunk, terms)
    flow.begin(gain_chunk)
    for j in range(gain_chunk - out_chunk):
        size = chunks[out_chunk + j][0]
        terms = []
        for o in range(4):
            at = o * quarter + j * size
            terms.append(
                dot_tn(need("hidden")[:, at : at + size], r.half_grad[...]).astype(jnp.bfloat16)
            )
        flow.put_all(out_chunk + j, terms)
        flow.begin(out_chunk + j)
        flow.spend(2.7)
    for j in range(ff // width):
        total = dot_tn(need("normed")[...], r.dpre[:, j * width : (j + 1) * width])
        flow.put_all(in_chunk + j, total.astype(jnp.bfloat16).reshape(4, shard, width))
        flow.begin(in_chunk + j)
        flow.spend(1.6)
    flow.drain()
    for copy in heads:
        copy.wait_send()
    for copy in sends:
        copy.wait()


def closing(packs, conv_sums, back_sums, grad_taps, weights, big, collective_id):
    bf16, f32 = jnp.bfloat16, jnp.float32
    anywhere, vmem = pl.ANY, pltpu.VMEM
    dma = pltpu.SemaphoreType.DMA
    span, width = big["x"].shape
    ff = big["hidden"].shape[1]
    n = lax.axis_size("tm")
    shard, quarter, half, frames = width // 4, ff // 4, width // 2, span // n
    chunks = [(shard, width, bf16, i >= 3 + DIRECT_FROM) for i in range(3 + ff // width)]
    chunks += [(quarter // 2, width, bf16, False)] * 2 + [(64, shard, f32, False)]
    inputs = {"packs": (packs, vmem), "conv_sums": (conv_sums, vmem)}
    inputs |= {"back_sums": (back_sums, vmem), "grad_taps": (grad_taps, vmem)}
    inputs |= {name: (x, vmem) for name, x in weights.items()}
    inputs |= {name: (x, anywhere) for name, x in big.items()}
    outputs = {
        "part_in": ((shard, ff), f32, vmem),
        "part_out": ((quarter, width), f32, vmem),
        "part_query": ((shard, width), f32, vmem),
        "part_key": ((shard, width), f32, vmem),
        "part_value": ((shard, width), f32, vmem),
        "part_gains": (chunks[-1][:2], f32, vmem),
        "home": ((n, frames, width), bf16, anywhere),
    }
    scratch = {
        "held_" + name: vmem(big[name].shape, bf16)
        for name in ("dq", "dk", "dv", "mixer", "hidden", "normed")
    }
    scratch |= {
        "load": dma((6,)),
        "grad_slots": vmem((2, 2 * frames, width), f32),
        "after_slots": vmem((2, 2 * frames, width), f32),
        "x_slots": vmem((2, 2 * frames, width), bf16),
        "slope_slots": vmem((2, 2 * frames, ff), bf16),
        "row_load": dma((2, 4)),
        "far": vmem((3, span, half), bf16),
        "far_send": dma((3,)),
        "far_recv": dma((3,)),
        "half_grad": vmem((span, width), bf16),
        "dpre": vmem((span, ff), bf16),
        "home_rows": vmem((span, width), bf16),
        "home_send": dma((n,)),
        "home_recv": dma((n,)),
    }
    return named_call(
        functools.partial(closing_kernel, chunks), "closing", inputs, outputs, scratch,
        chunk_scratch(chunks), collective_id, span * (8 * ff * width + 12 * width * width),
    )


def finish_kernel(taps_count, r, _):
    n = r.home.shape[0]
    slots = lax.axis_index("slots")
    shard = r.gains.shape[1]
    moved = [name for name in r.__dict__ if name.startswith("from_")]
    pairs = [(r.home.at[r.rank[u]], r.held_home.at[u], r.features.at[u]) for u in range(n)]
    pairs += [(r.parts.at[r.rank[u]], r.held_parts.at[u], r.output.at[u]) for u in range(n)]
    for name in moved:
        bare = name[len("from_") :]
        pairs.append((getattr(r, name), getattr(r, "held_" + bare), getattr(r, "to_" + bare)))
    loads = [pltpu.make_async_copy(a, b, r.load.at[i]) for i, (a, b, _) in enumerate(pairs)]
    stores = [pltpu.make_async_copy(b, c, r.store.at[i]) for i, (_, b, c) in enumerate(pairs)]
    for copy in loads:
        copy.start()
    for i, ref in enumerate((r.front_gain, r.mixer_gain, r.conv_gain, r.back_gain, r.final_gain)):
        ref[...] = r.gains[i : i + 1, :].reshape(shard)
    taps = jnp.transpose(r.gains[5:37, :])
    r.depth[...] = taps[:, :taps_count]
    lanes = pl.ds(pl.multiple_of(slots * shard, shard), shard)
    r.batch_bias[...] = r.sums[0:1, lanes].reshape(shard)
    r.batch_gain[...] = r.sums[1:2, lanes].reshape(shard)
    width = r.output_weight.shape[1]
    for j in range(2):
        r.expand[:, j * width : (j + 1) * width] = r.middle[j * shard : (j + 1) * shard].astype(jnp.float32)
    r.output_weight[...] = r.middle[2 * shard :].astype(jnp.float32)
    for before, after in zip(loads, stores):
        before.wait()
        after.start()
    for copy in stores:
        copy.wait()


def finish(rank, home, out_parts, gains, sums, middle, taps_count, parts):
    f32, vmem, anywhere = jnp.float32, pltpu.VMEM, pl.ANY
    dma = pltpu.SemaphoreType.DMA
    shard, width = gains.shape[1], middle.shape[1]
    inputs = {"rank": (rank, pltpu.SMEM), "home": (home, anywhere), "gains": (gains, vmem)}
    inputs |= {"sums": (sums, vmem), "middle": (middle, vmem), "parts": (out_parts, anywhere)}
    inputs |= {"from_" + name: (x, anywhere) for name, x in parts.items()}
    outputs = {"features": (home.shape, home.dtype, anywhere)}
    outputs |= {"output": (home.shape, home.dtype, anywhere)}
    outputs |= {
        name: ((shard,), f32, vmem)
        for name in ("front_gain", "mixer_gain", "conv_gain", "back_gain", "final_gain", "batch_bias", "batch_gain")
    }
    outputs |= {"depth": ((shard, taps_count), f32, vmem)}
    outputs |= {"expand": ((shard, 2 * width), f32, vmem), "output_weight": ((shard, width), f32, vmem)}
    outputs |= {"to_" + name: (x.shape, x.dtype, anywhere) for name, x in parts.items()}
    scratch = {"held_home": vmem(home.shape, home.dtype), "held_parts": vmem(home.shape, home.dtype)}
    scratch |= {"held_" + name: vmem(x.shape, x.dtype) for name, x in parts.items()}
    count = 2 * home.shape[0] + len(parts)
    scratch |= {"load": dma((count,)), "store": dma((count,))}
    return named_call(
        functools.partial(finish_kernel, taps_count), "finish", inputs, outputs, scratch, [], None, 0
    )


def with_halo(block, sides, width):
    for axis, dim in sides:
        count = lax.axis_size(axis)
        forward = [(i, i + 1) for i in range(count - 1)]
        backward = [(target, source) for source, target in forward]
        low = lax.ppermute(
            lax.slice_in_dim(block, block.shape[dim] - width, None, axis=dim), axis, forward
        )
        high = lax.ppermute(lax.slice_in_dim(block, 0, width, axis=dim), axis, backward)
        block = jnp.concatenate([low, block, high], axis=dim)
    return block


def layer_norm(inputs, norm_gain):
    centred = inputs - jnp.mean(inputs, -1, keepdims=True)
    spread = jnp.mean(centred * centred, -1, keepdims=True)
    return centred * lax.rsqrt(spread + EPSILON) * norm_gain


def norm_back(inputs, norm_gain, incoming):
    result, pullback = jax.vjp(layer_norm, inputs, norm_gain)
    return pullback(incoming)


def matmul(left_side, right_side):
    return jnp.dot(left_side, right_side, preferred_element_type=jnp.float32)


def matmul_tn(left_side, right_side):
    return lax.dot_general(
        left_side, right_side, (((0,), (0,)), ((), ())), preferred_element_type=jnp.float32
    )


def matmul_nt(left_side, right_side):
    return lax.dot_general(
        left_side, right_side, (((1,), (1,)), ((), ())), preferred_element_type=jnp.float32
    )


def silu_slope(inputs):
    sigmoid_gate = jax.nn.sigmoid(inputs)
    return sigmoid_gate * (1.0 + inputs * (1.0 - sigmoid_gate))


def feed_forward(residual_rows, norm_gain, w_in, w_out):
    normed = layer_norm(residual_rows, norm_gain).astype(jnp.bfloat16)
    before_act = matmul(normed, w_in)
    hidden = jax.nn.silu(before_act).astype(jnp.bfloat16)
    return (residual_rows + 0.5 * matmul(hidden, w_out), (normed, before_act, hidden))


def feed_back(residual_rows, norm_gain, w_in, w_out, kept, incoming):
    normed, before_act, hidden = kept
    grad_top = (0.5 * incoming).astype(jnp.bfloat16)
    grad_w_out = matmul_tn(hidden, grad_top)
    grad_before = (matmul_nt(grad_top, w_out) * silu_slope(before_act)).astype(jnp.bfloat16)
    grad_w_in = matmul_tn(normed, grad_before)
    grad_normed = matmul_nt(grad_before, w_in)
    grad_rows, grad_gain = norm_back(residual_rows, norm_gain, grad_normed)
    return (incoming + grad_rows, grad_gain, grad_w_in, grad_w_out)


def exchange(x, pairs=CORE_PAIRS):
    return lax.ppermute(x, "slots", pairs)


def on_device_fast(
    features, lengths, cotangent, front_gain, front_in, front_out, mixer_gain, query_weight,
    key_weight, value_weight, output_weight, conv_gain, expand_weight, depth_weight, batch_gain,
    batch_bias, project_weight, back_gain, back_in, back_out, final_gain,
):
    slot_count, frames_dev, width = features.shape
    full_length = slot_count * frames_dev
    head_dim = width // HEADS
    half = width // 2
    tm, slots = lax.axis_index("tm"), lax.axis_index("slots")
    core = lax.rem(slots, 2)
    shard = front_gain.shape[0]
    taps_count = depth_weight.shape[1]

    feats, cots, pack, others, rank, length = arrange(
        lengths, features, cotangent, [expand_weight, output_weight, project_weight],
        [front_gain, mixer_gain, conv_gain, batch_gain, batch_bias, back_gain, final_gain],
        depth_weight.astype(jnp.float32).T,
    )
    first = opening(
        feats, length,
        dict(pack=pack, w_in=front_in, w_out=front_out, w_query=query_weight, w_key=key_weight,
             w_value=value_weight),
        0,
    )
    packs = first.out_pack
    others, back_in, back_out, cots, _ = lax.optimization_barrier(
        (others, back_in, back_out, cots, packs)
    )
    gather = functools.partial(lax.all_gather, axis_name="slots", axis=0, tiled=True)
    full_others, full_back_in, full_back_out = gather(others), gather(back_in), gather(back_out)
    cot_rows = lax.all_to_all(cots, "tm", 0, 1, tiled=True)[0]

    bf16, f32 = jnp.bfloat16, jnp.float32
    ff = front_in.shape[1]
    own_att, near_att, own_qa, near_qa = attend(first.own_qkv, first.near_qkv, first.lengths)
    far_att = exchange(near_att)
    after_mixer, conv_normed, gated, glu_slope = row_call(
        expand_kernel, "expand", length, [own_att, far_att, first.after],
        [packs, (full_others, width, 2), (full_others, 2 * width, 0)],
        [(width, f32), (width, bf16), (width, bf16), (2 * width, bf16)],
        0, 512, 6 * width * width,
    )
    filtered, stats = filter_frames(gated, packs, taps_count, length)
    shared = share_stats(stats, merge_spreads, 1)
    (output_rows, grad_rows, dbn, swish, conv_top, back_hidden, back_dpre, back_normed, back_half,
     back_sums) = row_call(
        back_kernel, "back", length, [filtered, after_mixer, cot_rows],
        [shared, packs, (full_others, width, 3), full_back_in, full_back_out],
        [(width, bf16), (width, f32), (width, f32), (width, bf16), (width, bf16), (ff, bf16),
         (ff, bf16), (width, bf16), (width, bf16)],
        1, 384, 8 * width * ff + 4 * width * width,
    )
    mid = middle(
        length, back_sums, shared, packs, taps_count,
        dict(hidden=back_hidden, dpre=back_dpre, half=back_half, normed=back_normed, swish=swish,
             top=conv_top, filtered=filtered, dbn=dbn, gated=gated, glu_slope=glu_slope,
             grad=grad_rows, after=after_mixer, conv_normed=conv_normed, own_att=own_att,
             far_att=far_att, others=full_others),
        2,
    )
    output_rows, _ = lax.optimization_barrier((output_rows, mid.sums_out))
    parts = lax.all_to_all(
        output_rows.reshape(slot_count, frames_dev, width), "tm", 0, 0, tiled=True
    )
    part_middle = lax.psum(mid.part_middle, "tm")
    own_dqkv, near_dqkv = attend_back(
        (own_qa, first.own_qkv, mid.own_grad, own_att),
        (near_qa, first.near_qkv, mid.near_grad, near_att),
        first.lengths,
    )
    last = closing(
        packs, mid.conv_sums, back_sums, mid.grad_taps,
        dict(w_in=first.out_w_in, w_out=first.out_w_out, w_query=first.out_w_query,
             w_key=first.out_w_key, w_value=first.out_w_value),
        dict(dq=own_dqkv[0], dk=own_dqkv[1], dv=own_dqkv[2],
             near_dq=near_dqkv[0], near_dk=near_dqkv[1], near_dv=near_dqkv[2], mixer=first.mixer,
             hidden=first.hidden, normed=first.normed, grad=mid.grad_out, after=first.after,
             x=first.rows, slope=first.slope),
        3,
    )
    done = finish(
        rank, last.home, parts, last.part_gains, mid.sums_out, part_middle, taps_count,
        dict(front_in=last.part_in, front_out=last.part_out, query=last.part_query,
             key=last.part_key, value=last.part_value, project=mid.part_project,
             back_in=mid.part_in, back_out=mid.part_out),
    )
    return (
        done.output,
        done.features,
        done.front_gain,
        done.to_front_in,
        done.to_front_out,
        done.mixer_gain,
        done.to_query,
        done.to_key,
        done.to_value,
        done.output_weight,
        done.conv_gain,
        done.expand,
        done.depth,
        done.batch_gain,
        done.batch_bias,
        done.to_project,
        done.back_gain,
        done.to_back_in,
        done.to_back_out,
        done.final_gain,
    )


def on_device(features, *rest):
    whole = features.shape[0] == lax.axis_size("tm") and lax.axis_size("slots") == 4
    return (on_device_fast if whole else on_device_general)(features, *rest)


def on_device_general(
    features,
    lengths,
    cotangent,
    front_gain,
    front_in,
    front_out,
    mixer_gain,
    query_weight,
    key_weight,
    value_weight,
    output_weight,
    conv_gain,
    expand_weight,
    depth_weight,
    batch_gain,
    batch_bias,
    project_weight,
    back_gain,
    back_in,
    back_out,
    final_gain,
):
    gathered = (
        lax.all_gather(front_gain, "slots", axis=0, tiled=True),
        lax.all_gather(front_in, "slots", axis=0, tiled=True),
        lax.all_gather(front_out, "slots", axis=0, tiled=True),
        lax.all_gather(mixer_gain, "slots", axis=0, tiled=True),
        lax.all_gather(query_weight, "slots", axis=0, tiled=True),
        lax.all_gather(key_weight, "slots", axis=0, tiled=True),
        lax.all_gather(value_weight, "slots", axis=0, tiled=True),
        lax.all_gather(output_weight, "slots", axis=0, tiled=True),
        lax.all_gather(conv_gain, "slots", axis=0, tiled=True),
        lax.all_gather(expand_weight, "slots", axis=0, tiled=True),
        lax.all_gather(depth_weight, "slots", axis=0, tiled=True),
        lax.all_gather(batch_gain, "slots", axis=0, tiled=True),
        lax.all_gather(batch_bias, "slots", axis=0, tiled=True),
        lax.all_gather(project_weight, "slots", axis=0, tiled=True),
        lax.all_gather(back_gain, "slots", axis=0, tiled=True),
        lax.all_gather(back_in, "slots", axis=0, tiled=True),
        lax.all_gather(back_out, "slots", axis=0, tiled=True),
        lax.all_gather(final_gain, "slots", axis=0, tiled=True),
    )
    (
        full_front_gain,
        full_front_in,
        full_front_out,
        full_mixer_gain,
        full_query,
        full_key,
        full_value,
        full_output,
        full_conv_gain,
        full_expand,
        full_depth,
        full_batch_gain,
        full_batch_bias,
        full_project,
        full_back_gain,
        full_back_in,
        full_back_out,
        full_final_gain,
    ) = gathered
    front_norm_gain = full_front_gain.astype(jnp.float32)
    mixer_norm_gain = full_mixer_gain.astype(jnp.float32)
    conv_norm_gain = full_conv_gain.astype(jnp.float32)
    batch_scale = full_batch_gain.astype(jnp.float32)
    batch_shift = full_batch_bias.astype(jnp.float32)
    back_norm_gain = full_back_gain.astype(jnp.float32)
    final_norm_gain = full_final_gain.astype(jnp.float32)
    depth_taps = full_depth.astype(jnp.float32)
    slot_count, frames_dev, width = features.shape
    row_count = slot_count * frames_dev
    full_length = frames_dev * lax.axis_size("tm")
    head_dim = width // HEADS
    taps_count = full_depth.shape[1]
    half_width = taps_count // 2
    score_scale = 1.0 / math.sqrt(head_dim)
    head_numbers = jnp.arange(HEADS, dtype=jnp.int32)
    frame_index = lax.axis_index("tm") * frames_dev + jnp.arange(frames_dev, dtype=jnp.int32)
    frame_mask = (frame_index[None, :] < lengths[:, None]).astype(jnp.float32).reshape(row_count, 1)
    residual_rows = features.astype(jnp.float32).reshape(row_count, width)
    after_front, front_kept = feed_forward(
        residual_rows, front_norm_gain, full_front_in, full_front_out
    )
    mixer_normed = layer_norm(after_front, mixer_norm_gain).astype(jnp.bfloat16)
    query_rows = (
        matmul(mixer_normed, full_query).astype(jnp.bfloat16).reshape(slot_count, frames_dev, width)
    )
    key_rows = (
        matmul(mixer_normed, full_key).astype(jnp.bfloat16).reshape(slot_count, frames_dev, width)
    )
    value_rows = (
        matmul(mixer_normed, full_value).astype(jnp.bfloat16).reshape(slot_count, frames_dev, width)
    )

    def head_scores(head_index, key_part):
        span_keys = key_part.shape[1]
        query_head = lax.dynamic_slice_in_dim(query_rows, head_index * head_dim, head_dim, 2)
        key_head = lax.dynamic_slice_in_dim(key_part, head_index * head_dim, head_dim, 2)
        products = jnp.einsum(
            "ucd,und->ucn", query_head, key_head, preferred_element_type=jnp.float32
        )
        key_index = jnp.arange(span_keys, dtype=jnp.int32)
        slope_head = 64.0 * 2.0 ** (-head_index.astype(jnp.float32)) / full_length
        distance = jnp.abs(frame_index[:, None] - key_index[None, :]).astype(jnp.float32)
        scores = products * score_scale - slope_head * distance
        usable = key_index[None, None, :] < lengths[:, None, None]
        return (scores, usable, query_head, key_head)

    start_state = (
        jnp.full((HEADS, slot_count, frames_dev), -1e30, jnp.float32),
        jnp.zeros((HEADS, slot_count, frames_dev), jnp.float32),
        jnp.zeros((HEADS, slot_count, frames_dev, head_dim), jnp.float32),
    )
    key_part = lax.all_gather(key_rows, "tm", axis=1, tiled=True)
    value_part = lax.all_gather(value_rows, "tm", axis=1, tiled=True)

    def absorb_per_head(inputs):
        head_index, run_max, run_sum, accumulator = inputs
        scores, usable, query_head, key_head = head_scores(head_index, key_part)
        value_head = lax.dynamic_slice_in_dim(value_part, head_index * head_dim, head_dim, 2)
        new_max = jnp.maximum(run_max, jnp.max(jnp.where(usable, scores, -1e30), -1))
        weights_now = jnp.where(usable, jnp.exp(scores - new_max[..., None]), 0.0)
        factor = jnp.exp(run_max - new_max)
        new_sum = run_sum * factor + jnp.sum(weights_now, -1)
        new_accum = accumulator * factor[..., None] + jnp.einsum(
            "ucn,und->ucd",
            weights_now.astype(jnp.bfloat16),
            value_head,
            preferred_element_type=jnp.float32,
        )
        return (new_max, new_sum, new_accum)

    run_max, run_sum, accumulator = lax.map(absorb_per_head, (head_numbers,) + tuple(start_state))
    attended = accumulator / run_sum[..., None]
    log_total = run_max + jnp.log(run_sum)
    mixture = jnp.transpose(attended, (1, 2, 0, 3)).reshape(row_count, width).astype(jnp.bfloat16)
    after_mixer = after_front + matmul(mixture, full_output)
    conv_normed = layer_norm(after_mixer, conv_norm_gain).astype(jnp.bfloat16)
    expand = matmul(conv_normed, full_expand)
    linear_half = expand[:, :width]
    sigmoid_gate = jax.nn.sigmoid(expand[:, width:])
    gated = (
        (linear_half * sigmoid_gate * frame_mask)
        .astype(jnp.bfloat16)
        .reshape(slot_count, frames_dev, width)
    )
    padded = with_halo(gated, (("tm", 1),), half_width)
    filtered = padded[:, 0:frames_dev, :] * depth_taps[:, 0]
    for kernel_tap in range(1, taps_count):
        filtered = (
            filtered
            + padded[:, kernel_tap : kernel_tap + frames_dev, :] * depth_taps[:, kernel_tap]
        )
    filtered = filtered.reshape(row_count, width)
    mask_total, frames_total = lax.psum(
        (jnp.sum(filtered * frame_mask, 0), jnp.sum(frame_mask)), ("tm", "slots")
    )
    middle = mask_total / frames_total
    offset = filtered - middle
    spread = lax.psum(jnp.sum(frame_mask * offset * offset, 0), ("tm", "slots")) / frames_total
    inverse_spread = lax.rsqrt(spread + EPSILON)
    unit_conv = offset * inverse_spread
    batch_normed = unit_conv * batch_scale + batch_shift
    swish = jax.nn.silu(batch_normed).astype(jnp.bfloat16)
    after_conv = after_mixer + matmul(swish, full_project)
    after_back, back_kept = feed_forward(after_conv, back_norm_gain, full_back_in, full_back_out)
    output = (
        layer_norm(after_back, final_norm_gain)
        .astype(jnp.bfloat16)
        .reshape(slot_count, frames_dev, width)
    )
    incoming = cotangent.astype(jnp.float32).reshape(row_count, width)
    grad_rows, grad_final = norm_back(after_back, final_norm_gain, incoming)
    grad_rows, grad_back_gain, grad_back_in, grad_back_out = feed_back(
        after_conv, back_norm_gain, full_back_in, full_back_out, back_kept, grad_rows
    )
    grad_conv_top = grad_rows.astype(jnp.bfloat16)
    grad_project = matmul_tn(swish, grad_conv_top)
    grad_batch_normed = matmul_nt(grad_conv_top, full_project) * silu_slope(batch_normed)
    grad_batch_scale = jnp.sum(grad_batch_normed * unit_conv, 0)
    grad_batch_shift = jnp.sum(grad_batch_normed, 0)
    grad_unit = grad_batch_normed * batch_scale
    sum_plain, sum_scaled = lax.psum(
        (jnp.sum(grad_unit, 0), jnp.sum(grad_unit * unit_conv, 0)), ("tm", "slots")
    )
    grad_filtered = inverse_spread * (
        grad_unit - frame_mask * (sum_plain + unit_conv * sum_scaled) / frames_total
    )
    grad_grid = grad_filtered.reshape(slot_count, frames_dev, width)
    grad_padded = with_halo(grad_grid.astype(jnp.bfloat16), (("tm", 1),), half_width).astype(
        grad_grid.dtype
    )
    grad_gated = jnp.zeros((slot_count, frames_dev, width), jnp.float32)
    taps_grad = []
    for kernel_tap in range(taps_count):
        lead = 2 * half_width - kernel_tap
        grad_gated = (
            grad_gated + depth_taps[:, kernel_tap] * grad_padded[:, lead : lead + frames_dev, :]
        )
        taps_grad.append(
            jnp.sum(grad_grid * padded[:, kernel_tap : kernel_tap + frames_dev, :], axis=(0, 1))
        )
    grad_depth = jnp.stack(taps_grad, axis=1)
    grad_gated_low = lax.optimization_barrier(
        grad_gated.reshape(row_count, width).astype(jnp.bfloat16)
    ).astype(jnp.float32)
    grad_masked = grad_gated_low * frame_mask
    grad_linear = grad_masked * sigmoid_gate
    grad_gate = grad_masked * linear_half * sigmoid_gate * (1.0 - sigmoid_gate)
    grad_expand = jnp.concatenate([grad_linear, grad_gate], 1).astype(jnp.bfloat16)
    grad_expand_weight = matmul_tn(conv_normed, grad_expand)
    grad_conv_normed = matmul_nt(grad_expand, full_expand)
    delta_rows, grad_conv_gain = norm_back(after_mixer, conv_norm_gain, grad_conv_normed)
    grad_rows = grad_rows + delta_rows
    grad_mix_top = grad_rows.astype(jnp.bfloat16)
    grad_output_weight = matmul_tn(mixture, grad_mix_top)
    grad_mixture = matmul_nt(grad_mix_top, full_output).astype(jnp.bfloat16)
    grad_heads = jnp.transpose(
        grad_mixture.reshape(slot_count, frames_dev, HEADS, head_dim), (2, 0, 1, 3)
    )
    delta_heads = jnp.sum(grad_heads.astype(jnp.float32) * attended, -1)
    start_grads = (
        jnp.zeros((HEADS, slot_count, frames_dev, head_dim), jnp.float32),
        jnp.zeros((HEADS, slot_count, full_length, head_dim), jnp.float32),
        jnp.zeros((HEADS, slot_count, full_length, head_dim), jnp.float32),
    )
    collect_key_part = lax.all_gather(key_rows, "tm", axis=1, tiled=True)
    collect_value_part = lax.all_gather(value_rows, "tm", axis=1, tiled=True)
    span_keys = collect_key_part.shape[1]

    def collect_per_head(inputs):
        head_index, grad_query, key_sums, value_sums, total_log, delta_head, grad_head = inputs
        scores, usable, query_head, key_head = head_scores(head_index, collect_key_part)
        value_head = lax.dynamic_slice_in_dim(
            collect_value_part, head_index * head_dim, head_dim, 2
        )
        probs = jnp.where(usable, jnp.exp(scores - total_log[..., None]), 0.0)
        grad_probs = jnp.einsum(
            "ucd,und->ucn", grad_head, value_head, preferred_element_type=jnp.float32
        )
        grad_raw = (probs * (grad_probs - delta_head[..., None]) * score_scale).astype(jnp.bfloat16)
        grad_query = grad_query + jnp.einsum(
            "ucn,und->ucd", grad_raw, key_head, preferred_element_type=jnp.float32
        )
        key_term = jnp.einsum(
            "ucn,ucd->und", grad_raw, query_head, preferred_element_type=jnp.float32
        )
        value_term = jnp.einsum(
            "ucn,ucd->und",
            probs.astype(jnp.bfloat16),
            grad_head,
            preferred_element_type=jnp.float32,
        )
        key_sums = key_sums + key_term
        value_sums = value_sums + value_term
        return (grad_query, key_sums, value_sums)

    folded = lax.map(
        collect_per_head,
        (head_numbers,) + tuple(start_grads) + (log_total, delta_heads, grad_heads),
    )
    grad_query_heads, key_sums, value_sums = folded
    grad_key_heads, grad_value_heads = (
        lax.psum_scatter(
            key_sums.astype(jnp.bfloat16), "tm", scatter_dimension=2, tiled=True
        ).astype(jnp.float32),
        lax.psum_scatter(
            value_sums.astype(jnp.bfloat16), "tm", scatter_dimension=2, tiled=True
        ).astype(jnp.float32),
    )

    def to_rows(heads_array):
        return (
            jnp.transpose(heads_array, (1, 2, 0, 3)).reshape(row_count, width).astype(jnp.bfloat16)
        )

    grad_query_rows = to_rows(grad_query_heads)
    grad_key_rows = to_rows(grad_key_heads)
    grad_value_rows = to_rows(grad_value_heads)
    grad_query_weight = matmul_tn(mixer_normed, grad_query_rows)
    grad_key_weight = matmul_tn(mixer_normed, grad_key_rows)
    grad_value_weight = matmul_tn(mixer_normed, grad_value_rows)
    grad_mixer_normed = (
        matmul_nt(grad_query_rows, full_query)
        + matmul_nt(grad_key_rows, full_key)
        + matmul_nt(grad_value_rows, full_value)
    )
    delta_rows, grad_mixer_gain = norm_back(after_front, mixer_norm_gain, grad_mixer_normed)
    grad_rows = grad_rows + delta_rows
    grad_rows, grad_front_gain, grad_front_in, grad_front_out = feed_back(
        residual_rows, front_norm_gain, full_front_in, full_front_out, front_kept, grad_rows
    )
    grad_features = grad_rows.astype(jnp.bfloat16).reshape(slot_count, frames_dev, width)
    partial_rows = (
        lax.psum_scatter(
            grad_front_gain.astype(jnp.bfloat16), "slots", scatter_dimension=0, tiled=True
        ).astype(jnp.float32),
        lax.psum_scatter(
            grad_front_in.astype(jnp.bfloat16), "slots", scatter_dimension=0, tiled=True
        ).astype(jnp.float32),
        lax.psum_scatter(
            grad_front_out.astype(jnp.bfloat16), "slots", scatter_dimension=0, tiled=True
        ).astype(jnp.float32),
        lax.psum_scatter(
            grad_mixer_gain.astype(jnp.bfloat16), "slots", scatter_dimension=0, tiled=True
        ).astype(jnp.float32),
        lax.psum_scatter(
            grad_query_weight.astype(jnp.bfloat16), "slots", scatter_dimension=0, tiled=True
        ).astype(jnp.float32),
        lax.psum_scatter(
            grad_key_weight.astype(jnp.bfloat16), "slots", scatter_dimension=0, tiled=True
        ).astype(jnp.float32),
        lax.psum_scatter(
            grad_value_weight.astype(jnp.bfloat16), "slots", scatter_dimension=0, tiled=True
        ).astype(jnp.float32),
        lax.psum_scatter(
            grad_output_weight.astype(jnp.bfloat16), "slots", scatter_dimension=0, tiled=True
        ).astype(jnp.float32),
        lax.psum_scatter(
            grad_conv_gain.astype(jnp.bfloat16), "slots", scatter_dimension=0, tiled=True
        ).astype(jnp.float32),
        lax.psum_scatter(
            grad_expand_weight.astype(jnp.bfloat16), "slots", scatter_dimension=0, tiled=True
        ).astype(jnp.float32),
        lax.psum_scatter(
            grad_depth.astype(jnp.bfloat16), "slots", scatter_dimension=0, tiled=True
        ).astype(jnp.float32),
        lax.psum_scatter(
            grad_batch_scale.astype(jnp.bfloat16), "slots", scatter_dimension=0, tiled=True
        ).astype(jnp.float32),
        lax.psum_scatter(
            grad_batch_shift.astype(jnp.bfloat16), "slots", scatter_dimension=0, tiled=True
        ).astype(jnp.float32),
        lax.psum_scatter(
            grad_project.astype(jnp.bfloat16), "slots", scatter_dimension=0, tiled=True
        ).astype(jnp.float32),
        lax.psum_scatter(
            grad_back_gain.astype(jnp.bfloat16), "slots", scatter_dimension=0, tiled=True
        ).astype(jnp.float32),
        lax.psum_scatter(
            grad_back_in.astype(jnp.bfloat16), "slots", scatter_dimension=0, tiled=True
        ).astype(jnp.float32),
        lax.psum_scatter(
            grad_back_out.astype(jnp.bfloat16), "slots", scatter_dimension=0, tiled=True
        ).astype(jnp.float32),
        lax.psum_scatter(
            grad_final.astype(jnp.bfloat16), "slots", scatter_dimension=0, tiled=True
        ).astype(jnp.float32),
    )
    (
        part_front_gain,
        part_front_in,
        part_front_out,
        part_mixer_gain,
        part_query,
        part_key,
        part_value,
        part_output,
        part_conv_gain,
        part_expand,
        part_depth,
        part_batch_gain,
        part_batch_bias,
        part_project,
        part_back_gain,
        part_back_in,
        part_back_out,
        part_final_gain,
    ) = partial_rows
    shards = (
        lax.psum(part_front_gain.astype(jnp.bfloat16), "tm").astype(jnp.float32),
        lax.psum(part_front_in.astype(jnp.bfloat16), "tm").astype(jnp.float32),
        lax.psum(part_front_out.astype(jnp.bfloat16), "tm").astype(jnp.float32),
        lax.psum(part_mixer_gain.astype(jnp.bfloat16), "tm").astype(jnp.float32),
        lax.psum(part_query.astype(jnp.bfloat16), "tm").astype(jnp.float32),
        lax.psum(part_key.astype(jnp.bfloat16), "tm").astype(jnp.float32),
        lax.psum(part_value.astype(jnp.bfloat16), "tm").astype(jnp.float32),
        lax.psum(part_output.astype(jnp.bfloat16), "tm").astype(jnp.float32),
        lax.psum(part_conv_gain.astype(jnp.bfloat16), "tm").astype(jnp.float32),
        lax.psum(part_expand.astype(jnp.bfloat16), "tm").astype(jnp.float32),
        lax.psum(part_depth.astype(jnp.bfloat16), "tm").astype(jnp.float32),
        lax.psum(part_batch_gain.astype(jnp.bfloat16), "tm").astype(jnp.float32),
        lax.psum(part_batch_bias.astype(jnp.bfloat16), "tm").astype(jnp.float32),
        lax.psum(part_project.astype(jnp.bfloat16), "tm").astype(jnp.float32),
        lax.psum(part_back_gain.astype(jnp.bfloat16), "tm").astype(jnp.float32),
        lax.psum(part_back_in.astype(jnp.bfloat16), "tm").astype(jnp.float32),
        lax.psum(part_back_out.astype(jnp.bfloat16), "tm").astype(jnp.float32),
        lax.psum(part_final_gain.astype(jnp.bfloat16), "tm").astype(jnp.float32),
    )
    return (output, grad_features) + tuple(shards)


def solution(mesh):
    in_specs = (
        P("slots", "tm", None),
        P("slots"),
        P("slots", "tm", None),
        P("slots"),
        P("slots", None),
        P("slots", None),
        P("slots"),
        P("slots", None),
        P("slots", None),
        P("slots", None),
        P("slots", None),
        P("slots"),
        P("slots", None),
        P("slots", None),
        P("slots"),
        P("slots"),
        P("slots", None),
        P("slots"),
        P("slots", None),
        P("slots", None),
        P("slots"),
    )
    out_specs = (
        P("slots", "tm", None),
        P("slots", "tm", None),
        P("slots"),
        P("slots", None),
        P("slots", None),
        P("slots"),
        P("slots", None),
        P("slots", None),
        P("slots", None),
        P("slots", None),
        P("slots"),
        P("slots", None),
        P("slots", None),
        P("slots"),
        P("slots"),
        P("slots", None),
        P("slots"),
        P("slots", None),
        P("slots", None),
        P("slots"),
    )
    return jax.shard_map(
        on_device, mesh=mesh, in_specs=in_specs, out_specs=out_specs, check_vma=False
    )
```
